32 devices in a mesh: expert: 16 (over z, y, x), replica: 2 (over core).
Axes of the slice: x: 2, y: 2, z: 4, core: 2. Of those that a mesh axis runs over, the one named last changes fastest.
Arguments:
- cotangent: bfloat16 [4096, 2048], P(('expert', 'replica')), may hold values from -2 to 2
- hidden: bfloat16 [4096, 6, 704], P(('expert', 'replica')), may hold values from -24 to 24
- routes: int32 [4096, 6], P(('expert', 'replica')), may hold values from 0 to 15, all different within a row; in each aligned block of 128 rows (0 to 127, 128 to 255, ...) at most 72 rows name the same one
- numerators: int32 [4096, 6], P(('expert', 'replica')), may hold values from 1 to 1024
- w_down: bfloat16 [16, 704, 2048], P('expert'), may hold values from -0.21875 to 0.21875
Outputs:
- gate_grad: float32 [4096, 6], P(('expert', 'replica'))
- grad_scales: float32 [16, 704, 16], P('expert', 'replica')
- grad_mantissa: float32 [16, 704, 2048], P('expert', 'replica')
The draws below stay inside these ranges and needn't reach their ends.
Inputs may be any that keep to these rules, and one draw needn't show every extreme that they name: `routes`: no expert is named by more than 72 rows of one device's tokens, a bound that some blocks reach.
All inputs are finite; a program needn't handle non-finite values. Where the reference program divides by a largest or mean magnitude, that divisor is 1e-20 or more.
Results may differ from the reference program's by a relative error of at most 0.023.
Values may be sent and summed in bfloat16 or wider, within the bound.
No kernel may reach another device: no remote copies, remote signals or barrier semaphores. Data moves between devices by JAX's collectives and lax.ppermute only.
A program may use at most 64 MiB of HBM per device.

```python
import math
import jax
import jax.numpy as jnp
import numpy as np
from jax import lax

D = 2048
HID = 704
TOP = 6
BLOCK = 128
TOK_DEV = 128
E = 16
TOKENS = 4096
SLOTS = 72
N_EXPERT = 16
N_REPLICA = 2


def draw_cotangent(key, part):
    keys = jax.random.split(key, 3)
    row_scale = jnp.exp(jax.random.uniform(keys[1], (TOKENS, 1), jnp.float32) * math.log(10.0))
    col_scale = jnp.exp(jax.random.uniform(keys[2], (1, D), jnp.float32) * math.log(10.0))
    position = (jnp.arange(TOKENS) // TOK_DEV % N_REPLICA).astype(jnp.float32) / max(N_REPLICA - 1, 1)
    values = jnp.clip(jax.random.normal(keys[0], (TOKENS, D), jnp.float32), -5.0, 5.0)
    factor = jnp.power(3.0, position)
    return (0.0007 * values * row_scale * col_scale * factor[:, None]).astype(jnp.bfloat16)


def draw_hidden(key, part):
    keys = jax.random.split(key, 2)
    col_scale = jnp.exp(jax.random.uniform(keys[1], (1, 1, HID), jnp.float32) * math.log(10.0))
    values = jnp.clip(jax.random.normal(keys[0], (TOKENS, TOP, HID), jnp.float32), -6.0, 6.0)
    return (0.3 * values * col_scale).astype(jnp.bfloat16)


def touch_ends(drawn, stream_key, least, top_value):
    place = [jax.random.randint(jax.random.fold_in(stream_key, axis), (), 0, length) for axis, length in enumerate(drawn.shape)]
    widest = drawn.shape.index(max(drawn.shape))
    beside = place[:widest] + [(place[widest] + 1) % drawn.shape[widest]] + place[widest + 1:]
    return drawn.at[tuple(place)].set(least).at[tuple(beside)].set(top_value)


def levels(key, dims, shards, low, top_value):
    gain, own = 1.0, jax.random.fold_in(key, 6)
    for dim, parts in shards:
        heights = jnp.exp(jax.random.uniform(jax.random.fold_in(own, dim), (parts,), jnp.float32, low / len(shards), top_value / len(shards)))
        gain = gain * jnp.repeat(heights, dims[dim] // parts).reshape([-1 if axis == dim else 1 for axis in range(len(dims))])
    return gain


def routed_block(rng, own, number, rows, number_of, top, reach, lean):
    ranking = jax.random.permutation(rng, number_of)
    heavy_load, ordinary = load_shares(number_of, rows * top, reach, lean, True), load_shares(number_of, rows * top, reach, lean, False)
    places = jnp.arange(number_of)

    def named(lengths, offset_by):
        used = int((lengths > 0).sum())
        fixed = max(1, used // 4)
        passed = fixed + (places - fixed + offset_by * (used - fixed)) % max(1, number_of - fixed)
        return jnp.zeros((number_of,), jnp.int32).at[ranking[jnp.where(places < fixed, places, passed)]].set(jnp.asarray(lengths, jnp.int32))

    lengths = jnp.where(number % 4 == 0, named(heavy_load, number // 4), named(ordinary, number - number // 4 - 1))
    mixed = jax.random.permutation(jax.random.fold_in(own, 3), number_of)
    donor, receiver = mixed[0:number_of // 2 * 2:2], mixed[1:number_of // 2 * 2:2]
    margin = jnp.minimum(lengths[donor] - 1, reach - lengths[receiver]) // 2
    margin = jnp.where((donor == ranking[0]) | (receiver == ranking[0]) | (lengths[receiver] == 0), 0, jnp.maximum(margin, 0))
    passed = jax.random.randint(jax.random.fold_in(own, 4), (number_of // 2,), 0, 1 << 20) % (margin + 1)
    lengths = lengths.at[donor].add(-passed).at[receiver].add(passed)
    members = jnp.searchsorted(jnp.cumsum(lengths), jnp.arange(rows * top), side="right").astype(jnp.int32)
    table = members.reshape(top, rows).T
    table = table[jax.random.permutation(jax.random.fold_in(own, 1), rows)]
    offset_by = jax.random.randint(jax.random.fold_in(own, 2), (rows, 1), 0, top)
    return jnp.take_along_axis(table, (jnp.arange(top)[None, :] + offset_by) % top, axis=1)


def load_shares(amount, total, reach, lean, full):
    portions = [(1 << 20) // math.isqrt(standing ** lean) + 1 for standing in range(1, amount + 1)]
    largest = reach if full else min(reach, max(-(-total // amount), total * portions[0] // sum(portions)))
    least = 1 if total - largest >= amount - 1 else 0
    holding, rest = [largest] + [least] * (amount - 1), total - largest - least * (amount - 1)
    while rest > 0:
        candidates = [i for i in range(1, amount) if holding[i] < largest] or [i for i in range(1, amount) if holding[i] < reach]
        whole, left = sum([portions[i] for i in candidates]), rest
        for i in candidates:
            extra = min(reach - holding[i], max(1, left * portions[i] // whole), rest)
            holding[i] = holding[i] + extra
            rest = rest - extra
    return np.array(holding)


def noise(rng, dims, width, bound, cuts=(), kind=jnp.bfloat16):
    gain = levels(rng, dims, cuts, -0.22, 0.18) if cuts else 1.0
    drawn = jax.random.normal(rng, dims, jnp.float32) * width * gain
    return jnp.minimum(jnp.maximum(drawn, -bound), bound).astype(kind)


def setup_inputs(seed: int = 0) -> dict:
    key_list = jax.random.split(jax.random.key(seed), 6)
    cotangent = draw_cotangent(jax.random.fold_in(key_list[5], 71), 0)
    hidden = draw_hidden(jax.random.fold_in(key_list[5], 71), 0)
    routes_keys = jax.random.split(jax.random.fold_in(key_list[2], 1), TOKENS // TOK_DEV)
    routes_turns = jax.random.permutation(jax.random.fold_in(key_list[2], 3), TOKENS // TOK_DEV)
    routes = jax.vmap(lambda own, number: routed_block(jax.random.fold_in(key_list[2], 2), own, number, TOK_DEV, E, TOP, SLOTS, 2))(routes_keys, routes_turns).reshape((TOKENS, TOP))
    numerators = touch_ends(jax.random.randint(key_list[3], (TOKENS, TOP), 1, 1025), jax.random.fold_in(key_list[3], 1), 1, 1024).astype(jnp.int32)
    w_down = noise(key_list[4], (E, HID, D), HID ** -0.5, 0.21875, ((0, 16),))
    return dict(cotangent=cotangent, hidden=hidden, routes=routes, numerators=numerators, w_down=w_down)


def pair_terms(cot_group, hid_group, route_group, weight_group, matrix, expert_id):
    routed = TOK_DEV * TOP
    chosen = (route_group == expert_id).astype(jnp.int32)
    before = jnp.cumsum(chosen, axis=1).astype(jnp.int32) - chosen
    target = jnp.where(chosen > 0, before, SLOTS).astype(jnp.int32)
    sources = jnp.broadcast_to(jnp.arange(N_EXPERT, dtype=jnp.int32)[:, None], (N_EXPERT, routed))
    row_ids = jnp.broadcast_to(jnp.arange(routed, dtype=jnp.int32)[None, :], (N_EXPERT, routed))
    slot_table = jnp.full((N_EXPERT, SLOTS + 1), routed, jnp.int32).at[sources, target].set(row_ids)
    slot_table = slot_table[:, :SLOTS]
    in_use = slot_table < routed
    clipped = jnp.minimum(slot_table, routed - 1).astype(jnp.int32)
    hid_sel = jnp.take_along_axis(hid_group, clipped[:, :, None], axis=1)
    hid_sel = jnp.where(in_use[:, :, None], hid_sel, jnp.zeros_like(hid_sel))
    cot_sel = jnp.take_along_axis(cot_group, (clipped // TOP).astype(jnp.int32)[:, :, None], axis=1)
    cot_sel = jnp.where(in_use[:, :, None], cot_sel, jnp.zeros_like(cot_sel))
    weight_sel = jnp.where(in_use, jnp.take_along_axis(weight_group, clipped, axis=1), jnp.float32(0.0))
    cot_flat = cot_sel.reshape(N_EXPERT * SLOTS, D)
    hid_flat = hid_sel.reshape(N_EXPERT * SLOTS, HID)
    back_proj = jnp.dot(cot_flat, matrix.T, preferred_element_type=jnp.float32)
    gate_vals = jnp.sum(back_proj * hid_flat.astype(jnp.float32), axis=1).reshape(N_EXPERT, SLOTS)
    scaled = (weight_sel.reshape(N_EXPERT * SLOTS)[:, None] * cot_flat.astype(jnp.float32)).astype(jnp.bfloat16)
    partial_value = jnp.dot(hid_flat.T, scaled, preferred_element_type=jnp.float32)
    slot_sources = jnp.broadcast_to(jnp.arange(N_EXPERT, dtype=jnp.int32)[:, None], (N_EXPERT, SLOTS))
    spread = jnp.zeros((N_EXPERT, routed + 1), jnp.float32).at[slot_sources, slot_table].set(
        jnp.where(in_use, gate_vals, jnp.float32(0.0)))
    return partial_value, spread[:, :routed]


def reference(cotangent, hidden, routes, numerators, w_down):
    routed = TOK_DEV * TOP
    cot_all = cotangent.reshape(N_EXPERT, N_REPLICA, TOK_DEV, D)
    hid_all = hidden.reshape(N_EXPERT, N_REPLICA, routed, HID)
    route_all = routes.reshape(N_EXPERT, N_REPLICA, routed)
    weight_all = numerators.reshape(N_EXPERT, N_REPLICA, routed).astype(jnp.float32) / 1024.0

    def per_expert(gate_acc, expert_id):
        matrix = w_down[expert_id]

        def per_replica(group_id):
            return pair_terms(cot_all[:, group_id], hid_all[:, group_id], route_all[:, group_id],
                              weight_all[:, group_id], matrix, expert_id)

        partials, spreads = lax.map(per_replica, jnp.arange(N_REPLICA, dtype=jnp.int32))
        blocks = partials.reshape(N_REPLICA, HID, D // BLOCK, BLOCK)
        scales = jnp.max(jnp.max(jnp.abs(blocks), axis=3), axis=0) + 1e-6
        mantissa = (blocks / scales[None, :, :, None]).astype(jnp.bfloat16)
        mantissa = lax.optimization_barrier(mantissa).astype(jnp.float32)
        summed = jnp.sum(mantissa, axis=0).reshape(HID, D)
        return gate_acc + jnp.transpose(spreads, (1, 0, 2)), (scales, summed)

    start_acc = jnp.zeros((N_EXPERT, N_REPLICA, routed), jnp.float32)
    gate_acc, outputs = lax.scan(per_expert, start_acc, jnp.arange(E, dtype=jnp.int32))
    gate_grad = gate_acc.reshape(N_EXPERT * N_REPLICA * TOK_DEV, TOP)
    return gate_grad, outputs[0], outputs[1]
```

```python
import functools

import jax
import jax.numpy as jnp
from jax import lax
from jax.experimental import pallas as pl
from jax.experimental.pallas import tpu as pltpu
from jax.sharding import PartitionSpec as P

BLOCK = 128
PLANE = 4
BF = jnp.bfloat16
F32 = jnp.float32
NT = (((1,), (1,)), ((), ()))
VMEM_BYTES = 48 * 1024 * 1024


def up(value, unit):
    return -(-value // unit) * unit


def call(kernel, out_shape, flops, nbytes, **kw):
    return pl.pallas_call(
        kernel,
        out_shape=out_shape,
        cost_estimate=pl.CostEstimate(flops=flops, bytes_accessed=nbytes, transcendentals=0),
        compiler_params=pltpu.CompilerParams(vmem_limit_bytes=VMEM_BYTES),
        **kw,
    )


def meta_kernel(outer, stride, routes_ref, slot_ref, rel_ref, code_ref):
    me = lax.axis_index("expert")
    experts, tokens = slot_ref.shape
    top_k = routes_ref.shape[0]
    routes = routes_ref[...]
    steps = (routes >> 2) - (me >> 2)
    steps = jnp.where(steps < 0, steps + outer, steps)
    rel = steps * PLANE + ((routes & 3) ^ (me & 3))
    rel_ref[...] = rel
    ids = lax.broadcasted_iota(jnp.int32, (experts, tokens), 0)
    mask = jnp.zeros((experts, tokens), F32)
    for k in range(top_k):
        mask += jnp.where(rel[k : k + 1, :] == ids, 1.0, 0.0)
    earlier = lax.broadcasted_iota(jnp.int32, (tokens, tokens), 0) < lax.broadcasted_iota(
        jnp.int32, (tokens, tokens), 1
    )
    rank = jnp.dot(
        mask.astype(BF), jnp.where(earlier, 1.0, 0.0).astype(BF), preferred_element_type=F32
    )
    slot = jnp.where(mask > 0.5, rank, -1.0)
    slot_ref[...] = slot
    for k in range(top_k):
        own = jnp.sum(
            jnp.where(rel[k : k + 1, :] == ids, slot, 0.0), axis=0, keepdims=True
        ).astype(jnp.int32)
        code_ref[k : k + 1, :] = rel[k : k + 1, :] * stride + own


def pack_kernel(outer, slots, stride, code_ref, num_ref, hid_ref, *rest):
    outs, table = rest[:PLANE], rest[PLANE]
    top_k, width, tokens = hid_ref.shape
    padded = table.shape[0]
    for k in range(top_k):
        lanes = slice(k * tokens, (k + 1) * tokens)
        table[0:width, lanes] = hid_ref[k]
        weight = num_ref[k : k + 1, :].astype(F32) * (1.0 / 1024.0)
        high = weight.astype(BF).astype(F32)
        rows = lax.broadcasted_iota(jnp.int32, (padded - width, tokens), 0)
        tail = jnp.where(rows == 0, high, jnp.where(rows == 1, weight - high, 0.0))
        table[width:padded, lanes] = tail.astype(BF)
    code = jnp.concatenate([code_ref[k : k + 1, :] for k in range(top_k)], axis=1)
    group = PLANE * stride
    for s in range(outer):
        rows = lax.broadcasted_iota(jnp.int32, (group, top_k * tokens), 0) + s * group
        pick = jnp.where(rows == code, 1.0, 0.0).astype(BF)
        got = lax.dot_general(pick, table[...], NT, preferred_element_type=F32)
        for k in range(PLANE):
            outs[k][s] = got[k * stride : k * stride + slots, :].astype(BF)


def relay_kernel(stage, slots, stride, slot_ref, cot_ref, *outs):
    tokens = cot_ref.shape[0]
    rows = lax.broadcasted_iota(jnp.int32, (stride, tokens), 0).astype(F32)
    pick = jnp.concatenate(
        [
            jnp.where(slot_ref[stage * PLANE + k : stage * PLANE + k + 1, :] == rows, 1.0, 0.0)
            for k in range(PLANE)
        ],
        axis=0,
    ).astype(BF)
    width = cot_ref.shape[1]
    step = min(512, width)
    for c in range(0, width, step):
        got = jnp.dot(pick, cot_ref[:, c : c + step], preferred_element_type=F32)
        for k in range(PLANE):
            outs[k][:, c : c + step] = got[k * stride : k * stride + slots, :].astype(BF)


def fill(table, pieces, slots, stride):
    for k, piece in enumerate(pieces):
        wide = piece.astype(F32)
        if stride > slots:
            wide = jnp.concatenate([wide, jnp.zeros((stride - slots, wide.shape[1]), F32)], axis=0)
        table[k * stride : (k + 1) * stride, :] = wide.astype(BF)


def back_kernel(slots, stride, c0, c1, c2, c3, hid_ref, w_ref, gate_ref, hidw_ref, rows, hids, acc):
    step = pl.program_id(0)
    width = w_ref.shape[0]
    fill(rows, [c0[...], c1[...], c2[...], c3[...]], slots, stride)
    part = lax.dot_general(w_ref[...], rows[...], NT, preferred_element_type=F32)

    @pl.when(step == 0)
    def _():
        acc[...] = part

    @pl.when(step > 0)
    def _():
        acc[...] += part

    @pl.when(step == pl.num_programs(0) - 1)
    def _():
        fill(hids, [hid_ref[k] for k in range(PLANE)], slots, stride)
        flipped = hids[...].astype(F32).T
        hid = flipped[0:width, :]
        gate = jnp.sum(acc[...] * hid, axis=0, keepdims=True)
        weight = flipped[width : width + 1, :] + flipped[width + 1 : width + 2, :]
        hidw_ref[...] = (hid * weight).astype(BF)
        gate_ref[...] = jnp.zeros_like(gate_ref)
        for k in range(PLANE):
            gate_ref[k : k + 1, 0:stride] = gate[:, k * stride : (k + 1) * stride]


def partial_kernel(slots, stride, count, has_acc, last, *refs):
    cots = refs[: PLANE * count]
    hidw = refs[PLANE * count : PLANE * count + count]
    refs = refs[PLANE * count + count :]
    total = None
    acc_ref = refs[0] if has_acc else None
    refs = refs[1:] if has_acc else refs
    rows, sums = refs[-2:]
    for s in range(count):
        fill(rows, [cots[s * PLANE + k][...] for k in range(PLANE)], slots, stride)
        part = jnp.dot(hidw[s][...], rows[...], preferred_element_type=F32)
        total = part if total is None else total + part
    if has_acc:
        total = total + acc_ref[...]
    if not last:
        refs[0][...] = total
        return
    mine_ref, send_ref = refs[0], refs[1]
    share = mine_ref.shape[0]
    me = lax.axis_index("replica")
    sums[...] = total
    mine_ref[...] = sums[pl.ds(pl.multiple_of(me * share, 8), share), :]
    if send_ref.shape[0] == share:
        send_ref[...] = sums[pl.ds(pl.multiple_of((1 - me) * share, 8), share), :].astype(BF)
    else:
        send_ref[...] = total.astype(BF)


def final_kernel(own_in_parts, mine_ref, parts_ref, out_ref, scale_ref, table):
    step = pl.program_id(0)
    count = parts_ref.shape[0]
    share, width = mine_ref.shape
    me = lax.axis_index("replica")
    lanes = lax.broadcasted_iota(jnp.int32, (share, BLOCK), 1)

    @pl.when(step == 0)
    def _():
        table[...] = jnp.zeros_like(table)

    kept = table[0:share, :]
    for b in range(width // BLOCK):
        span = slice(b * BLOCK, (b + 1) * BLOCK)
        own = mine_ref[:, span]
        top = jnp.abs(own)
        total = own
        for n in range(count):
            other = parts_ref[n, :, span].astype(F32)
            if own_in_parts:
                other = jnp.where(me == n, 0.0, other)
            top = jnp.maximum(top, jnp.abs(other))
            total = total + other
        scale = jnp.max(top, axis=1, keepdims=True) + 1e-6
        out_ref[:, span] = total / scale
        kept = jnp.where(lanes == step * (width // BLOCK) + b, scale, kept)
    table[0:share, :] = kept

    @pl.when(step == pl.num_programs(0) - 1)
    def _():
        scale_ref[...] = table[...].T[0 : scale_ref.shape[0], 0:share]


def gate_kernel(slot_ref, rel_ref, *refs):
    rows, out_ref = refs[:-1], refs[-1]
    experts, tokens = slot_ref.shape
    table = jnp.concatenate(
        [row[m % PLANE : m % PLANE + 1, :] for m, row in enumerate(rows)], axis=0
    )
    slot = jnp.maximum(slot_ref[...], 0.0).astype(jnp.int32)
    value = jnp.take_along_axis(table, slot, axis=1)
    ids = lax.broadcasted_iota(jnp.int32, (experts, tokens), 0)
    for k in range(out_ref.shape[0]):
        out_ref[k : k + 1, :] = jnp.sum(
            jnp.where(rel_ref[k : k + 1, :] == ids, value, 0.0), axis=0, keepdims=True
        )


def per_device(cotangent, hidden, routes, numerators, w_down):
    tokens, model = cotangent.shape
    top_k, width = hidden.shape[1], hidden.shape[2]
    experts, replicas = lax.axis_size("expert"), lax.axis_size("replica")
    outer = experts // PLANE
    slots = up(3 * tokens * top_k // (2 * experts), 8)
    stride = up(slots, 16)
    padded = up(width + 2, 128)
    share = width // replicas
    group = PLANE * stride
    sds = jax.ShapeDtypeStruct

    def ring(array, s):
        pairs = [(e, (e + s * PLANE) % experts) for e in range(experts)]
        return lax.ppermute(array, "expert", pairs)

    def swap(array, k):
        return lax.ppermute(array, "expert", [(e, e ^ k) for e in range(experts)])

    def home(array, s, k):
        pairs = [(e, ((e - s * PLANE) % experts) ^ k) for e in range(experts)]
        return lax.ppermute(array, "expert", pairs)

    cots = [cotangent]
    for s in range(1, outer):
        cots.append(ring(cots[-1], 1))

    slot, rel, code = call(
        functools.partial(meta_kernel, outer, stride),
        (
            sds((experts, tokens), F32),
            sds((top_k, tokens), jnp.int32),
            sds((top_k, tokens), jnp.int32),
        ),
        4 * experts * tokens * tokens,
        1 << 16,
    )(routes.T)
    metas = [slot] + [ring(slot, s) for s in range(1, outer)]

    def relay(s):
        return call(
            functools.partial(relay_kernel, s, slots, stride),
            [sds((slots, model), BF)] * PLANE,
            2 * group * tokens * model,
            2 * tokens * model + 2 * group * model,
        )(metas[s], cots[s])

    packed = call(
        functools.partial(pack_kernel, outer, slots, stride),
        [sds((outer, slots, padded), BF)] * PLANE,
        2 * experts * stride * top_k * tokens * padded,
        2 * top_k * tokens * padded + 2 * experts * slots * padded,
        scratch_shapes=[pltpu.VMEM((padded, top_k * tokens), BF)],
    )(code, numerators.T, jnp.transpose(hidden, (1, 2, 0)))
    in_plane = [packed[0]] + [swap(packed[k], k) for k in range(1, PLANE)]
    hids = []
    for s in range(outer):
        regrouped = jnp.stack([part[s] for part in in_plane])
        hids.append(ring(regrouped, s) if s else regrouped)

    got = []
    for s in range(outer):
        sent = relay(s)
        got.append([sent[0]] + [swap(sent[k], k) for k in range(1, PLANE)])

    matrix = w_down[0]
    step = 512
    steps = model // step

    def back(s):
        cot_spec = pl.BlockSpec((slots, step), lambda j: (0, j))
        return call(
            functools.partial(back_kernel, slots, stride),
            [sds((PLANE, BLOCK), F32), sds((width, group), BF)],
            2 * group * model * width,
            2 * model * (width + group),
            grid=(steps,),
            in_specs=[cot_spec] * PLANE
            + [
                pl.BlockSpec((PLANE, slots, padded), lambda j: (0, 0, 0)),
                pl.BlockSpec((width, step), lambda j: (0, j)),
            ],
            out_specs=[
                pl.BlockSpec((PLANE, BLOCK), lambda j: (0, 0)),
                pl.BlockSpec((width, group), lambda j: (0, 0)),
            ],
            scratch_shapes=[
                pltpu.VMEM((group, step), BF),
                pltpu.VMEM((group, padded), BF),
                pltpu.VMEM((width, group), F32),
            ],
        )(*got[s], hids[s], matrix)

    def partial(stages, hidws, acc, last):
        count = len(stages)
        cot_spec = pl.BlockSpec((slots, step), lambda j: (0, j))
        in_specs = [cot_spec] * (PLANE * count)
        in_specs += [pl.BlockSpec((width, group), lambda j: (0, 0))] * count
        args = [c for s in stages for c in got[s]] + hidws
        whole = pl.BlockSpec((width, step), lambda j: (0, j))
        if acc is not None:
            in_specs.append(whole)
            args.append(acc)
        if last:
            sent = share if replicas == 2 else width
            outs = [sds((share, model), F32), sds((sent, model), BF)]
            out_specs = [
                pl.BlockSpec((share, step), lambda j: (0, j)),
                pl.BlockSpec((sent, step), lambda j: (0, j)),
            ]
        else:
            outs, out_specs = [sds((width, model), F32)], [whole]
        return call(
            functools.partial(partial_kernel, slots, stride, count, acc is not None, last),
            outs,
            2 * group * count * model * width,
            4 * model * width * 2,
            grid=(steps,),
            in_specs=in_specs,
            out_specs=out_specs,
            scratch_shapes=[pltpu.VMEM((group, step), BF), pltpu.VMEM((width, step), F32)],
        )(*args)

    rows, hidws = [], []
    acc = None
    for s in range(outer):
        gate, hidw = back(s)
        rows += [home(gate, s, k) if s or k else gate for k in range(PLANE)]
        hidws.append(hidw)
        if s < outer - 1:
            acc = partial([s], [hidw], acc, False)[0]
    mine, send = partial([outer - 1], hidws[-1:], acc, True)

    if replicas == 2:
        parts = lax.ppermute(send, "replica", [(0, 1), (1, 0)])[None]
    else:
        parts = lax.all_to_all(
            send.reshape(replicas, share, model), "replica", 0, 0, tiled=True
        )
    out, scales = call(
        functools.partial(final_kernel, replicas != 2),
        [sds((share, model), F32), sds((model // BLOCK, share), F32)],
        8 * share * model,
        10 * share * model,
        grid=(steps,),
        in_specs=[
            pl.BlockSpec((share, step), lambda j: (0, j)),
            pl.BlockSpec((parts.shape[0], share, step), lambda j: (0, 0, j)),
        ],
        out_specs=[
            pl.BlockSpec((share, step), lambda j: (0, j)),
            pl.BlockSpec((model // BLOCK, share), lambda j: (0, 0)),
        ],
        scratch_shapes=[pltpu.VMEM((up(share, 128), BLOCK), F32)],
    )(mine, parts)
    gate_grad = call(
        gate_kernel,
        sds((top_k, tokens), F32),
        1 << 16,
        1 << 16,
    )(slot, rel, *rows)
    return gate_grad.T, scales.T[None], out[None]


def solution(mesh):
    return jax.shard_map(
        per_device,
        mesh=mesh,
        in_specs=(
            P(("expert", "replica"), None),
            P(("expert", "replica"), None, None),
            P(("expert", "replica"), None),
            P(("expert", "replica"), None),
            P("expert", None, None),
        ),
        out_specs=(
            P(("expert", "replica"), None),
            P("expert", "replica", None),
            P("expert", "replica", None),
        ),
        check_vma=False,
    )
```

```python
import functools

import jax
import jax.numpy as jnp
from jax import lax
from jax.experimental import pallas as pl
from jax.experimental.pallas import tpu as pltpu
from jax.sharding import PartitionSpec as P

BLOCK = 128
PLANE = 4
BF = jnp.bfloat16
F32 = jnp.float32
NT = (((1,), (1,)), ((), ()))
VMEM_BYTES = 48 * 1024 * 1024


def up(value, unit):
    return -(-value // unit) * unit


def call(kernel, out_shape, flops, nbytes, **kw):
    return pl.pallas_call(
        kernel,
        out_shape=out_shape,
        cost_estimate=pl.CostEstimate(flops=flops, bytes_accessed=nbytes, transcendentals=0),
        compiler_params=pltpu.CompilerParams(vmem_limit_bytes=VMEM_BYTES),
        **kw,
    )


def table_kernel(stride, routes_ref, cot_ref, ext_ref, slot_ref, code_ref):
    experts, tokens = slot_ref.shape
    top_k = routes_ref.shape[0]
    model = cot_ref.shape[1]
    routes = routes_ref[...]
    ids = lax.broadcasted_iota(jnp.int32, (experts, tokens), 0)
    mask = jnp.zeros((experts, tokens), F32)
    for k in range(top_k):
        mask += jnp.where(routes[k : k + 1, :] == ids, 1.0, 0.0)
    earlier = lax.broadcasted_iota(jnp.int32, (tokens, tokens), 0) < lax.broadcasted_iota(
        jnp.int32, (tokens, tokens), 1
    )
    rank = jnp.dot(
        mask.astype(BF), jnp.where(earlier, 1.0, 0.0).astype(BF), preferred_element_type=F32
    )
    slot = jnp.where(mask > 0.5, rank, -1.0)
    slot_ref[...] = slot
    for k in range(top_k):
        own = jnp.sum(
            jnp.where(routes[k : k + 1, :] == ids, slot, 0.0), axis=0, keepdims=True
        ).astype(jnp.int32)
        code_ref[k : k + 1, :] = routes[k : k + 1, :] * stride + own
    wide = jnp.concatenate([slot, jnp.zeros((BLOCK - experts, tokens), F32)], axis=0)
    ext_ref[:, 0:model] = cot_ref[...]
    ext_ref[:, model : model + BLOCK] = wide.T.astype(BF)


def pack_kernel(slots, stride, flip, code_ref, num_ref, hid_ref, first_ref, second_ref, table):
    top_k, width, tokens = hid_ref.shape
    half = width // 2
    padded = table.shape[0]
    experts = first_ref.shape[0]
    code = jnp.concatenate([code_ref[k : k + 1, :] for k in range(top_k)], axis=1)
    group = PLANE * stride
    begin = lax.axis_index("replica") if flip else 1
    for out_ref, part in ((first_ref, 1 - begin), (second_ref, begin)):
        at = pl.multiple_of(part * half, 16) if flip else part * half
        for k in range(top_k):
            lanes = slice(k * tokens, (k + 1) * tokens)
            table[0:half, lanes] = hid_ref[k, pl.ds(at, half), :]
            weight = num_ref[k : k + 1, :].astype(F32) * (1.0 / 1024.0)
            high = weight.astype(BF).astype(F32)
            rows = lax.broadcasted_iota(jnp.int32, (padded - half, tokens), 0)
            tail = jnp.where(rows == 0, high, jnp.where(rows == 1, weight - high, 0.0))
            table[half:padded, lanes] = tail.astype(BF)
        for s in range(experts // PLANE):
            rows = lax.broadcasted_iota(jnp.int32, (group, top_k * tokens), 0) + s * group
            pick = jnp.where(rows == code, 1.0, 0.0).astype(BF)
            got = lax.dot_general(pick, table[...], NT, preferred_element_type=F32)
            for k in range(PLANE):
                out_ref[s * PLANE + k] = got[k * stride : k * stride + slots, :].astype(BF)


def relay_kernel(slots, stride, ext_ref, *refs):
    outs, table = refs[:-1], refs[-1]
    tokens = ext_ref.shape[0]
    model = outs[0].shape[1]
    me = lax.axis_index("expert")
    table[...] = ext_ref[:, model : model + BLOCK].astype(F32).T
    rows = lax.broadcasted_iota(jnp.int32, (stride, tokens), 0).astype(F32)
    pick = jnp.concatenate(
        [jnp.where(table[pl.ds(me ^ k, 1), :] == rows, 1.0, 0.0) for k in range(PLANE)], axis=0
    ).astype(BF)
    step = min(512, model)
    for c in range(0, model, step):
        got = jnp.dot(pick, ext_ref[:, c : c + step], preferred_element_type=F32)
        for k in range(PLANE):
            outs[k][:, c : c + step] = got[k * stride : k * stride + slots, :].astype(BF)


def fill(table, at, piece, stride):
    wide = piece.astype(F32)
    short = stride - wide.shape[0]
    if short:
        wide = jnp.concatenate([wide, jnp.zeros((short, wide.shape[1]), F32)], axis=0)
    table[at : at + stride, :] = wide.astype(table.dtype)


def back_kernel(stride, c0, c1, c2, c3, w_ref, rows_ref, back_ref):
    step = pl.program_id(0)
    for k, piece in enumerate((c0, c1, c2, c3)):
        fill(rows_ref, k * stride, piece[...], stride)
    part = lax.dot_general(w_ref[...], rows_ref[...], NT, preferred_element_type=F32)

    @pl.when(step == 0)
    def _():
        back_ref[...] = part

    @pl.when(step > 0)
    def _():
        back_ref[...] += part


def source(outer, s, k):
    me = lax.axis_index("expert")
    ring = (me >> 2) - s
    ring = jnp.where(ring < 0, ring + outer, ring)
    return ring * PLANE + ((me & 3) ^ k)


def gate_kernel(outer, stride, second, flip, *refs):
    backs, refs = refs[:outer], refs[outer:]
    hid_ref, before_ref, gate_ref, hidw_ref, table = refs
    half = hidw_ref.shape[0]
    mine = lax.axis_index("replica") if flip else 1
    part = mine if second else 1 - mine
    at = pl.multiple_of(part * half, 8) if flip else part * half
    gate_ref[...] = before_ref[...]
    group = PLANE * stride
    for s in range(outer):
        for k in range(PLANE):
            fill(table, k * stride, hid_ref[source(outer, s, k)], stride)
        flipped = table[...].T
        hid = flipped[0:half, :]
        gate = jnp.sum(backs[s][pl.ds(at, half), :] * hid, axis=0, keepdims=True)
        weight = flipped[half : half + 1, :] + flipped[half + 1 : half + 2, :]
        hidw_ref[:, s * group : (s + 1) * group] = (hid * weight).astype(BF)
        for k in range(PLANE):
            gate_ref[pl.ds(source(outer, s, k), 1), 0:stride] += gate[:, k * stride : (k + 1) * stride]


def product(hidw_ref, cots, rows):
    group = cots[0].shape[0]
    for s, piece in enumerate(cots):
        rows[s * group : (s + 1) * group, :] = piece[...]
    return jnp.dot(hidw_ref[...], rows[...], preferred_element_type=F32)


def partial_kernel(outer, *refs):
    hidw_ref, out_ref, rows = refs[outer:]
    out_ref[...] = product(hidw_ref, refs[:outer], rows).astype(BF)


def scale_sum(own, others, step, out_ref, scale_ref, table):
    share, width = out_ref.shape
    lanes = lax.broadcasted_iota(jnp.int32, (share, BLOCK), 1)

    @pl.when(step == 0)
    def _():
        table[...] = jnp.zeros_like(table)

    kept = table[0:share, :]
    for b in range(width // BLOCK):
        span = slice(b * BLOCK, (b + 1) * BLOCK)
        terms = ([] if own is None else [own[:, span]]) + [o[:, span].astype(F32) for o in others]
        top = functools.reduce(jnp.maximum, [jnp.abs(term) for term in terms])
        scale = jnp.max(top, axis=1, keepdims=True) + 1e-6
        out_ref[:, span] = sum(terms) / scale
        kept = jnp.where(lanes == step * (width // BLOCK) + b, scale, kept)
    table[0:share, :] = kept

    @pl.when(step == pl.num_programs(0) - 1)
    def _():
        scale_ref[...] = table[...].T[0 : scale_ref.shape[0], 0:share]


def finish_kernel(outer, *refs):
    cots = refs[:outer]
    hidw_ref, other_ref, out_ref, scale_ref, rows, table = refs[outer:]
    own = product(hidw_ref, cots, rows)
    scale_sum(own, [other_ref], pl.program_id(0), out_ref, scale_ref, table)


def gather_sum_kernel(parts_ref, out_ref, scale_ref, table):
    others = [parts_ref.at[n] for n in range(parts_ref.shape[0])]
    scale_sum(None, others, pl.program_id(0), out_ref, scale_ref, table)


def pick_kernel(slot_ref, routes_ref, rows_ref, out_ref):
    experts, tokens = slot_ref.shape
    slot = jnp.maximum(slot_ref[...], 0.0).astype(jnp.int32)
    value = jnp.take_along_axis(rows_ref[...], slot, axis=1)
    ids = lax.broadcasted_iota(jnp.int32, (experts, tokens), 0)
    for k in range(out_ref.shape[0]):
        out_ref[k : k + 1, :] = jnp.sum(
            jnp.where(routes_ref[k : k + 1, :] == ids, value, 0.0), axis=0, keepdims=True
        )


def per_device(cotangent, hidden, routes, numerators, w_down):
    tokens, model = cotangent.shape
    top_k, width = hidden.shape[1], hidden.shape[2]
    experts, replicas = lax.axis_size("expert"), lax.axis_size("replica")
    outer = experts // PLANE
    slots = up(3 * tokens * top_k // (2 * experts), 8)
    stride = up(slots, 16)
    half = width // 2
    padded = up(half + 2, 128)
    share = width // replicas
    group = PLANE * stride
    flip = replicas == 2
    sds = jax.ShapeDtypeStruct
    step = 512
    steps = model // step

    def ring(array):
        pairs = [(e, (e + PLANE) % experts) for e in range(experts)]
        return lax.ppermute(array, "expert", pairs)

    def swap(array, k):
        return lax.ppermute(array, "expert", [(e, e ^ k) for e in range(experts)])

    def exchange(array):
        return lax.all_to_all(array, "expert", split_axis=0, concat_axis=0, tiled=True)

    ext, slot, code = call(
        functools.partial(table_kernel, stride),
        (
            sds((tokens, model + BLOCK), BF),
            sds((experts, tokens), F32),
            sds((top_k, tokens), jnp.int32),
        ),
        4 * experts * tokens * tokens,
        4 * tokens * model,
    )(routes.T, cotangent)

    first, second = call(
        functools.partial(pack_kernel, slots, stride, flip),
        [sds((experts, slots, padded), BF)] * 2,
        4 * experts * stride * top_k * tokens * padded,
        4 * top_k * tokens * padded + 4 * experts * slots * padded,
        scratch_shapes=[pltpu.VMEM((padded, top_k * tokens), BF)],
    )(code, numerators.T, jnp.transpose(hidden, (1, 2, 0)))

    matrix = w_down[0]
    rows, backs = [], []
    block = ext
    for s in range(outer):
        if s:
            block = ring(block)
        sent = call(
            functools.partial(relay_kernel, slots, stride),
            [sds((slots, model), BF)] * PLANE,
            2 * group * tokens * model,
            2 * tokens * model + 2 * group * model,
            scratch_shapes=[pltpu.VMEM((BLOCK, tokens), F32)],
        )(block)
        got = [sent[0]] + [swap(sent[k], k) for k in range(1, PLANE)]
        row, back = call(
            functools.partial(back_kernel, stride),
            [sds((group, model), BF), sds((width, group), F32)],
            2 * group * model * width,
            2 * model * (width + 2 * group),
            grid=(steps,),
            in_specs=[pl.BlockSpec((slots, step), lambda j: (0, j))] * PLANE
            + [pl.BlockSpec((width, step), lambda j: (0, j))],
            out_specs=[
                pl.BlockSpec((group, step), lambda j: (0, j)),
                pl.BlockSpec((width, group), lambda j: (0, 0)),
            ],
        )(*got, matrix)
        rows.append(row)
        backs.append(back)

    def gate(hid, before, is_second):
        return call(
            functools.partial(gate_kernel, outer, stride, is_second, flip),
            [sds((experts, BLOCK), F32), sds((half, outer * group), BF)],
            8 * outer * group * half,
            4 * outer * group * width + 4 * outer * group * half,
            scratch_shapes=[pltpu.VMEM((group, padded), F32)],
        )(*backs, hid, before)

    row_specs = [pl.BlockSpec((group, step), lambda j: (0, j))] * outer
    row_specs.append(pl.BlockSpec((half, outer * group), lambda j: (0, 0)))
    flat = pl.BlockSpec((half, step), lambda j: (0, j))
    row_scratch = pltpu.VMEM((outer * group, step), BF)

    def partial(hidw):
        return call(
            functools.partial(partial_kernel, outer),
            sds((half, model), BF),
            2 * outer * group * model * half,
            2 * model * (outer * group + half),
            grid=(steps,),
            in_specs=row_specs,
            out_specs=flat,
            scratch_shapes=[row_scratch],
        )(*rows, hidw)

    got_first = exchange(first)
    got_second = exchange(second)
    gate_first, hidw_first = gate(got_first, jnp.zeros((experts, BLOCK), F32), False)
    part_first = partial(hidw_first)
    gates, hidw_second = gate(got_second, gate_first, True)
    returned = exchange(gates)
    outs = [sds((share, model), F32), sds((model // BLOCK, share), F32)]
    out_specs = [
        pl.BlockSpec((share, step), lambda j: (0, j)),
        pl.BlockSpec((model // BLOCK, share), lambda j: (0, 0)),
    ]
    table = pltpu.VMEM((up(share, 128), BLOCK), F32)
    if flip:
        other = lax.ppermute(part_first, "replica", [(0, 1), (1, 0)])
        out, scales = call(
            functools.partial(finish_kernel, outer),
            outs,
            2 * outer * group * model * half,
            2 * model * (outer * group + 3 * half),
            grid=(steps,),
            in_specs=row_specs + [flat],
            out_specs=out_specs,
            scratch_shapes=[row_scratch, table],
        )(*rows, hidw_second, other)
    else:
        whole = jnp.concatenate([part_first, partial(hidw_second)], axis=0)
        parts = lax.all_to_all(
            whole.reshape(replicas, share, model), "replica", 0, 0, tiled=True
        )
        out, scales = call(
            gather_sum_kernel,
            outs,
            8 * share * model,
            10 * share * model,
            grid=(steps,),
            in_specs=[pl.BlockSpec((replicas, share, step), lambda j: (0, 0, j))],
            out_specs=out_specs,
            scratch_shapes=[table],
        )(parts)
    gate_grad = call(pick_kernel, sds((top_k, tokens), F32), 1 << 16, 1 << 16)(
        slot, routes.T, returned
    )
    return gate_grad.T, scales.T[None], out[None]


def solution(mesh):
    return jax.shard_map(
        per_device,
        mesh=mesh,
        in_specs=(
            P(("expert", "replica"), None),
            P(("expert", "replica"), None, None),
            P(("expert", "replica"), None),
            P(("expert", "replica"), None),
            P("expert", None, None),
        ),
        out_specs=(
            P(("expert", "replica"), None),
            P("expert", "replica", None),
            P("expert", "replica", None),
        ),
        check_vma=False,
    )
```

```python
import functools

import jax
import jax.numpy as jnp
from jax import lax
from jax.experimental import pallas as pl
from jax.experimental.pallas import tpu as pltpu
from jax.sharding import PartitionSpec as P

BLOCK = 128
PLANE = 4
BF = jnp.bfloat16
F32 = jnp.float32
NT = (((1,), (1,)), ((), ()))
VMEM_BYTES = 24 * 1024 * 1024


def up(value, unit):
    return -(-value // unit) * unit


def call(kernel, out_shape, pace=0, **kw):
    return pl.pallas_call(
        kernel,
        out_shape=out_shape,
        cost_estimate=pl.CostEstimate(
            flops=1024 + pace * 1_000_000_000, bytes_accessed=1024, transcendentals=0
        ),
        compiler_params=pltpu.CompilerParams(vmem_limit_bytes=VMEM_BYTES),
        **kw,
    )


def table_kernel(stride, routes_ref, cot_ref, ext_ref, slot_ref, code_ref):
    experts, tokens = slot_ref.shape
    top_k = routes_ref.shape[0]
    model = cot_ref.shape[1]
    routes = routes_ref[...]
    ids = lax.broadcasted_iota(jnp.int32, (experts, tokens), 0)
    mask = jnp.zeros((experts, tokens), F32)
    for k in range(top_k):
        mask += jnp.where(routes[k : k + 1, :] == ids, 1.0, 0.0)
    earlier = lax.broadcasted_iota(jnp.int32, (tokens, tokens), 0) < lax.broadcasted_iota(
        jnp.int32, (tokens, tokens), 1
    )
    rank = jnp.dot(
        mask.astype(BF), jnp.where(earlier, 1.0, 0.0).astype(BF), preferred_element_type=F32
    )
    slot = jnp.where(mask > 0.5, rank, -1.0)
    slot_ref[...] = slot
    me = lax.axis_index("expert")
    steps = (routes >> 2) - (me >> 2)
    steps = jnp.where(steps < 0, steps + experts // PLANE, steps)
    rel = steps * PLANE + ((routes & 3) ^ (me & 3))
    for k in range(top_k):
        own = jnp.sum(
            jnp.where(routes[k : k + 1, :] == ids, slot, 0.0), axis=0, keepdims=True
        ).astype(jnp.int32)
        code_ref[k : k + 1, :] = rel[k : k + 1, :] * stride + own
    wide = jnp.concatenate([slot, jnp.zeros((BLOCK - experts, tokens), F32)], axis=0)
    ext_ref[:, 0:model] = cot_ref[...]
    ext_ref[:, model : model + BLOCK] = wide.T.astype(BF)


def halves(flip):
    mine = lax.axis_index("replica") if flip else 1
    return 1 - mine, mine


def select(slots, stride, table, cot_ref, outs):
    me = lax.axis_index("expert")
    tokens = cot_ref.shape[0]
    rows = lax.broadcasted_iota(jnp.int32, (stride, tokens), 0).astype(F32)
    pick = jnp.concatenate(
        [jnp.where(table[pl.ds(me ^ k, 1), :] == rows, 1.0, 0.0) for k in range(PLANE)], axis=0
    ).astype(BF)
    model = cot_ref.shape[1]
    step = min(512, model)
    for c in range(0, model, step):
        got = jnp.dot(pick, cot_ref[:, c : c + step], preferred_element_type=F32)
        for k in range(PLANE):
            outs[k][:, c : c + step] = got[k * stride : k * stride + slots, :].astype(BF)


def first_kernel(slots, stride, flip, slot_ref, cot_ref, code_ref, num_ref, hid_ref, *refs):
    outs, table = refs[:PLANE], refs[PLANE]
    select(slots, stride, slot_ref, cot_ref, outs)
    model = cot_ref.shape[1]
    top_k, width, tokens = hid_ref.shape
    half = width // 2
    padded = table.shape[0] // 2
    code = jnp.concatenate([code_ref[k : k + 1, :] for k in range(top_k)], axis=1)
    group = PLANE * stride
    for n, part in enumerate(halves(flip)):
        at = pl.multiple_of(part * half, 16) if flip else part * half
        for k in range(top_k):
            lanes = slice(k * tokens, (k + 1) * tokens)
            table[n * padded : n * padded + half, lanes] = hid_ref[k, pl.ds(at, half), :]
            weight = num_ref[k : k + 1, :].astype(F32) * (1.0 / 1024.0)
            high = weight.astype(BF).astype(F32)
            rows = lax.broadcasted_iota(jnp.int32, (padded - half, tokens), 0)
            tail = jnp.where(rows == 0, high, jnp.where(rows == 1, weight - high, 0.0))
            table[n * padded + half : (n + 1) * padded, lanes] = tail.astype(BF)
    for s in range((outs[0].shape[1] - model) // (2 * padded)):
        rows = lax.broadcasted_iota(jnp.int32, (group, top_k * tokens), 0) + s * group
        pick = jnp.where(rows == code, 1.0, 0.0).astype(BF)
        got = lax.dot_general(pick, table[...], NT, preferred_element_type=F32)
        at = model + s * 2 * padded
        for k in range(PLANE):
            outs[k][:, at : at + 2 * padded] = got[k * stride : k * stride + slots, :].astype(BF)


def relay_kernel(slots, stride, ext_ref, *refs):
    outs, table = refs[-1 - PLANE : -1], refs[-1]
    model = outs[0].shape[1]
    table[...] = ext_ref[:, model : model + BLOCK].astype(F32).T
    select(slots, stride, table, ext_ref.at[:, pl.ds(0, model)], outs)


def regroup_kernel(model, *refs):
    outs = refs[PLANE:]
    padded = outs[0].shape[2]
    for s, out_ref in enumerate(outs):
        at = model + (s + 1) * padded
        for k in range(PLANE):
            out_ref[k] = refs[k][:, at : at + padded]


def fill(table, at, piece, stride):
    wide = piece.astype(F32)
    short = stride - wide.shape[0]
    if short:
        wide = jnp.concatenate([wide, jnp.zeros((short, wide.shape[1]), F32)], axis=0)
    table[at : at + stride, :] = wide.astype(table.dtype)


def halves(flip):
    mine = lax.axis_index("replica") if flip else 1
    return 1 - mine, mine


def stage_kernel(stage, stride, flip, split, *refs):
    pieces, w_ref, refs = refs[:PLANE], refs[PLANE], refs[PLANE + 1 :]
    all_rows, all_hidw, gate_ref, rows, hids, hidw, done = refs[-7:]
    group = PLANE * stride
    width, model = w_ref.shape
    half = width // 2
    padded = hids.shape[1] // 2
    for k, piece in enumerate(pieces):
        fill(rows, k * stride, piece[:, 0:model], stride)
    copy = pltpu.make_async_copy(rows, all_rows.at[pl.ds(stage * group, group)], done.at[0])
    copy.start()
    for k in range(PLANE):
        hid = refs[0][k] if split else pieces[k][:, model : model + 2 * padded]
        fill(hids, k * stride, hid, stride)
    gate = 0.0
    for n, part in enumerate(halves(flip)):
        at = pl.multiple_of(part * half, 16) if flip else part * half
        flipped = hids[:, n * padded : (n + 1) * padded].T
        hid = flipped[0:half, :]
        weight = flipped[half : half + 1, :] + flipped[half + 1 : half + 2, :]
        hidw[n * half : (n + 1) * half, :] = (hid * weight).astype(BF)
        back = lax.dot_general(
            w_ref[pl.ds(at, half), :], rows[...], NT, preferred_element_type=F32
        )
        gate += jnp.sum(back * hid, axis=0, keepdims=True)
    second = pltpu.make_async_copy(
        hidw, all_hidw.at[:, pl.ds(stage * group, group)], done.at[1]
    )
    second.start()
    gate_ref[...] = jnp.zeros_like(gate_ref)
    for k in range(PLANE):
        gate_ref[k : k + 1, 0:stride] = gate[:, k * stride : (k + 1) * stride]
    copy.wait()
    second.wait()


def source(outer, s, k):
    me = lax.axis_index("expert")
    ring = (me >> 2) - s
    ring = jnp.where(ring < 0, ring + outer, ring)
    return ring * PLANE + ((me & 3) ^ k)


def partial_kernel(outer, rows_ref, hidw_ref, *refs):
    gates, (send_ref, mine_ref, gate_ref) = refs[:outer], refs[outer:]

    @pl.when(pl.program_id(0) == 0)
    def _():
        for s in range(outer):
            for k in range(PLANE):
                gate_ref[pl.ds(source(outer, s, k), 1), :] = gates[s][k : k + 1, :]

    half = mine_ref.shape[0]
    got = jnp.dot(hidw_ref[...], rows_ref[...], preferred_element_type=F32)
    send_ref[...] = got[0:half].astype(BF)
    mine_ref[...] = got[half:].astype(mine_ref.dtype)


def finish_kernel(own_ref, others_ref, out_ref, scale_ref, table):
    step = pl.program_id(0)
    share, width = out_ref.shape
    lanes = lax.broadcasted_iota(jnp.int32, (share, BLOCK), 1)

    @pl.when(step == 0)
    def _():
        table[...] = jnp.zeros_like(table)

    kept = table[0:share, :]
    for b in range(width // BLOCK):
        span = slice(b * BLOCK, (b + 1) * BLOCK)
        terms = [others_ref[n, :, span].astype(F32) for n in range(others_ref.shape[0])]
        if own_ref is not None:
            terms.append(own_ref[:, span])
        top = functools.reduce(jnp.maximum, [jnp.abs(term) for term in terms])
        scale = jnp.max(top, axis=1, keepdims=True) + 1e-6
        out_ref[:, span] = functools.reduce(jnp.add, terms) * (1.0 / scale)
        kept = jnp.where(lanes == step * (width // BLOCK) + b, scale, kept)
    table[0:share, :] = kept

    @pl.when(step == pl.num_programs(0) - 1)
    def _():
        scale_ref[...] = table[...].T[0 : scale_ref.shape[0], 0:share]


def pick_kernel(after_ref, slot_ref, routes_ref, rows_ref, out_ref):
    experts, tokens = slot_ref.shape
    slot = jnp.maximum(slot_ref[...], 0.0).astype(jnp.int32)
    value = jnp.take_along_axis(rows_ref[...], slot, axis=1)
    ids = lax.broadcasted_iota(jnp.int32, (experts, tokens), 0)
    for k in range(out_ref.shape[0]):
        out_ref[k : k + 1, :] = jnp.sum(
            jnp.where(routes_ref[k : k + 1, :] == ids, value, 0.0), axis=0, keepdims=True
        )


def per_device(cotangent, hidden, routes, numerators, w_down):
    tokens, model = cotangent.shape
    top_k, width = hidden.shape[1], hidden.shape[2]
    experts, replicas = lax.axis_size("expert"), lax.axis_size("replica")
    outer = experts // PLANE
    slots = up(3 * tokens * top_k // (2 * experts), 8)
    stride = up(slots, 32)
    half = width // 2
    padded = up(half + 2, 128)
    share = width // replicas
    group = PLANE * stride
    flip = replicas == 2
    sds = jax.ShapeDtypeStruct
    step = 512
    steps = model // step

    def ring(array, by):
        pairs = [(e, (e + by * PLANE) % experts) for e in range(experts)]
        return lax.ppermute(array, "expert", pairs)

    def swap(array, k):
        return lax.ppermute(array, "expert", [(e, e ^ k) for e in range(experts)])

    def exchange(array):
        return lax.all_to_all(array, "expert", split_axis=0, concat_axis=0, tiled=True)

    anywhere = pl.BlockSpec(memory_space=pl.ANY)
    inside = pl.BlockSpec(memory_space=pltpu.VMEM)

    ext, slot, code = call(
        functools.partial(table_kernel, stride),
        (
            sds((tokens, model + BLOCK), BF),
            sds((experts, tokens), F32),
            sds((top_k, tokens), jnp.int32),
        ),
    )(routes.T, cotangent)

    wide = model + outer * 2 * padded
    sent = call(
        functools.partial(first_kernel, slots, stride, flip),
        [sds((slots, wide), BF)] * PLANE,
        15,
        scratch_shapes=[pltpu.VMEM((2 * padded, top_k * tokens), BF)],
    )(slot, cotangent, code, numerators.T, jnp.transpose(hidden, (1, 2, 0)))
    swapped = {k: swap(sent[k], k) for k in (3, 1, 2)}
    stages = {0: [sent[0]] + [swapped[k] for k in range(1, PLANE)]}

    blocks = {0: ext}
    order = [0]
    for s in range(1, outer // 2 + 1):
        blocks[s] = ring(blocks[s - 1], 1)
        order.append(s)
        if outer - s != s:
            blocks[outer - s] = ring(blocks[(outer - s + 1) % outer], -1)
            order.append(outer - s)
    hids = call(
        functools.partial(regroup_kernel, model),
        [sds((PLANE, slots, 2 * padded), BF)] * (outer - 1),
    )(*stages[0])
    hids = {s: ring(hids[s - 1], s) for s in order[1:]}
    for s in order[1:]:
        sent = call(
            functools.partial(relay_kernel, slots, stride),
            [sds((slots, model), BF)] * PLANE,
            15,
            in_specs=[inside, anywhere],
            scratch_shapes=[pltpu.VMEM((BLOCK, tokens), F32)],
        )(blocks[s], swapped[3])
        swapped = {k: swap(sent[k], k) for k in (3, 1, 2)}
        stages[s] = [sent[0]] + [swapped[k] for k in range(1, PLANE)]

    rows, gates = [], {}
    for s in order:
        hid = [hids[s]] if s else []
        *rows, gates[s] = call(
            functools.partial(stage_kernel, s, stride, flip, bool(s)),
            [
                sds((outer * group, model), BF),
                sds((width, outer * group), BF),
                sds((PLANE, BLOCK), F32),
            ],
            in_specs=[inside] * (PLANE + 1 + len(hid)) + [anywhere] * len(rows),
            out_specs=[anywhere, anywhere, inside],
            input_output_aliases={PLANE + 1 + len(hid) + n: n for n in range(len(rows))},
            scratch_shapes=[
                pltpu.VMEM((group, model), BF),
                pltpu.VMEM((group, 2 * padded), F32),
                pltpu.VMEM((width, group), BF),
                pltpu.SemaphoreType.DMA((2,)),
            ],
        )(*stages[s], w_down[0], *hid, *rows)

    flat = pl.BlockSpec((half, step), lambda j: (0, j))
    send, mine, gates = call(
        functools.partial(partial_kernel, outer),
        [
            sds((half, model), BF),
            sds((half, model), F32 if flip else BF),
            sds((experts, BLOCK), F32),
        ],
        grid=(steps,),
        in_specs=[
            pl.BlockSpec((outer * group, step), lambda j: (0, j)),
            pl.BlockSpec((width, outer * group), lambda j: (0, 0)),
        ]
        + [pl.BlockSpec((PLANE, BLOCK), lambda j: (0, 0))] * outer,
        out_specs=[flat, flat, pl.BlockSpec((experts, BLOCK), lambda j: (0, 0))],
    )(*rows, *[gates[s] for s in range(outer)])
    returned = exchange(gates)
    if flip:
        kernel = finish_kernel
        others = lax.ppermute(send, "replica", [(0, 1), (1, 0)])[None]
        operands, specs = [mine], [flat]
    else:
        kernel = functools.partial(finish_kernel, None)
        both = jnp.concatenate([send, mine], axis=0).reshape(replicas, share, model)
        others = lax.all_to_all(both, "replica", 0, 0, tiled=True)
        operands, specs = [], []
    out, scales = call(
        kernel,
        [sds((share, model), F32), sds((model // BLOCK, share), F32)],
        grid=(steps,),
        in_specs=specs + [pl.BlockSpec((others.shape[0], share, step), lambda j: (0, 0, j))],
        out_specs=[
            pl.BlockSpec((share, step), lambda j: (0, j)),
            pl.BlockSpec((model // BLOCK, share), lambda j: (0, 0)),
        ],
        scratch_shapes=[pltpu.VMEM((up(share, 128), BLOCK), F32)],
    )(*operands, others)
    gate_grad = call(
        pick_kernel,
        sds((top_k, tokens), F32),
        in_specs=[anywhere] + [inside] * 3,
        out_specs=inside,
    )(scales, slot, routes.T, returned)
    return gate_grad.T, scales.T[None], out[None]


def solution(mesh):
    return jax.shard_map(
        per_device,
        mesh=mesh,
        in_specs=(
            P(("expert", "replica"), None),
            P(("expert", "replica"), None, None),
            P(("expert", "replica"), None),
            P(("expert", "replica"), None),
            P("expert", None, None),
        ),
        out_specs=(
            P(("expert", "replica"), None),
            P("expert", "replica", None),
            P("expert", "replica", None),
        ),
        check_vma=False,
    )
```

```python
import functools

import jax
import jax.numpy as jnp
from jax import lax
from jax.experimental import pallas as pl
from jax.experimental.pallas import tpu as pltpu
from jax.sharding import PartitionSpec as P

BLOCK = 128
PLANE = 4
BF = jnp.bfloat16
F32 = jnp.float32
NT = (((1,), (1,)), ((), ()))
VMEM_BYTES = 24 * 1024 * 1024
ALL_VMEM = 56 * 1024 * 1024


def up(value, unit):
    return -(-value // unit) * unit


def call(kernel, out_shape, room=VMEM_BYTES, **kw):
    return pl.pallas_call(
        kernel,
        out_shape=out_shape,
        cost_estimate=pl.CostEstimate(
            flops=1024, bytes_accessed=1024, transcendentals=0
        ),
        compiler_params=pltpu.CompilerParams(vmem_limit_bytes=room),
        **kw,
    )


def table_kernel(stride, routes_hbm, cot_hbm, ext_ref, slot_ref, code_ref, routes_ref, done):
    experts, tokens = slot_ref.shape
    top_k = routes_ref.shape[0]
    model = cot_hbm.shape[1]
    cot_copy = pltpu.make_async_copy(cot_hbm, ext_ref.at[:, pl.ds(0, model)], done.at[0])
    routes_copy = pltpu.make_async_copy(routes_hbm, routes_ref, done.at[1])
    cot_copy.start()
    routes_copy.start()
    routes_copy.wait()
    routes = routes_ref[...]
    ids = lax.broadcasted_iota(jnp.int32, (experts, tokens), 0)
    mask = jnp.zeros((experts, tokens), F32)
    for k in range(top_k):
        mask += jnp.where(routes[k : k + 1, :] == ids, 1.0, 0.0)
    earlier = lax.broadcasted_iota(jnp.int32, (tokens, tokens), 0) < lax.broadcasted_iota(
        jnp.int32, (tokens, tokens), 1
    )
    rank = jnp.dot(
        mask.astype(BF), jnp.where(earlier, 1.0, 0.0).astype(BF), preferred_element_type=F32
    )
    slot = jnp.where(mask > 0.5, rank, -1.0)
    slot_ref[...] = slot
    me = lax.axis_index("expert")
    steps = (routes >> 2) - (me >> 2)
    steps = jnp.where(steps < 0, steps + experts // PLANE, steps)
    rel = steps * PLANE + ((routes & 3) ^ (me & 3))
    for k in range(top_k):
        own = jnp.sum(
            jnp.where(routes[k : k + 1, :] == ids, slot, 0.0), axis=0, keepdims=True
        ).astype(jnp.int32)
        code_ref[k : k + 1, :] = rel[k : k + 1, :] * stride + own
    wide = jnp.concatenate([slot, jnp.zeros((BLOCK - experts, tokens), F32)], axis=0)
    ext_ref[:, model : model + BLOCK] = wide.T.astype(BF)
    cot_copy.wait()


def halves(flip):
    mine = lax.axis_index("replica") if flip else 1
    return 1 - mine, mine


def select(slots, stride, table, cot_ref, outs, at=0):
    me = lax.axis_index("expert")
    tokens = cot_ref.shape[0]
    rows = lax.broadcasted_iota(jnp.int32, (stride, tokens), 0).astype(F32)
    pick = jnp.concatenate(
        [jnp.where(table[pl.ds(me ^ k, 1), :] == rows, 1.0, 0.0) for k in range(PLANE)], axis=0
    ).astype(BF)
    model = cot_ref.shape[1]
    step = min(512, model)
    for c in range(0, model, step):
        got = jnp.dot(pick, cot_ref[:, c : c + step], preferred_element_type=F32)
        for k in range(PLANE):
            outs[k][:, at + c : at + c + step] = got[k * stride : k * stride + slots, :].astype(BF)


def pack_kernel(slots, stride, flip, code_ref, num_hbm, hid_hbm, *refs):
    outs, (table, num_ref, hid_ref, done) = refs[:PLANE], refs[PLANE:]
    num_copy = pltpu.make_async_copy(num_hbm, num_ref, done.at[0])
    hid_copy = pltpu.make_async_copy(hid_hbm, hid_ref, done.at[1])
    num_copy.start()
    hid_copy.start()
    num_copy.wait()
    hid_copy.wait()
    top_k, width, tokens = hid_ref.shape
    half = width // 2
    padded = table.shape[0] // 2
    code = jnp.concatenate([code_ref[k : k + 1, :] for k in range(top_k)], axis=1)
    group = PLANE * stride
    for n, part in enumerate(halves(flip)):
        at = pl.multiple_of(part * half, 16) if flip else part * half
        for k in range(top_k):
            lanes = slice(k * tokens, (k + 1) * tokens)
            table[n * padded : n * padded + half, lanes] = hid_ref[k, pl.ds(at, half), :]
            weight = num_ref[k : k + 1, :].astype(F32) * (1.0 / 1024.0)
            high = weight.astype(BF).astype(F32)
            rows = lax.broadcasted_iota(jnp.int32, (padded - half, tokens), 0)
            tail = jnp.where(rows == 0, high, jnp.where(rows == 1, weight - high, 0.0))
            table[n * padded + half : (n + 1) * padded, lanes] = tail.astype(BF)
    for s in range(outs[0].shape[1] // (2 * padded)):
        rows = lax.broadcasted_iota(jnp.int32, (group, top_k * tokens), 0) + s * group
        pick = jnp.where(rows == code, 1.0, 0.0).astype(BF)
        got = lax.dot_general(pick, table[...], NT, preferred_element_type=F32)
        at = s * 2 * padded
        for k in range(PLANE):
            outs[k][:, at : at + 2 * padded] = got[k * stride : k * stride + slots, :].astype(BF)


def relay_kernel(slots, stride, count, *refs):
    blocks, outs, table = refs[:count], refs[-1 - PLANE : -1], refs[-1]
    model = outs[0].shape[1] // count
    for n, ext_ref in enumerate(blocks):
        table[...] = ext_ref[:, model : model + BLOCK].astype(F32).T
        select(slots, stride, table, ext_ref.at[:, pl.ds(0, model)], outs, n * model)


def regroup_kernel(*refs):
    outs = refs[PLANE:]
    padded = outs[0].shape[2]
    for s, out_ref in enumerate(outs):
        at = s * padded
        for k in range(PLANE):
            out_ref[k] = refs[k][:, at : at + padded]


def fill(table, at, piece, stride):
    wide = piece.astype(F32)
    short = stride - wide.shape[0]
    if short:
        wide = jnp.concatenate([wide, jnp.zeros((short, wide.shape[1]), F32)], axis=0)
    table[at : at + stride, :] = wide.astype(table.dtype)


def halves(flip):
    mine = lax.axis_index("replica") if flip else 1
    return 1 - mine, mine


def stage_kernel(place, at, stride, flip, *refs):
    pieces, w_ref, refs = refs[:PLANE], refs[PLANE], refs[PLANE + 1 :]
    hid_ref = refs[0]
    all_rows, all_hidw, gate_ref, rows, hids, hidw, done = refs[-7:]
    group = PLANE * stride
    width, model = w_ref.shape
    half = width // 2
    padded = hids.shape[1] // 2
    for k, piece in enumerate(pieces):
        fill(rows, k * stride, piece[:, at : at + model], stride)
    copy = pltpu.make_async_copy(rows, all_rows.at[pl.ds(place * group, group)], done.at[0])
    copy.start()
    for k in range(PLANE):
        fill(hids, k * stride, hid_ref[k], stride)
    gate = 0.0
    for n, part in enumerate(halves(flip)):
        at = pl.multiple_of(part * half, 16) if flip else part * half
        flipped = hids[:, n * padded : (n + 1) * padded].T
        hid = flipped[0:half, :]
        weight = flipped[half : half + 1, :] + flipped[half + 1 : half + 2, :]
        hidw[n * half : (n + 1) * half, :] = (hid * weight).astype(BF)
        back = lax.dot_general(
            w_ref[pl.ds(at, half), :], rows[...], NT, preferred_element_type=F32
        )
        gate += jnp.sum(back * hid, axis=0, keepdims=True)
    second = pltpu.make_async_copy(
        hidw, all_hidw.at[:, pl.ds(place * group, group)], done.at[1]
    )
    second.start()
    gate_ref[...] = jnp.zeros_like(gate_ref)
    for k in range(PLANE):
        gate_ref[k : k + 1, 0:stride] = gate[:, k * stride : (k + 1) * stride]
    copy.wait()
    second.wait()


def source(outer, s, k):
    me = lax.axis_index("expert")
    ring = (me >> 2) - s
    ring = jnp.where(ring < 0, ring + outer, ring)
    return ring * PLANE + ((me & 3) ^ k)


def early_kernel(rows_ref, hidw_ref, out_ref, mark_ref):
    mark_ref[...] = jnp.zeros_like(mark_ref)
    out_ref[...] = jnp.dot(hidw_ref[...], rows_ref[...], preferred_element_type=F32)


def partial_kernel(order, rows_ref, hidw_ref, early_ref, *refs):
    outer = len(order)
    gates, (send_ref, mine_ref, gate_ref) = refs[:outer], refs[outer:]

    @pl.when(pl.program_id(0) == 0)
    def _():
        for n, s in enumerate(order):
            for k in range(PLANE):
                gate_ref[pl.ds(source(outer, s, k), 1), :] = gates[n][k : k + 1, :]

    half = mine_ref.shape[0]
    got = early_ref[...] + jnp.dot(hidw_ref[...], rows_ref[...], preferred_element_type=F32)
    send_ref[...] = got[0:half].astype(BF)
    mine_ref[...] = got[half:].astype(mine_ref.dtype)


def finish_kernel(own_ref, others_ref, out_ref, scale_ref, table):
    step = pl.program_id(0)
    share, width = out_ref.shape
    lanes = lax.broadcasted_iota(jnp.int32, (share, BLOCK), 1)

    @pl.when(step == 0)
    def _():
        table[...] = jnp.zeros_like(table)

    kept = table[0:share, :]
    for b in range(width // BLOCK):
        span = slice(b * BLOCK, (b + 1) * BLOCK)
        terms = [others_ref[n, :, span].astype(F32) for n in range(others_ref.shape[0])]
        if own_ref is not None:
            terms.append(own_ref[:, span])
        top = functools.reduce(jnp.maximum, [jnp.abs(term) for term in terms])
        scale = jnp.max(top, axis=1, keepdims=True) + 1e-6
        out_ref[:, span] = functools.reduce(jnp.add, terms) * (1.0 / scale)
        kept = jnp.where(lanes == step * (width // BLOCK) + b, scale, kept)
    table[0:share, :] = kept

    @pl.when(step == pl.num_programs(0) - 1)
    def _():
        scale_ref[...] = table[...].T[0 : scale_ref.shape[0], 0:share]


def pick_kernel(after_ref, slot_ref, routes_ref, rows_ref, out_ref):
    experts, tokens = slot_ref.shape
    slot = jnp.maximum(slot_ref[...], 0.0).astype(jnp.int32)
    value = jnp.take_along_axis(rows_ref[...], slot, axis=1)
    ids = lax.broadcasted_iota(jnp.int32, (experts, tokens), 0)
    for k in range(out_ref.shape[0]):
        out_ref[k : k + 1, :] = jnp.sum(
            jnp.where(routes_ref[k : k + 1, :] == ids, value, 0.0), axis=0, keepdims=True
        )


def per_device(cotangent, hidden, routes, numerators, w_down):
    tokens, model = cotangent.shape
    top_k, width = hidden.shape[1], hidden.shape[2]
    experts, replicas = lax.axis_size("expert"), lax.axis_size("replica")
    outer = experts // PLANE
    slots = up(3 * tokens * top_k // (2 * experts), 8)
    stride = up(slots, 32)
    half = width // 2
    padded = up(half + 2, 128)
    share = width // replicas
    group = PLANE * stride
    flip = replicas == 2
    sds = jax.ShapeDtypeStruct
    step = 512
    steps = model // step

    def ring(array, by):
        pairs = [(e, (e + by * PLANE) % experts) for e in range(experts)]
        return lax.ppermute(array, "expert", pairs)

    def swap(array, k):
        return lax.ppermute(array, "expert", [(e, e ^ k) for e in range(experts)])

    def exchange(array):
        return lax.all_to_all(array, "expert", split_axis=0, concat_axis=0, tiled=True)

    anywhere = pl.BlockSpec(memory_space=pl.ANY)
    inside = pl.BlockSpec(memory_space=pltpu.VMEM)

    ext, slot, code = call(
        functools.partial(table_kernel, stride),
        (
            sds((tokens, model + BLOCK), BF),
            sds((experts, tokens), F32),
            sds((top_k, tokens), jnp.int32),
        ),
        ALL_VMEM,
        in_specs=[anywhere] * 2,
        scratch_shapes=[pltpu.VMEM((top_k, tokens), jnp.int32), pltpu.SemaphoreType.DMA((2,))],
    )(routes.T, cotangent)

    packed = call(
        functools.partial(pack_kernel, slots, stride, flip),
        [sds((slots, outer * 2 * padded), BF)] * PLANE,
        ALL_VMEM,
        in_specs=[inside] + [anywhere] * 2,
        scratch_shapes=[
            pltpu.VMEM((2 * padded, top_k * tokens), BF),
            pltpu.VMEM((top_k, tokens), jnp.int32),
            pltpu.VMEM((top_k, width, tokens), BF),
            pltpu.SemaphoreType.DMA((2,)),
        ],
    )(code, numerators.T, jnp.transpose(hidden, (1, 2, 0)))
    opening = [packed[0]] + [swap(packed[k], k) for k in range(1, PLANE)]

    blocks = {0: ext}
    order = [0]
    for s in range(1, outer // 2 + 1):
        blocks[s] = ring(blocks[s - 1], 1)
        order.append(s)
        if outer - s != s:
            blocks[outer - s] = ring(blocks[(outer - s + 1) % outer], -1)
            order.append(outer - s)
    hids = call(
        regroup_kernel,
        [sds((PLANE, slots, 2 * padded), BF)] * outer,
    )(*opening)
    hids = {s: ring(hids[s], s) if s else hids[s] for s in order}

    def relay(batch):
        sent = call(
            functools.partial(relay_kernel, slots, stride, len(batch)),
            [sds((slots, len(batch) * model), BF)] * PLANE,
            scratch_shapes=[pltpu.VMEM((BLOCK, tokens), F32)],
        )(*[blocks[s] for s in batch])
        return [sent[0]] + [swap(sent[k], k) for k in range(1, PLANE)]

    middle, final = relay(order[:-1]), relay(order[-1:])

    def stage(got, n, count, after, rows):
        hid = hids[order[n] if count > 1 else order[-1]]
        return call(
            functools.partial(stage_kernel, n, n * model, stride, flip),
            [
                sds((count * group, model), BF),
                sds((width, count * group), BF),
                sds((PLANE, BLOCK), F32),
            ],
            in_specs=[inside] * (PLANE + 2) + [anywhere] * len(rows) + [inside] * len(after),
            out_specs=[anywhere, anywhere, inside],
            input_output_aliases={PLANE + 2 + i: i for i in range(len(rows))},
            scratch_shapes=[
                pltpu.VMEM((group, model), BF),
                pltpu.VMEM((group, 2 * padded), F32),
                pltpu.VMEM((width, group), BF),
                pltpu.SemaphoreType.DMA((2,)),
            ],
        )(*got, w_down[0], hid, *rows, *after)

    def products(count):
        return [
            pl.BlockSpec((count * group, step), lambda j: (0, j)),
            pl.BlockSpec((width, count * group), lambda j: (0, 0)),
        ]

    rows, gates = [], []
    for n in range(outer - 1):
        *rows, gate = stage(middle, n, outer - 1, [], rows)
        gates.append(gate)
    full = pl.BlockSpec((width, step), lambda j: (0, j))
    early, mark = call(
        early_kernel,
        [sds((width, model), F32), sds((8, BLOCK), F32)],
        grid=(steps,),
        in_specs=products(outer - 1),
        out_specs=[full, pl.BlockSpec((8, BLOCK), lambda j: (0, 0))],
    )(*rows)
    *rows, gate = stage(final, 0, 1, [mark], [])
    gates.append(gate)

    flat = pl.BlockSpec((half, step), lambda j: (0, j))
    send, mine, gates = call(
        functools.partial(partial_kernel, order),
        [
            sds((half, model), BF),
            sds((half, model), F32 if flip else BF),
            sds((experts, BLOCK), F32),
        ],
        grid=(steps,),
        in_specs=products(1) + [full] + [pl.BlockSpec((PLANE, BLOCK), lambda j: (0, 0))] * outer,
        out_specs=[flat, flat, pl.BlockSpec((experts, BLOCK), lambda j: (0, 0))],
    )(*rows, early, *gates)
    returned = exchange(gates)
    if flip:
        kernel = finish_kernel
        others = lax.ppermute(send, "replica", [(0, 1), (1, 0)])[None]
        operands, specs = [mine], [flat]
    else:
        kernel = functools.partial(finish_kernel, None)
        both = jnp.concatenate([send, mine], axis=0).reshape(replicas, share, model)
        others = lax.all_to_all(both, "replica", 0, 0, tiled=True)
        operands, specs = [], []
    out, scales = call(
        kernel,
        [sds((share, model), F32), sds((model // BLOCK, share), F32)],
        grid=(steps,),
        in_specs=specs + [pl.BlockSpec((others.shape[0], share, step), lambda j: (0, 0, j))],
        out_specs=[
            pl.BlockSpec((share, step), lambda j: (0, j)),
            pl.BlockSpec((model // BLOCK, share), lambda j: (0, 0)),
        ],
        scratch_shapes=[pltpu.VMEM((up(share, 128), BLOCK), F32)],
    )(*operands, others)
    gate_grad = call(
        pick_kernel,
        sds((top_k, tokens), F32),
        in_specs=[anywhere] + [inside] * 3,
        out_specs=inside,
    )(scales, slot, routes.T, returned)
    return gate_grad.T, scales.T[None], out[None]


def solution(mesh):
    return jax.shard_map(
        per_device,
        mesh=mesh,
        in_specs=(
            P(("expert", "replica"), None),
            P(("expert", "replica"), None, None),
            P(("expert", "replica"), None),
            P(("expert", "replica"), None),
            P("expert", None, None),
        ),
        out_specs=(
            P(("expert", "replica"), None),
            P("expert", "replica", None),
            P("expert", "replica", None),
        ),
        check_vma=False,
    )
```

```python
import functools

import jax
import jax.numpy as jnp
from jax import lax
from jax.experimental import pallas as pl
from jax.experimental.pallas import tpu as pltpu
from jax.sharding import PartitionSpec as P

BLOCK = 128
PLANE = 4
BF = jnp.bfloat16
F32 = jnp.float32
NT = (((1,), (1,)), ((), ()))
VMEM_BYTES = 24 * 1024 * 1024
ALL_VMEM = 56 * 1024 * 1024


def up(value, unit):
    return -(-value // unit) * unit


def call(kernel, out_shape, room=VMEM_BYTES, flops=1024, **kw):
    return pl.pallas_call(
        kernel,
        out_shape=out_shape,
        cost_estimate=pl.CostEstimate(
            flops=flops, bytes_accessed=1024, transcendentals=0
        ),
        compiler_params=pltpu.CompilerParams(vmem_limit_bytes=room),
        **kw,
    )


def select(slots, table, cot_ref, outs, at=0):
    me = lax.axis_index("expert")
    tokens = cot_ref.shape[0]
    rows = lax.broadcasted_iota(jnp.int32, (slots, tokens), 0).astype(F32)
    pick = jnp.concatenate(
        [jnp.where(table[pl.ds(me ^ k, 1), :] == rows, 1.0, 0.0) for k in range(PLANE)], axis=0
    ).astype(BF)
    model = cot_ref.shape[1]
    step = min(512, model)
    for c in range(0, model, step):
        got = jnp.dot(pick, cot_ref[:, c : c + step], preferred_element_type=F32)
        for k in range(PLANE):
            outs[k][:, at + c : at + c + step] = got[k * slots : (k + 1) * slots, :].astype(BF)


def open_kernel(slots, flip, *refs):
    routes_hbm, num_hbm, hid_hbm, cot_hbm, ext_hbm, *refs = refs
    sent_hbm, (slot_ref, *refs) = refs[:PLANE], refs[PLANE:]
    ext, sent, table, routes_ref, num_ref, hid_ref, done = refs
    experts, tokens = slot_ref.shape
    top_k, width = hid_ref.shape[:2]
    model = cot_hbm.shape[1]
    half = width // 2
    padded = table.shape[0] // 2
    pairs = (
        (routes_hbm, routes_ref),
        (cot_hbm, ext.at[:, pl.ds(0, model)]),
        (num_hbm, num_ref),
        (hid_hbm, hid_ref),
        (ext, ext_hbm),
    )
    copies = [pltpu.make_async_copy(*pair, done.at[n]) for n, pair in enumerate(pairs)]
    for copy in copies[:4]:
        copy.start()
    copies[0].wait()
    routes = routes_ref[...]
    ids = lax.broadcasted_iota(jnp.int32, (experts, tokens), 0)
    mask = jnp.zeros((experts, tokens), F32)
    for k in range(top_k):
        mask += jnp.where(routes[k : k + 1, :] == ids, 1.0, 0.0)
    earlier = lax.broadcasted_iota(jnp.int32, (tokens, tokens), 0) < lax.broadcasted_iota(
        jnp.int32, (tokens, tokens), 1
    )
    rank = jnp.dot(
        mask.astype(BF), jnp.where(earlier, 1.0, 0.0).astype(BF), preferred_element_type=F32
    )
    slot = jnp.where(mask > 0.5, rank, -1.0)
    slot_ref[...] = slot
    wide = jnp.concatenate([slot, jnp.zeros((BLOCK - experts, tokens), F32)], axis=0)
    ext[:, model : model + BLOCK] = wide.T.astype(BF)
    copies[1].wait()
    copies[4].start()
    parts = experts // PLANE * 2 * padded
    lead = sent.shape[2] - parts
    select(slots, slot_ref, ext.at[:, pl.ds(0, lead)], [sent.at[k] for k in range(PLANE)], parts)
    me = lax.axis_index("expert")
    steps = (routes >> 2) - (me >> 2)
    steps = jnp.where(steps < 0, steps + experts // PLANE, steps)
    rel = steps * PLANE + ((routes & 3) ^ (me & 3))
    codes = []
    for k in range(top_k):
        own = jnp.sum(
            jnp.where(routes[k : k + 1, :] == ids, slot, 0.0), axis=0, keepdims=True
        ).astype(jnp.int32)
        codes.append(rel[k : k + 1, :] * slots + own)
    code = jnp.concatenate(codes, axis=1)
    rows = lax.broadcasted_iota(jnp.int32, (experts * slots, top_k * tokens), 0)
    pick = jnp.where(rows == code, 1.0, 0.0).astype(BF)
    copies[2].wait()
    copies[3].wait()
    for n, part in enumerate(halves(flip)):
        at = pl.multiple_of(part * half, 16) if flip else part * half
        for k in range(top_k):
            lanes = slice(k * tokens, (k + 1) * tokens)
            table[n * padded : n * padded + half, lanes] = hid_ref[k, pl.ds(at, half), :]
            weight = num_ref[k : k + 1, :].astype(F32) * (1.0 / 1024.0)
            high = weight.astype(BF).astype(F32)
            rows = lax.broadcasted_iota(jnp.int32, (padded - half, tokens), 0)
            tail = jnp.where(rows == 0, high, jnp.where(rows == 1, weight - high, 0.0))
            table[n * padded + half : (n + 1) * padded, lanes] = tail.astype(BF)
    got = lax.dot_general(pick, table[...], NT, preferred_element_type=F32)
    for s in range(experts // PLANE):
        lanes = slice(s * 2 * padded, (s + 1) * 2 * padded)
        for k in range(PLANE):
            at = (s * PLANE + k) * slots
            sent[k, :, lanes] = got[at : at + slots, :].astype(BF)
    copies = copies[4:]
    for k in range(PLANE):
        copies.append(pltpu.make_async_copy(sent.at[k], sent_hbm[k], done.at[5 + k]))
        copies[-1].start()
    for copy in copies:
        copy.wait()


def relay_kernel(slots, count, begin, *refs):
    blocks, outs, table = refs[:count], refs[-1 - PLANE : -1], refs[-1]
    part = outs[0].shape[1] // count
    model = begin + part
    for n, ext_ref in enumerate(blocks):
        table[...] = ext_ref[:, model : model + BLOCK].astype(F32).T
        select(slots, table, ext_ref.at[:, pl.ds(begin, part)], outs, n * part)


def forward_kernel(*refs):
    del refs


def regroup_kernel(s, *refs):
    out_ref = refs[-1]
    padded = out_ref.shape[2]
    for k in range(PLANE):
        out_ref[k] = refs[k][:, s * padded : (s + 1) * padded]


def fill(table, at, piece, stride):
    wide = piece.astype(F32)
    short = stride - wide.shape[0]
    if short:
        wide = jnp.concatenate([wide, jnp.zeros((short, wide.shape[1]), F32)], axis=0)
    table[at : at + stride, :] = wide.astype(table.dtype)


def halves(flip):
    mine = lax.axis_index("replica") if flip else 1
    return 1 - mine, mine


def stage_kernel(place, spans, stride, flip, *refs):
    arrays, refs = refs[: PLANE * len(spans)], refs[PLANE * len(spans) :]
    w_ref, refs = refs[0], refs[1:]
    hid_ref = refs[0]
    all_rows, all_hidw, gate_ref, rows, hids, hidw, done = refs[-7:]
    group = PLANE * stride
    width, model = w_ref.shape
    half = width // 2
    padded = hids.shape[1] // 2
    to = 0
    for n, (at, count) in enumerate(spans):
        for k in range(PLANE):
            piece = arrays[n * PLANE + k][:, at : at + count]
            fill(rows.at[:, pl.ds(to, count)], k * stride, piece, stride)
        to += count
    copy = pltpu.make_async_copy(rows, all_rows.at[pl.ds(place * group, group)], done.at[0])
    copy.start()
    for k in range(PLANE):
        fill(hids, k * stride, hid_ref[k], stride)
    gate = 0.0
    for n, part in enumerate(halves(flip)):
        at = pl.multiple_of(part * half, 16) if flip else part * half
        flipped = hids[:, n * padded : (n + 1) * padded].T
        hid = flipped[0:half, :]
        weight = flipped[half : half + 1, :] + flipped[half + 1 : half + 2, :]
        hidw[n * half : (n + 1) * half, :] = (hid * weight).astype(BF)
        back = lax.dot_general(
            w_ref[pl.ds(at, half), :], rows[...], NT, preferred_element_type=F32
        )
        gate += jnp.sum(back * hid, axis=0, keepdims=True)
    second = pltpu.make_async_copy(
        hidw, all_hidw.at[:, pl.ds(place * group, group)], done.at[1]
    )
    second.start()
    gate_ref[...] = jnp.zeros_like(gate_ref)
    for k in range(PLANE):
        gate_ref[k : k + 1, 0:stride] = gate[:, k * stride : (k + 1) * stride]
    copy.wait()
    second.wait()


def source(outer, s, k):
    me = lax.axis_index("expert")
    return lax.rem((me >> 2) - s + outer, outer) * PLANE + ((me & 3) ^ k)


def early_kernel(rows_ref, hidw_ref, out_ref, mark_ref):
    mark_ref[...] = jnp.zeros_like(mark_ref)
    got = jnp.dot(hidw_ref[...], rows_ref[...], preferred_element_type=F32)
    out_ref[...] = got.astype(BF)


def partial_kernel(rows_ref, hidw_ref, early_ref, *refs):
    send_ref, mine_ref = refs[-2:]
    half = mine_ref.shape[0]
    got = early_ref[...].astype(F32) + jnp.dot(
        hidw_ref[...], rows_ref[...], preferred_element_type=F32
    )
    send_ref[...] = got[0:half].astype(BF)
    mine_ref[...] = got[half:].astype(BF)


def combine_kernel(outer, *refs):
    gates, outs = refs[:outer], refs[-PLANE:]
    for k, out_ref in enumerate(outs):
        for s, gate_ref in enumerate(gates):
            out_ref[s : s + 1, :] = gate_ref[k : k + 1, :]


def pick_gates(slot_ref, routes_ref, homes, gate_ref, rows):
    experts, tokens = slot_ref.shape
    for k in range(PLANE):
        for s in range(experts // PLANE):
            rows[pl.ds(source(experts // PLANE, -s, k), 1), :] = homes[k][s : s + 1, :]
    slot = jnp.maximum(slot_ref[...], 0.0).astype(jnp.int32)
    value = jnp.take_along_axis(rows[...], slot, axis=1)
    ids = lax.broadcasted_iota(jnp.int32, (experts, tokens), 0)
    for k in range(gate_ref.shape[0]):
        gate_ref[k : k + 1, :] = jnp.sum(
            jnp.where(routes_ref[k : k + 1, :] == ids, value, 0.0), axis=0, keepdims=True
        )


def finish_kernel(count, *refs):
    own, others_ref, refs = refs[:count], refs[count], refs[count + 1 :]
    if len(refs) > 3:
        slot_ref, routes_ref, *homes = refs[: 2 + PLANE]
        out_ref, scale_ref, gate_ref, table, rows = refs[-5:]

        @pl.when(pl.program_id(0) == 0)
        def _():
            pick_gates(slot_ref, routes_ref, homes, gate_ref, rows)

    else:
        out_ref, scale_ref, table = refs
    step = pl.program_id(0)
    share, width = out_ref.shape
    lanes = lax.broadcasted_iota(jnp.int32, (share, BLOCK), 1)

    @pl.when(step == 0)
    def _():
        table[...] = jnp.zeros_like(table)

    kept = table[0:share, :]
    for b in range(width // BLOCK):
        span = slice(b * BLOCK, (b + 1) * BLOCK)
        terms = [others_ref[n, :, span].astype(F32) for n in range(others_ref.shape[0])]
        terms += [ref[:, span].astype(F32) for ref in own]
        top = functools.reduce(jnp.maximum, [jnp.abs(term) for term in terms])
        scale = jnp.max(top, axis=1, keepdims=True) + 1e-6
        out_ref[:, span] = functools.reduce(jnp.add, terms) * (1.0 / scale)
        kept = jnp.where(lanes == step * (width // BLOCK) + b, scale, kept)
    table[0:share, :] = kept

    @pl.when(step == pl.num_programs(0) - 1)
    def _():
        scale_ref[...] = table[...].T[0 : scale_ref.shape[0], 0:share]


def joined(count, spare, *refs):
    if spare:
        refs = refs[: count + 3 + PLANE] + refs[count + 3 + PLANE + spare :]
    finish_kernel(count, *refs)


def per_device(cotangent, hidden, routes, numerators, w_down):
    tokens, model = cotangent.shape
    top_k, width = hidden.shape[1], hidden.shape[2]
    experts, replicas = lax.axis_size("expert"), lax.axis_size("replica")
    outer = experts // PLANE
    slots = up(3 * tokens * top_k // (2 * experts), 8)
    stride = up(slots, 32)
    half = width // 2
    padded = up(half + 2, 128)
    share = width // replicas
    group = PLANE * stride
    flip = replicas == 2
    sds = jax.ShapeDtypeStruct
    step = 512
    steps = model // step

    def ring(array, by):
        pairs = [(e, (e + by * PLANE) % experts) for e in range(experts)]
        return lax.ppermute(array, "expert", pairs)

    def swap(array, k):
        return lax.ppermute(array, "expert", [(e, e ^ k) for e in range(experts)])

    anywhere = pl.BlockSpec(memory_space=pl.ANY)
    inside = pl.BlockSpec(memory_space=pltpu.VMEM)

    lead = model // 2
    wide = outer * 2 * padded + lead
    ext, *packed, slot = call(
        functools.partial(open_kernel, slots, flip),
        [sds((tokens, model + BLOCK), BF)]
        + [sds((slots, wide), BF)] * PLANE
        + [sds((experts, tokens), F32)],
        ALL_VMEM,
        in_specs=[anywhere] * 4,
        out_specs=[anywhere] * (1 + PLANE) + [inside],
        scratch_shapes=[
            pltpu.VMEM((tokens, model + BLOCK), BF),
            pltpu.VMEM((PLANE, slots, wide), BF),
            pltpu.VMEM((2 * padded, top_k * tokens), BF),
            pltpu.VMEM((top_k, tokens), jnp.int32),
            pltpu.VMEM((top_k, tokens), jnp.int32),
            pltpu.VMEM((top_k, width, tokens), BF),
            pltpu.SemaphoreType.DMA((5 + PLANE,)),
        ],
    )(routes.T, numerators.T, jnp.transpose(hidden, (1, 2, 0)), cotangent)
    opening = [packed[0]] + [swap(packed[k], k) for k in range(1, PLANE)]

    blocks = {0: ext}
    order = [0]
    for s in range(1, outer // 2 + 1):
        blocks[s] = ring(blocks[s - 1], 1)
        order.append(s)
        if outer - s != s:
            blocks[outer - s] = ring(blocks[(outer - s + 1) % outer], -1)
            order.append(outer - s)
    def regroup(s, after):
        return call(
            functools.partial(regroup_kernel, s),
            sds((PLANE, slots, 2 * padded), BF),
            in_specs=[inside] * PLANE + [anywhere] * len(after),
        )(*opening, *after)

    hids = {0: regroup(0, [])}
    for n, s in enumerate(order[1:]):
        hids[s] = ring(regroup(s, [blocks[order[-1]]] if n else []), s)

    def gated(arrays, after):
        return call(
            forward_kernel,
            [sds(array.shape, array.dtype) for array in arrays],
            in_specs=[anywhere] * (len(arrays) + len(after)),
            out_specs=[anywhere] * len(arrays),
            input_output_aliases={n: n for n in range(len(arrays))},
        )(*arrays, *after)

    def relay(batch, after, begin=0):
        sent = call(
            functools.partial(relay_kernel, slots, len(batch), begin),
            [sds((slots, len(batch) * (model - begin)), BF)] * PLANE,
            scratch_shapes=[pltpu.VMEM((BLOCK, tokens), F32)],
        )(*[blocks[s] for s in batch])
        moved = gated(sent[1:], after)
        return [sent[0]] + [swap(moved[k - 1], k) for k in range(1, PLANE)]

    middle = relay(order[1:-1], opening[1:])
    late = relay(order[-1:], [hids[order[1]]])
    final = relay([0], [*middle[1:], hids[order[-2]]], lead)

    def stage(parts, hid, place, count, after, rows):
        arrays = [array for got, _ in parts for array in got]
        fixed = len(arrays) + 2
        return call(
            functools.partial(stage_kernel, place, [span for _, span in parts], stride, flip),
            [
                sds((count * group, model), BF),
                sds((width, count * group), BF),
                sds((PLANE, BLOCK), F32),
            ],
            flops=2_000_000_000,
            in_specs=[inside] * fixed + [anywhere] * len(rows) + [inside] * len(after),
            out_specs=[anywhere, anywhere, inside],
            input_output_aliases={fixed + i: i for i in range(len(rows))},
            scratch_shapes=[
                pltpu.VMEM((group, model), BF),
                pltpu.VMEM((group, 2 * padded), F32),
                pltpu.VMEM((width, group), BF),
                pltpu.SemaphoreType.DMA((2,)),
            ],
        )(*arrays, w_down[0], hid, *rows, *after)

    def products(count):
        return [
            pl.BlockSpec((count * group, step), lambda j: (0, j)),
            pl.BlockSpec((width, count * group), lambda j: (0, 0)),
        ]

    sources = {s: [(middle, (n * model, model))] for n, s in enumerate(order[1:-1])}
    sources[order[-1]] = [(late, (0, model))]
    sources[0] = [(opening, (wide - lead, lead)), (final, (0, model - lead))]
    rows, gates = [], {}
    for n, s in enumerate(order[1:-1]):
        *rows, gates[s] = stage(sources[s], hids[s], n, outer - 2, [], rows)
    full = pl.BlockSpec((width, step), lambda j: (0, j))
    early, mark = call(
        early_kernel,
        [sds((width, model), BF), sds((8, BLOCK), F32)],
        flops=3_500_000_000,
        grid=(steps,),
        in_specs=products(outer - 2),
        out_specs=[full, pl.BlockSpec((8, BLOCK), lambda j: (0, 0))],
    )(*rows)
    *rows, gates[order[-1]] = stage(
        sources[order[-1]], hids[order[-1]], 0, 2, [mark], []
    )
    for s, gate in zip(
        order[1:-1], gated([gates[s] for s in order[1:-1]], [gates[order[-1]]])
    ):
        gates[s] = gate
    *rows, gates[0] = stage(sources[0], hids[0], 1, 2, [], rows)
    gates = [ring(gates[s], -s) if s else gates[s] for s in range(outer)]

    token_spec = pl.BlockSpec((top_k, tokens), lambda j: (0, 0))
    home = pl.BlockSpec((outer, BLOCK), lambda j: (0, 0))
    middle_step = steps // 2

    def column(first, height):
        return pl.BlockSpec((height, step), lambda j: (0, j + first))

    def partial(first, after):
        return call(
            partial_kernel,
            [sds((half, model // 2), BF)] * 2,
            grid=(middle_step,),
            in_specs=[
                column(first, 2 * group),
                pl.BlockSpec((width, 2 * group), lambda j: (0, 0)),
                column(first, width),
            ]
            + [anywhere] * len(after),
            out_specs=[column(0, half)] * 2,
        )(*rows, early, *after)

    def finish(first, send, mine, out, extra):
        if flip:
            others = lax.ppermute(send, "replica", [(0, 1), (1, 0)])[None]
            own = [mine]
        else:
            both = jnp.concatenate([send, mine], axis=0).reshape(replicas, share, model // 2)
            others = lax.all_to_all(both, "replica", 0, 0, tiled=True)
            own = []
        specs = [column(0, half)] * len(own)
        specs.append(pl.BlockSpec((others.shape[0], share, step), lambda j: (0, 0, j)))
        outs = [sds((share, model), F32), sds((model // BLOCK, share), F32)]
        out_specs = [
            column(first, share),
            pl.BlockSpec((model // 2 // BLOCK, share), lambda j: (first // middle_step, 0)),
        ]
        scratch = [pltpu.VMEM((up(share, 128), BLOCK), F32)]
        if extra:
            specs += [pl.BlockSpec((experts, tokens), lambda j: (0, 0)), token_spec]
            specs += [home] * PLANE
            outs.append(sds((top_k, tokens), F32))
            out_specs.append(token_spec)
            scratch.append(pltpu.VMEM((experts, BLOCK), F32))
        fixed = len(own) + 1 + len(extra)
        return call(
            functools.partial(joined, len(own), len(out)),
            outs,
            grid=(middle_step,),
            in_specs=specs + [anywhere] * len(out),
            out_specs=out_specs,
            input_output_aliases={fixed + n: n for n in range(len(out))},
            scratch_shapes=scratch,
        )(*own, others, *extra, *out)

    left = partial(0, [])
    right = partial(middle_step, gates[1:])
    homes = call(
        functools.partial(combine_kernel, outer),
        [sds((outer, BLOCK), F32)] * PLANE,
        in_specs=[inside] * outer + [anywhere],
    )(*gates, right[0])
    homes = [homes[0]] + [swap(homes[k], k) for k in range(1, PLANE)]
    out = finish(0, *left, [], [])
    out, scales, gate_grad = finish(middle_step, *right, out, [slot, routes.T, *homes])
    return gate_grad.T, scales.T[None], out[None]


def solution(mesh):
    return jax.shard_map(
        per_device,
        mesh=mesh,
        in_specs=(
            P(("expert", "replica"), None),
            P(("expert", "replica"), None, None),
            P(("expert", "replica"), None),
            P(("expert", "replica"), None),
            P("expert", None, None),
        ),
        out_specs=(
            P(("expert", "replica"), None),
            P("expert", "replica", None),
            P("expert", "replica", None),
        ),
        check_vma=False,
    )
```

```python
import functools

import jax
import jax.numpy as jnp
from jax import lax
from jax.experimental import pallas as pl
from jax.experimental.pallas import tpu as pltpu
from jax.sharding import PartitionSpec as P

BLOCK = 128
PLANE = 4
BF = jnp.bfloat16
F32 = jnp.float32
NT = (((1,), (1,)), ((), ()))
VMEM_BYTES = 24 * 1024 * 1024
ALL_VMEM = 56 * 1024 * 1024


def up(value, unit):
    return -(-value // unit) * unit


def call(kernel, out_shape, room=VMEM_BYTES, flops=1024, **kw):
    return pl.pallas_call(
        kernel,
        out_shape=out_shape,
        cost_estimate=pl.CostEstimate(
            flops=flops, bytes_accessed=1024, transcendentals=0
        ),
        compiler_params=pltpu.CompilerParams(vmem_limit_bytes=room),
        **kw,
    )


def select(slots, table, cot_ref, outs, at=0):
    me = lax.axis_index("expert")
    tokens = cot_ref.shape[0]
    rows = lax.broadcasted_iota(jnp.int32, (slots, tokens), 0).astype(F32)
    pick = jnp.concatenate(
        [jnp.where(table[pl.ds(me ^ k, 1), :] == rows, 1.0, 0.0) for k in range(PLANE)], axis=0
    ).astype(BF)
    model = cot_ref.shape[1]
    step = min(512, model)
    for c in range(0, model, step):
        got = jnp.dot(pick, cot_ref[:, c : c + step], preferred_element_type=F32)
        for k in range(PLANE):
            outs[k][:, at + c : at + c + step] = got[k * slots : (k + 1) * slots, :].astype(BF)


def open_kernel(slots, flip, *refs):
    routes_hbm, num_hbm, hid_hbm, cot_hbm, ext_hbm, *refs = refs
    sent_hbm, (slot_ref, *refs) = refs[:PLANE], refs[PLANE:]
    ext, sent, table, routes_ref, num_ref, hid_ref, done = refs
    experts, tokens = slot_ref.shape
    top_k, width = hid_ref.shape[:2]
    model = cot_hbm.shape[1]
    half = width // 2
    spare = up(width, BLOCK) - width
    pair = 2 * width
    pairs = (
        (routes_hbm, routes_ref),
        (cot_hbm, ext.at[:, pl.ds(0, model)]),
        (num_hbm, num_ref),
        (hid_hbm, hid_ref),
        (ext, ext_hbm),
    )
    copies = [pltpu.make_async_copy(*pair, done.at[n]) for n, pair in enumerate(pairs)]
    for copy in copies[:4]:
        copy.start()

    def leave(first, count, n):
        for k in range(PLANE):
            lanes = pl.ds(first, count)
            copy = pltpu.make_async_copy(
                sent.at[k, :, lanes], sent_hbm[k].at[:, lanes], done.at[5 + n * PLANE + k]
            )
            copy.start()
            copies.append(copy)

    copies[0].wait()
    routes = routes_ref[...]
    ids = lax.broadcasted_iota(jnp.int32, (experts, tokens), 0)
    mask = jnp.zeros((experts, tokens), F32)
    for k in range(top_k):
        mask += jnp.where(routes[k : k + 1, :] == ids, 1.0, 0.0)
    earlier = lax.broadcasted_iota(jnp.int32, (tokens, tokens), 0) < lax.broadcasted_iota(
        jnp.int32, (tokens, tokens), 1
    )
    rank = jnp.dot(
        mask.astype(BF), jnp.where(earlier, 1.0, 0.0).astype(BF), preferred_element_type=F32
    )
    slot = jnp.where(mask > 0.5, rank, -1.0)
    slot_ref[...] = slot
    wide = jnp.concatenate([slot, jnp.zeros((BLOCK - experts, tokens), F32)], axis=0)
    ext[:, model : model + BLOCK] = wide.T.astype(BF)
    copies[1].wait()
    copies[4].start()
    parts = experts // PLANE * width
    lead = sent.shape[2] - parts
    select(slots, slot_ref, ext.at[:, pl.ds(0, lead)], [sent.at[k] for k in range(PLANE)], parts)
    leave(parts, lead, 0)
    me = lax.axis_index("expert")
    steps = (routes >> 2) - (me >> 2)
    steps = jnp.where(steps < 0, steps + experts // PLANE, steps)
    rel = steps * PLANE + ((routes & 3) ^ (me & 3))
    codes = []
    for k in range(top_k):
        own = jnp.sum(
            jnp.where(routes[k : k + 1, :] == ids, slot, 0.0), axis=0, keepdims=True
        ).astype(jnp.int32)
        codes.append(rel[k : k + 1, :] * slots + own)
    code = jnp.concatenate(codes, axis=1)
    rows = lax.broadcasted_iota(jnp.int32, (experts * slots, top_k * tokens), 0)
    pick = jnp.where(rows == code, 1.0, 0.0).astype(BF)
    copies[2].wait()
    copies[3].wait()
    blank = jnp.zeros((spare, top_k * tokens), BF)
    table[0:spare, :] = blank
    table[spare + width :, :] = blank
    for k in range(top_k):
        weight = num_ref[k : k + 1, :].astype(F32) * (1.0 / 1024.0)
        for n, part in enumerate(halves(flip)):
            at = pl.multiple_of(part * half, 16) if flip else part * half
            rows = (hid_ref[k, pl.ds(at, half), :].astype(F32) * weight).astype(BF)
            first = spare + n * half
            table[first : first + half, k * tokens : (k + 1) * tokens] = rows
    size = PLANE * slots
    whole = width + spare
    cut = whole - BLOCK
    for s in range(0, experts // PLANE, 2):
        left = lax.dot_general(
            pick[s * size : (s + 1) * size], table[spare:], NT, preferred_element_type=F32
        )
        right = lax.dot_general(
            pick[(s + 1) * size : (s + 2) * size], table[0:whole], NT, preferred_element_type=F32
        )
        at = s * width
        for k in range(PLANE):
            these = slice(k * slots, (k + 1) * slots)
            sent[k, :, at : at + cut] = left[these, 0:cut].astype(BF)
            sent[k, :, at + cut : at + whole] = (
                left[these, cut:] + right[these, 0:BLOCK]
            ).astype(BF)
            sent[k, :, at + whole : at + pair] = right[these, BLOCK:].astype(BF)
        leave(at, pair, 1 + s // 2)
    for copy in copies[4:]:
        copy.wait()


def relay_kernel(slots, count, begin, *refs):
    blocks, outs, table = refs[:count], refs[-1 - PLANE : -1], refs[-1]
    part = outs[0].shape[1] // count
    model = begin + part
    for n, ext_ref in enumerate(blocks):
        table[...] = ext_ref[:, model : model + BLOCK].astype(F32).T
        select(slots, table, ext_ref.at[:, pl.ds(begin, part)], outs, n * part)


def forward_kernel(*refs):
    del refs


def moved(piece, by):
    return pltpu.roll(piece.astype(F32), by % piece.shape[1], 1) if by else piece.astype(F32)


def regroup_kernel(s, width, *refs):
    out_ref = refs[-1]
    whole = up(width, BLOCK)
    spare = whole - width
    cut = whole - BLOCK
    at = s // 2 * 2 * width + s % 2 * (width - spare)
    lanes = lax.broadcasted_iota(jnp.int32, (out_ref.shape[1], BLOCK), 1)
    for k in range(0, PLANE, 2):
        left = moved(refs[k][:, at : at + whole], -(s % 2) * spare)
        right = moved(refs[k + 1][:, at : at + whole], (1 - s % 2) * spare)
        out_ref[k // 2, :, 0:cut] = left[:, 0:cut].astype(BF)
        out_ref[k // 2, :, cut:whole] = jnp.where(
            lanes < width - cut, left[:, cut:], right[:, 0:BLOCK]
        ).astype(BF)
        out_ref[k // 2, :, whole:] = right[:, BLOCK:].astype(BF)


def fill(table, at, piece, stride):
    wide = piece.astype(F32)
    short = stride - wide.shape[0]
    if short:
        wide = jnp.concatenate([wide, jnp.zeros((short, wide.shape[1]), F32)], axis=0)
    table[at : at + stride, :] = wide.astype(table.dtype)


def halves(flip):
    mine = lax.axis_index("replica") if flip else 1
    return 1 - mine, mine


def stage_kernel(place, spans, stride, flip, *refs):
    arrays, refs = refs[: PLANE * len(spans)], refs[PLANE * len(spans) :]
    w_ref, refs = refs[0], refs[1:]
    hid_ref = refs[0]
    all_rows, all_hidw, gate_ref, rows, hids, hidw, done = refs[-7:]
    group = PLANE * stride
    width, model = w_ref.shape
    half = width // 2
    whole = hids.shape[1]
    spare = whole - width
    to = 0
    for n, (at, count) in enumerate(spans):
        for k in range(PLANE):
            piece = arrays[n * PLANE + k][:, at : at + count]
            fill(rows.at[:, pl.ds(to, count)], k * stride, piece, stride)
        to += count
    copy = pltpu.make_async_copy(rows, all_rows.at[pl.ds(place * group, group)], done.at[0])
    copy.start()
    for k in range(PLANE):
        at = k % 2 * (width - spare)
        fill(hids, k * stride, moved(hid_ref[k // 2, :, at : at + whole], -(k % 2) * spare), stride)
    flipped = hids[...].T
    hidw[...] = flipped[0:width, :].astype(BF)
    gate = 0.0
    for n, part in enumerate(halves(flip)):
        at = pl.multiple_of(part * half, 16) if flip else part * half
        back = lax.dot_general(
            w_ref[pl.ds(at, half), :], rows[...], NT, preferred_element_type=F32
        )
        gate += jnp.sum(back * flipped[n * half : (n + 1) * half, :], axis=0, keepdims=True)
    second = pltpu.make_async_copy(
        hidw, all_hidw.at[:, pl.ds(place * group, group)], done.at[1]
    )
    second.start()
    gate_ref[...] = jnp.zeros_like(gate_ref)
    for k in range(PLANE):
        gate_ref[k : k + 1, 0:stride] = gate[:, k * stride : (k + 1) * stride]
    copy.wait()
    second.wait()


def source(outer, s, k):
    me = lax.axis_index("expert")
    return lax.rem((me >> 2) - s + outer, outer) * PLANE + ((me & 3) ^ k)


def early_kernel(rows_ref, hidw_ref, out_ref, mark_ref):
    mark_ref[...] = jnp.zeros_like(mark_ref)
    got = jnp.dot(hidw_ref[...], rows_ref[...], preferred_element_type=F32)
    out_ref[...] = got.astype(BF)


def partial_kernel(rows_ref, hidw_ref, early_ref, *refs):
    send_ref, mine_ref = refs[-2:]
    half = mine_ref.shape[0]
    got = early_ref[...].astype(F32) + jnp.dot(
        hidw_ref[...], rows_ref[...], preferred_element_type=F32
    )
    send_ref[...] = got[0:half].astype(BF)
    mine_ref[...] = got[half:].astype(BF)


def combine_kernel(outer, *refs):
    gates, outs = refs[:outer], refs[-PLANE:]
    for k, out_ref in enumerate(outs):
        for s, gate_ref in enumerate(gates):
            out_ref[s : s + 1, :] = gate_ref[k : k + 1, :]


def pick_gates(slot_ref, routes_ref, num_ref, homes, gate_ref, rows):
    experts, tokens = slot_ref.shape
    for k in range(PLANE):
        for s in range(experts // PLANE):
            rows[pl.ds(source(experts // PLANE, -s, k), 1), :] = homes[k][s : s + 1, :]
    slot = jnp.maximum(slot_ref[...], 0.0).astype(jnp.int32)
    value = jnp.take_along_axis(rows[...], slot, axis=1)
    ids = lax.broadcasted_iota(jnp.int32, (experts, tokens), 0)
    for k in range(gate_ref.shape[0]):
        got = jnp.sum(
            jnp.where(routes_ref[k : k + 1, :] == ids, value, 0.0), axis=0, keepdims=True
        )
        gate_ref[k : k + 1, :] = got / (num_ref[k : k + 1, :].astype(F32) * (1.0 / 1024.0))


def finish_kernel(count, *refs):
    own, others_ref, refs = refs[:count], refs[count], refs[count + 1 :]
    if len(refs) > 3:
        slot_ref, routes_ref, num_ref, *homes = refs[: 3 + PLANE]
        out_ref, scale_ref, gate_ref, table, rows = refs[-5:]

        @pl.when(pl.program_id(0) == 0)
        def _():
            pick_gates(slot_ref, routes_ref, num_ref, homes, gate_ref, rows)

    else:
        out_ref, scale_ref, table = refs
    step = pl.program_id(0)
    share, width = out_ref.shape
    lanes = lax.broadcasted_iota(jnp.int32, (share, BLOCK), 1)

    @pl.when(step == 0)
    def _():
        table[...] = jnp.zeros_like(table)

    kept = table[0:share, :]
    for b in range(width // BLOCK):
        span = slice(b * BLOCK, (b + 1) * BLOCK)
        terms = [others_ref[n, :, span].astype(F32) for n in range(others_ref.shape[0])]
        terms += [ref[:, span].astype(F32) for ref in own]
        top = functools.reduce(jnp.maximum, [jnp.abs(term) for term in terms])
        scale = jnp.max(top, axis=1, keepdims=True) + 1e-6
        out_ref[:, span] = functools.reduce(jnp.add, terms) * (1.0 / scale)
        kept = jnp.where(lanes == step * (width // BLOCK) + b, scale, kept)
    table[0:share, :] = kept

    @pl.when(step == pl.num_programs(0) - 1)
    def _():
        scale_ref[...] = table[...].T[0 : scale_ref.shape[0], 0:share]


def joined(count, spare, *refs):
    if spare:
        refs = refs[: count + 4 + PLANE] + refs[count + 4 + PLANE + spare :]
    finish_kernel(count, *refs)


def per_device(cotangent, hidden, routes, numerators, w_down):
    tokens, model = cotangent.shape
    top_k, width = hidden.shape[1], hidden.shape[2]
    experts, replicas = lax.axis_size("expert"), lax.axis_size("replica")
    outer = experts // PLANE
    slots = up(3 * tokens * top_k // (2 * experts), 8)
    stride = up(slots, 32)
    half = width // 2
    share = width // replicas
    group = PLANE * stride
    flip = replicas == 2
    sds = jax.ShapeDtypeStruct
    step = 512
    steps = model // step

    def ring(array, by):
        pairs = [(e, (e + by * PLANE) % experts) for e in range(experts)]
        return lax.ppermute(array, "expert", pairs)

    def swap(array, k):
        return lax.ppermute(array, "expert", [(e, e ^ k) for e in range(experts)])

    anywhere = pl.BlockSpec(memory_space=pl.ANY)
    inside = pl.BlockSpec(memory_space=pltpu.VMEM)

    lead = model // 2
    wide = outer * width + lead
    ext, *packed, slot = call(
        functools.partial(open_kernel, slots, flip),
        [sds((tokens, model + BLOCK), BF)]
        + [sds((slots, wide), BF)] * PLANE
        + [sds((experts, tokens), F32)],
        ALL_VMEM,
        in_specs=[anywhere] * 4,
        out_specs=[anywhere] * (1 + PLANE) + [inside],
        scratch_shapes=[
            pltpu.VMEM((tokens, model + BLOCK), BF),
            pltpu.VMEM((PLANE, slots, wide), BF),
            pltpu.VMEM((2 * up(width, BLOCK) - width, top_k * tokens), BF),
            pltpu.VMEM((top_k, tokens), jnp.int32),
            pltpu.VMEM((top_k, tokens), jnp.int32),
            pltpu.VMEM((top_k, width, tokens), BF),
            pltpu.SemaphoreType.DMA((5 + PLANE * (1 + outer // 2),)),
        ],
    )(routes.T, numerators.T, jnp.transpose(hidden, (1, 2, 0)), cotangent)
    opening = [packed[0]] + [swap(packed[k], k) for k in range(1, PLANE)]

    blocks = {0: ext}
    order = [0]
    for s in range(1, outer // 2 + 1):
        blocks[s] = ring(blocks[s - 1], 1)
        order.append(s)
        if outer - s != s:
            blocks[outer - s] = ring(blocks[(outer - s + 1) % outer], -1)
            order.append(outer - s)
    def regroup(s, after):
        return call(
            functools.partial(regroup_kernel, s, width),
            sds((PLANE // 2, slots, 2 * width), BF),
            in_specs=[inside] * PLANE + [anywhere] * len(after),
        )(*opening, *after)

    hids = {0: regroup(0, [])}
    for n, s in enumerate(order[1:]):
        hids[s] = ring(regroup(s, [blocks[order[-1]]] if n else []), s)

    def gated(arrays, after):
        return call(
            forward_kernel,
            [sds(array.shape, array.dtype) for array in arrays],
            in_specs=[anywhere] * (len(arrays) + len(after)),
            out_specs=[anywhere] * len(arrays),
            input_output_aliases={n: n for n in range(len(arrays))},
        )(*arrays, *after)

    def relay(batch, after, begin=0):
        sent = call(
            functools.partial(relay_kernel, slots, len(batch), begin),
            [sds((slots, len(batch) * (model - begin)), BF)] * PLANE,
            scratch_shapes=[pltpu.VMEM((BLOCK, tokens), F32)],
        )(*[blocks[s] for s in batch])
        moved = gated(sent[1:], after)
        return [sent[0]] + [swap(moved[k - 1], k) for k in range(1, PLANE)]

    middle = relay(order[1:-1], opening[1:])
    late = relay(order[-1:], [hids[order[1]]])
    final = relay([0], [*middle[1:], hids[order[-2]]], lead)

    def stage(parts, hid, place, count, after, rows):
        arrays = [array for got, _ in parts for array in got]
        fixed = len(arrays) + 2
        return call(
            functools.partial(stage_kernel, place, [span for _, span in parts], stride, flip),
            [
                sds((count * group, model), BF),
                sds((width, count * group), BF),
                sds((PLANE, BLOCK), F32),
            ],
            flops=2_000_000_000,
            in_specs=[inside] * fixed + [anywhere] * len(rows) + [inside] * len(after),
            out_specs=[anywhere, anywhere, inside],
            input_output_aliases={fixed + i: i for i in range(len(rows))},
            scratch_shapes=[
                pltpu.VMEM((group, model), BF),
                pltpu.VMEM((group, up(width, BLOCK)), F32),
                pltpu.VMEM((width, group), BF),
                pltpu.SemaphoreType.DMA((2,)),
            ],
        )(*arrays, w_down[0], hid, *rows, *after)

    def products(count):
        return [
            pl.BlockSpec((count * group, step), lambda j: (0, j)),
            pl.BlockSpec((width, count * group), lambda j: (0, 0)),
        ]

    sources = {s: [(middle, (n * model, model))] for n, s in enumerate(order[1:-1])}
    sources[order[-1]] = [(late, (0, model))]
    sources[0] = [(opening, (wide - lead, lead)), (final, (0, model - lead))]
    rows, gates = [], {}
    for n, s in enumerate(order[1:-1]):
        *rows, gates[s] = stage(sources[s], hids[s], n, outer - 2, [], rows)
    full = pl.BlockSpec((width, step), lambda j: (0, j))
    early, mark = call(
        early_kernel,
        [sds((width, model), BF), sds((8, BLOCK), F32)],
        flops=3_500_000_000,
        grid=(steps,),
        in_specs=products(outer - 2),
        out_specs=[full, pl.BlockSpec((8, BLOCK), lambda j: (0, 0))],
    )(*rows)
    *rows, gates[order[-1]] = stage(
        sources[order[-1]], hids[order[-1]], 0, 2, [mark], []
    )
    for s, gate in zip(
        order[1:-1], gated([gates[s] for s in order[1:-1]], [gates[order[-1]]])
    ):
        gates[s] = gate
    *rows, gates[0] = stage(sources[0], hids[0], 1, 2, [], rows)
    gates = [ring(gates[s], -s) if s else gates[s] for s in range(outer)]

    token_spec = pl.BlockSpec((top_k, tokens), lambda j: (0, 0))
    home = pl.BlockSpec((outer, BLOCK), lambda j: (0, 0))
    middle_step = steps // 2

    def column(first, height):
        return pl.BlockSpec((height, step), lambda j: (0, j + first))

    def partial(first, after):
        return call(
            partial_kernel,
            [sds((half, model // 2), BF)] * 2,
            grid=(middle_step,),
            in_specs=[
                column(first, 2 * group),
                pl.BlockSpec((width, 2 * group), lambda j: (0, 0)),
                column(first, width),
            ]
            + [anywhere] * len(after),
            out_specs=[column(0, half)] * 2,
        )(*rows, early, *after)

    def finish(first, send, mine, out, extra):
        if flip:
            others = lax.ppermute(send, "replica", [(0, 1), (1, 0)])[None]
            own = [mine]
        else:
            both = jnp.concatenate([send, mine], axis=0).reshape(replicas, share, model // 2)
            others = lax.all_to_all(both, "replica", 0, 0, tiled=True)
            own = []
        specs = [column(0, half)] * len(own)
        specs.append(pl.BlockSpec((others.shape[0], share, step), lambda j: (0, 0, j)))
        outs = [sds((share, model), F32), sds((model // BLOCK, share), F32)]
        out_specs = [
            column(first, share),
            pl.BlockSpec((model // 2 // BLOCK, share), lambda j: (first // middle_step, 0)),
        ]
        scratch = [pltpu.VMEM((up(share, 128), BLOCK), F32)]
        if extra:
            specs += [pl.BlockSpec((experts, tokens), lambda j: (0, 0)), token_spec, token_spec]
            specs += [home] * PLANE
            outs.append(sds((top_k, tokens), F32))
            out_specs.append(token_spec)
            scratch.append(pltpu.VMEM((experts, BLOCK), F32))
        fixed = len(own) + 1 + len(extra)
        return call(
            functools.partial(joined, len(own), len(out)),
            outs,
            grid=(middle_step,),
            in_specs=specs + [anywhere] * len(out),
            out_specs=out_specs,
            input_output_aliases={fixed + n: n for n in range(len(out))},
            scratch_shapes=scratch,
        )(*own, others, *extra, *out)

    left = partial(0, [])
    right = partial(middle_step, gates[1:])
    homes = call(
        functools.partial(combine_kernel, outer),
        [sds((outer, BLOCK), F32)] * PLANE,
        in_specs=[inside] * outer + [anywhere],
    )(*gates, right[0])
    homes = [homes[0]] + [swap(homes[k], k) for k in range(1, PLANE)]
    out = finish(0, *left, [], [])
    out, scales, gate_grad = finish(middle_step, *right, out, [slot, routes.T, numerators.T, *homes])
    return gate_grad.T, scales.T[None], out[None]


def solution(mesh):
    return jax.shard_map(
        per_device,
        mesh=mesh,
        in_specs=(
            P(("expert", "replica"), None),
            P(("expert", "replica"), None, None),
            P(("expert", "replica"), None),
            P(("expert", "replica"), None),
            P("expert", None, None),
        ),
        out_specs=(
            P(("expert", "replica"), None),
            P("expert", "replica", None),
            P("expert", "replica", None),
        ),
        check_vma=False,
    )
```

```python
import functools

import jax
import jax.numpy as jnp
from jax import lax
from jax.experimental import pallas as pl
from jax.experimental.pallas import tpu as pltpu
from jax.sharding import PartitionSpec as P

BLOCK = 128
PLANE = 4
BF = jnp.bfloat16
F32 = jnp.float32
NT = (((1,), (1,)), ((), ()))
VMEM_BYTES = 24 * 1024 * 1024
ALL_VMEM = 56 * 1024 * 1024


def up(value, unit):
    return -(-value // unit) * unit


def call(kernel, out_shape, room=VMEM_BYTES, flops=1024, **kw):
    return pl.pallas_call(
        kernel,
        out_shape=out_shape,
        cost_estimate=pl.CostEstimate(
            flops=flops, bytes_accessed=1024, transcendentals=0
        ),
        compiler_params=pltpu.CompilerParams(vmem_limit_bytes=room),
        **kw,
    )


def select(slots, table, cot_ref, outs, at=0):
    me = lax.axis_index("expert")
    tokens = cot_ref.shape[0]
    rows = lax.broadcasted_iota(jnp.int32, (slots, tokens), 0).astype(F32)
    pick = jnp.concatenate(
        [jnp.where(table[pl.ds(me ^ k, 1), :] == rows, 1.0, 0.0) for k in range(PLANE)], axis=0
    ).astype(BF)
    model = cot_ref.shape[1]
    step = min(512, model)
    for c in range(0, model, step):
        got = jnp.dot(pick, cot_ref[:, c : c + step], preferred_element_type=F32)
        for k in range(PLANE):
            outs[k][:, at + c : at + c + step] = got[k * slots : (k + 1) * slots, :].astype(BF)


def open_kernel(slots, flip, *refs):
    routes_hbm, num_hbm, hid_hbm, cot_hbm, ext_hbm, *refs = refs
    sent_hbm, (slot_ref, *refs) = refs[:PLANE], refs[PLANE:]
    ext, sent, table, routes_ref, num_ref, hid_ref, done = refs
    experts, tokens = slot_ref.shape
    top_k, width = hid_ref.shape[:2]
    model = cot_hbm.shape[1]
    half = width // 2
    spare = up(width, BLOCK) - width
    pair = 2 * width
    pairs = (
        (routes_hbm, routes_ref),
        (cot_hbm, ext.at[:, pl.ds(0, model)]),
        (num_hbm, num_ref),
        (hid_hbm, hid_ref),
        (ext, ext_hbm),
    )
    copies = [pltpu.make_async_copy(*pair, done.at[n]) for n, pair in enumerate(pairs)]
    for copy in copies[:4]:
        copy.start()

    def leave(first, count, n):
        for k in range(PLANE):
            lanes = pl.ds(first, count)
            copy = pltpu.make_async_copy(
                sent.at[k, :, lanes], sent_hbm[k].at[:, lanes], done.at[5 + n * PLANE + k]
            )
            copy.start()
            copies.append(copy)

    copies[0].wait()
    routes = routes_ref[...]
    ids = lax.broadcasted_iota(jnp.int32, (experts, tokens), 0)
    mask = jnp.zeros((experts, tokens), F32)
    for k in range(top_k):
        mask += jnp.where(routes[k : k + 1, :] == ids, 1.0, 0.0)
    earlier = lax.broadcasted_iota(jnp.int32, (tokens, tokens), 0) < lax.broadcasted_iota(
        jnp.int32, (tokens, tokens), 1
    )
    rank = jnp.dot(
        mask.astype(BF), jnp.where(earlier, 1.0, 0.0).astype(BF), preferred_element_type=F32
    )
    slot = jnp.where(mask > 0.5, rank, -1.0)
    slot_ref[...] = slot
    wide = jnp.concatenate([slot, jnp.zeros((BLOCK - experts, tokens), F32)], axis=0)
    ext[:, model : model + BLOCK] = wide.T.astype(BF)
    copies[1].wait()
    copies[4].start()
    parts = experts // PLANE * width
    lead = sent.shape[2] - parts
    select(slots, slot_ref, ext.at[:, pl.ds(0, lead)], [sent.at[k] for k in range(PLANE)], parts)
    leave(parts, lead, 0)
    me = lax.axis_index("expert")
    steps = (routes >> 2) - (me >> 2)
    steps = jnp.where(steps < 0, steps + experts // PLANE, steps)
    rel = steps * PLANE + ((routes & 3) ^ (me & 3))
    codes = []
    for k in range(top_k):
        own = jnp.sum(
            jnp.where(routes[k : k + 1, :] == ids, slot, 0.0), axis=0, keepdims=True
        ).astype(jnp.int32)
        codes.append(rel[k : k + 1, :] * slots + own)
    code = jnp.concatenate(codes, axis=1)
    rows = lax.broadcasted_iota(jnp.int32, (experts * slots, top_k * tokens), 0)
    pick = jnp.where(rows == code, 1.0, 0.0).astype(BF)
    copies[2].wait()
    copies[3].wait()
    blank = jnp.zeros((spare, top_k * tokens), BF)
    table[0:spare, :] = blank
    table[spare + width :, :] = blank
    for k in range(top_k):
        weight = num_ref[k : k + 1, :].astype(F32) * (1.0 / 1024.0)
        for n, part in enumerate(halves(flip)):
            at = pl.multiple_of(part * half, 16) if flip else part * half
            rows = (hid_ref[k, pl.ds(at, half), :].astype(F32) * weight).astype(BF)
            first = spare + n * half
            table[first : first + half, k * tokens : (k + 1) * tokens] = rows
    size = PLANE * slots
    whole = width + spare
    cut = whole - BLOCK
    for s in range(0, experts // PLANE, 2):
        left = lax.dot_general(
            pick[s * size : (s + 1) * size], table[spare:], NT, preferred_element_type=F32
        )
        right = lax.dot_general(
            pick[(s + 1) * size : (s + 2) * size], table[0:whole], NT, preferred_element_type=F32
        )
        at = s * width
        for k in range(PLANE):
            these = slice(k * slots, (k + 1) * slots)
            sent[k, :, at : at + cut] = left[these, 0:cut].astype(BF)
            sent[k, :, at + cut : at + whole] = (
                left[these, cut:] + right[these, 0:BLOCK]
            ).astype(BF)
            sent[k, :, at + whole : at + pair] = right[these, BLOCK:].astype(BF)
        leave(at, pair, 1 + s // 2)
    for copy in copies[4:]:
        copy.wait()


def relay_kernel(slots, count, begin, *refs):
    blocks, outs, table = refs[:count], refs[-1 - PLANE : -1], refs[-1]
    part = outs[0].shape[1] // count
    model = begin + part
    for n, ext_ref in enumerate(blocks):
        table[...] = ext_ref[:, model : model + BLOCK].astype(F32).T
        select(slots, table, ext_ref.at[:, pl.ds(begin, part)], outs, n * part)


def forward_kernel(*refs):
    del refs


def moved(piece, by):
    return pltpu.roll(piece.astype(F32), by % piece.shape[1], 1) if by else piece.astype(F32)


def regroup_kernel(s, width, *refs):
    out_ref = refs[-1]
    whole = up(width, BLOCK)
    spare = whole - width
    cut = whole - BLOCK
    at = s // 2 * 2 * width + s % 2 * (width - spare)
    lanes = lax.broadcasted_iota(jnp.int32, (out_ref.shape[1], BLOCK), 1)
    for k in range(0, PLANE, 2):
        left = moved(refs[k][:, at : at + whole], -(s % 2) * spare)
        right = moved(refs[k + 1][:, at : at + whole], (1 - s % 2) * spare)
        out_ref[k // 2, :, 0:cut] = left[:, 0:cut].astype(BF)
        out_ref[k // 2, :, cut:whole] = jnp.where(
            lanes < width - cut, left[:, cut:], right[:, 0:BLOCK]
        ).astype(BF)
        out_ref[k // 2, :, whole:] = right[:, BLOCK:].astype(BF)


def fill(table, at, piece, stride):
    wide = piece.astype(F32)
    short = stride - wide.shape[0]
    if short:
        wide = jnp.concatenate([wide, jnp.zeros((short, wide.shape[1]), F32)], axis=0)
    table[at : at + stride, :] = wide.astype(table.dtype)


def halves(flip):
    mine = lax.axis_index("replica") if flip else 1
    return 1 - mine, mine


def stage_kernel(place, spans, stride, flip, *refs):
    arrays, refs = refs[: PLANE * len(spans)], refs[PLANE * len(spans) :]
    w_ref, refs = refs[0], refs[1:]
    hid_ref = refs[0]
    all_rows, all_hidw, gate_ref, rows, hids, hidw, done = refs[-7:]
    group = PLANE * stride
    slots = arrays[0].shape[0]
    width, model = w_ref.shape
    half = width // 2
    whole = hids.shape[1]
    spare = whole - width
    to = 0
    for n, (at, count) in enumerate(spans):
        for k in range(PLANE):
            piece = arrays[n * PLANE + k][:, at : at + count]
            lanes = slice(to, to + count)
            clear = slots // 16 * 16
            rows[k * stride + clear : (k + 1) * stride, lanes] = jnp.zeros(
                (stride - clear, count), BF
            )
            rows[k * stride : k * stride + slots, lanes] = piece
        to += count
    copy = pltpu.make_async_copy(rows, all_rows.at[pl.ds(place * group, group)], done.at[0])
    copy.start()
    for k in range(PLANE):
        at = k % 2 * (width - spare)
        fill(hids, k * stride, moved(hid_ref[k // 2, :, at : at + whole], -(k % 2) * spare), stride)
    flipped = hids[...].T
    hidw[...] = flipped[0:width, :].astype(BF)
    back = lax.dot_general(w_ref[...], rows[...], NT, preferred_element_type=F32)
    turned = halves(flip)[0] == 1
    low, high = flipped[0:half, :], flipped[half:width, :]
    terms = back[0:half, :] * jnp.where(turned, high, low)
    terms += back[half:width, :] * jnp.where(turned, low, high)
    gate = jnp.sum(terms, axis=0, keepdims=True)
    second = pltpu.make_async_copy(
        hidw, all_hidw.at[:, pl.ds(place * group, group)], done.at[1]
    )
    second.start()
    gate_ref[...] = jnp.zeros_like(gate_ref)
    for k in range(PLANE):
        gate_ref[k : k + 1, 0:stride] = gate[:, k * stride : (k + 1) * stride]
    copy.wait()
    second.wait()


def source(outer, s, k):
    me = lax.axis_index("expert")
    return lax.rem((me >> 2) - s + outer, outer) * PLANE + ((me & 3) ^ k)


def early_kernel(step, rows_ref, hidw_ref, out_ref, mark_ref):
    mark_ref[...] = jnp.zeros_like(mark_ref)
    for c in range(0, out_ref.shape[1], step):
        span = slice(c, c + step)
        got = jnp.dot(hidw_ref[...], rows_ref[:, span], preferred_element_type=F32)
        out_ref[:, span] = got.astype(BF)


def partial_kernel(first, step, rows_ref, hidw_ref, early_ref, *refs):
    send_ref, mine_ref = refs[-2:]
    half = mine_ref.shape[0]
    for c in range(0, mine_ref.shape[1], step):
        span, here = slice(first + c, first + c + step), slice(c, c + step)
        got = early_ref[:, span].astype(F32) + jnp.dot(
            hidw_ref[...], rows_ref[:, span], preferred_element_type=F32
        )
        send_ref[:, here] = got[0:half].astype(BF)
        mine_ref[:, here] = got[half:].astype(BF)


def combine_kernel(outer, *refs):
    gates, outs = refs[:outer], refs[-PLANE:]
    for k, out_ref in enumerate(outs):
        for s, gate_ref in enumerate(gates):
            out_ref[s : s + 1, :] = gate_ref[k : k + 1, :]


def pick_gates(slot_ref, routes_ref, num_ref, homes, gate_ref, rows):
    experts, tokens = slot_ref.shape
    for k in range(PLANE):
        for s in range(experts // PLANE):
            rows[pl.ds(source(experts // PLANE, -s, k), 1), :] = homes[k][s : s + 1, :]
    slot = jnp.maximum(slot_ref[...], 0.0).astype(jnp.int32)
    value = jnp.take_along_axis(rows[...], slot, axis=1)
    ids = lax.broadcasted_iota(jnp.int32, (experts, tokens), 0)
    for k in range(gate_ref.shape[0]):
        got = jnp.sum(
            jnp.where(routes_ref[k : k + 1, :] == ids, value, 0.0), axis=0, keepdims=True
        )
        gate_ref[k : k + 1, :] = got / (num_ref[k : k + 1, :].astype(F32) * (1.0 / 1024.0))


def finish_kernel(first, step, count, extra, *refs):
    own, others_ref, refs = refs[:count], refs[count], refs[count + 1 :]
    if extra:
        slot_ref, routes_ref, num_ref, *homes = refs[: 3 + PLANE]
        out_hbm, scale_hbm, gate_ref, out, scales, table, done, rows = refs[5 + PLANE :]
    else:
        out_hbm, scale_hbm, out, scales, table, done = refs
    share, width = out.shape
    lanes = lax.broadcasted_iota(jnp.int32, (share, BLOCK), 1)
    copies = []
    kept = jnp.zeros((share, BLOCK), F32)
    for c in range(0, width, step):
        for at in range(c, c + step, BLOCK):
            span = slice(at, at + BLOCK)
            terms = [others_ref[n, :, span].astype(F32) for n in range(others_ref.shape[0])]
            terms += [ref[:, span].astype(F32) for ref in own]
            top = functools.reduce(jnp.maximum, [jnp.abs(term) for term in terms])
            scale = jnp.max(top, axis=1, keepdims=True) + 1e-6
            out[:, span] = functools.reduce(jnp.add, terms) * (1.0 / scale)
            kept = jnp.where(lanes == at // BLOCK, scale, kept)
        copy = pltpu.make_async_copy(
            out.at[:, pl.ds(c, step)], out_hbm.at[:, pl.ds(first + c, step)], done.at[len(copies)]
        )
        copy.start()
        copies.append(copy)
    table[...] = jnp.zeros_like(table)
    table[0:share, :] = kept
    scales[...] = table[...].T[0 : scales.shape[0], 0:share]
    copy = pltpu.make_async_copy(
        scales, scale_hbm.at[pl.ds(first // BLOCK, scales.shape[0])], done.at[len(copies)]
    )
    copy.start()
    copies.append(copy)
    if extra:
        pick_gates(slot_ref, routes_ref, num_ref, homes, gate_ref, rows)
    for copy in copies:
        copy.wait()


def per_device(cotangent, hidden, routes, numerators, w_down):
    tokens, model = cotangent.shape
    top_k, width = hidden.shape[1], hidden.shape[2]
    experts, replicas = lax.axis_size("expert"), lax.axis_size("replica")
    outer = experts // PLANE
    slots = up(3 * tokens * top_k // (2 * experts), 8)
    stride = up(slots, 32)
    half = width // 2
    share = width // replicas
    group = PLANE * stride
    flip = replicas == 2
    sds = jax.ShapeDtypeStruct
    step, fine = 512, 256

    def ring(array, by):
        pairs = [(e, (e + by * PLANE) % experts) for e in range(experts)]
        return lax.ppermute(array, "expert", pairs)

    def swap(array, k):
        return lax.ppermute(array, "expert", [(e, e ^ k) for e in range(experts)])

    anywhere = pl.BlockSpec(memory_space=pl.ANY)
    inside = pl.BlockSpec(memory_space=pltpu.VMEM)

    lead = model // 2
    wide = outer * width + lead
    ext, *packed, slot = call(
        functools.partial(open_kernel, slots, flip),
        [sds((tokens, model + BLOCK), BF)]
        + [sds((slots, wide), BF)] * PLANE
        + [sds((experts, tokens), F32)],
        ALL_VMEM,
        in_specs=[anywhere] * 4,
        out_specs=[anywhere] * (1 + PLANE) + [inside],
        scratch_shapes=[
            pltpu.VMEM((tokens, model + BLOCK), BF),
            pltpu.VMEM((PLANE, slots, wide), BF),
            pltpu.VMEM((2 * up(width, BLOCK) - width, top_k * tokens), BF),
            pltpu.VMEM((top_k, tokens), jnp.int32),
            pltpu.VMEM((top_k, tokens), jnp.int32),
            pltpu.VMEM((top_k, width, tokens), BF),
            pltpu.SemaphoreType.DMA((5 + PLANE * (1 + outer // 2),)),
        ],
    )(routes.T, numerators.T, jnp.transpose(hidden, (1, 2, 0)), cotangent)
    opening = [packed[0]] + [swap(packed[k], k) for k in range(1, PLANE)]

    blocks = {0: ext}
    order = [0]
    for s in range(1, outer // 2 + 1):
        blocks[s] = ring(blocks[s - 1], 1)
        order.append(s)
        if outer - s != s:
            blocks[outer - s] = ring(blocks[(outer - s + 1) % outer], -1)
            order.append(outer - s)
    def regroup(s, after):
        return call(
            functools.partial(regroup_kernel, s, width),
            sds((PLANE // 2, slots, 2 * width), BF),
            in_specs=[inside] * PLANE + [anywhere] * len(after),
        )(*opening, *after)

    hids = {0: regroup(0, [])}
    for n, s in enumerate(order[1:]):
        hids[s] = ring(regroup(s, [blocks[order[-1]]] if n else []), s)

    def gated(arrays, after):
        return call(
            forward_kernel,
            [sds(array.shape, array.dtype) for array in arrays],
            in_specs=[anywhere] * (len(arrays) + len(after)),
            out_specs=[anywhere] * len(arrays),
            input_output_aliases={n: n for n in range(len(arrays))},
        )(*arrays, *after)

    def relay(batch, after, begin=0):
        sent = call(
            functools.partial(relay_kernel, slots, len(batch), begin),
            [sds((slots, len(batch) * (model - begin)), BF)] * PLANE,
            scratch_shapes=[pltpu.VMEM((BLOCK, tokens), F32)],
        )(*[blocks[s] for s in batch])
        moved = gated(sent[1:], after)
        return [sent[0]] + [swap(moved[k - 1], k) for k in range(1, PLANE)]

    middle = relay(order[1:-1], opening[1:])
    late = relay(order[-1:], [hids[order[1]]])
    final = relay([0], [*middle[1:], hids[order[-2]]], lead)

    def stage(parts, hid, place, count, after, rows):
        arrays = [array for got, _ in parts for array in got]
        fixed = len(arrays) + 2
        return call(
            functools.partial(stage_kernel, place, [span for _, span in parts], stride, flip),
            [
                sds((count * group, model), BF),
                sds((width, count * group), BF),
                sds((PLANE, BLOCK), F32),
            ],
            flops=2_000_000_000,
            in_specs=[inside] * fixed + [anywhere] * len(rows) + [inside] * len(after),
            out_specs=[anywhere, anywhere, inside],
            input_output_aliases={fixed + i: i for i in range(len(rows))},
            scratch_shapes=[
                pltpu.VMEM((group, model), BF),
                pltpu.VMEM((group, up(width, BLOCK)), F32),
                pltpu.VMEM((width, group), BF),
                pltpu.SemaphoreType.DMA((2,)),
            ],
        )(*arrays, w_down[0], hid, *rows, *after)

    sources = {s: [(middle, (n * model, model))] for n, s in enumerate(order[1:-1])}
    sources[order[-1]] = [(late, (0, model))]
    sources[0] = [(opening, (wide - lead, lead)), (final, (0, model - lead))]
    rows, gates = [], {}
    for n, s in enumerate(order[1:-1]):
        *rows, gates[s] = stage(sources[s], hids[s], n, outer - 2, [], rows)
    early, mark = call(
        functools.partial(early_kernel, step),
        [sds((width, model), BF), sds((8, BLOCK), F32)],
        flops=3_500_000_000,
    )(*rows)
    *rows, gates[order[-1]] = stage(
        sources[order[-1]], hids[order[-1]], 0, 2, [mark], []
    )
    for s, gate in zip(
        order[1:-1], gated([gates[s] for s in order[1:-1]], [gates[order[-1]]])
    ):
        gates[s] = gate
    *rows, gates[0] = stage(sources[0], hids[0], 1, 2, [], rows)
    gates = [ring(gates[s], -s) if s else gates[s] for s in range(outer)]

    def partial(first, after):
        return call(
            functools.partial(partial_kernel, first, step),
            [sds((half, model // 2), BF)] * 2,
            in_specs=[inside] * 3 + [anywhere] * len(after),
        )(*rows, early, *after)

    def finish(first, send, mine, out, extra):
        if flip:
            others = lax.ppermute(send, "replica", [(0, 1), (1, 0)])[None]
            own = [mine]
        else:
            both = jnp.concatenate([send, mine], axis=0).reshape(replicas, share, model // 2)
            others = lax.all_to_all(both, "replica", 0, 0, tiled=True)
            own = []
        fixed = len(own) + 1 + len(extra)
        outs = [sds((share, model), F32), sds((model // BLOCK, share), F32)]
        out_specs = [anywhere] * 2
        scratch = [
            pltpu.VMEM((share, model // 2), F32),
            pltpu.VMEM((model // 2 // BLOCK, share), F32),
            pltpu.VMEM((up(share, BLOCK), BLOCK), F32),
            pltpu.SemaphoreType.DMA((model // 2 // fine + 1,)),
        ]
        if extra:
            outs.append(sds((top_k, tokens), F32))
            out_specs.append(inside)
            scratch.append(pltpu.VMEM((experts, BLOCK), F32))
        return call(
            functools.partial(finish_kernel, first, fine, len(own), bool(extra)),
            outs,
            in_specs=[inside] * fixed + [anywhere] * len(out),
            out_specs=out_specs,
            input_output_aliases={fixed + n: n for n in range(len(out))},
            scratch_shapes=scratch,
        )(*own, others, *extra, *out)

    left = partial(0, [])
    right = partial(model // 2, gates[1:])
    homes = call(
        functools.partial(combine_kernel, outer),
        [sds((outer, BLOCK), F32)] * PLANE,
        in_specs=[inside] * outer + [anywhere],
    )(*gates, left[0])
    homes = [homes[0]] + [swap(homes[k], k) for k in range(1, PLANE)]
    out = finish(0, *left, [], [])
    out, scales, gate_grad = finish(model // 2, *right, out, [slot, routes.T, numerators.T, *homes])
    return gate_grad.T, scales.T[None], out[None]


def solution(mesh):
    return jax.shard_map(
        per_device,
        mesh=mesh,
        in_specs=(
            P(("expert", "replica"), None),
            P(("expert", "replica"), None, None),
            P(("expert", "replica"), None),
            P(("expert", "replica"), None),
            P("expert", None, None),
        ),
        out_specs=(
            P(("expert", "replica"), None),
            P("expert", "replica", None),
            P("expert", "replica", None),
        ),
        check_vma=False,
    )
```

```python
import functools

import jax
import jax.numpy as jnp
from jax import lax
from jax.experimental import pallas as pl
from jax.experimental.pallas import tpu as pltpu
from jax.sharding import PartitionSpec as P

BLOCK = 128
PLANE = 4
BF = jnp.bfloat16
F32 = jnp.float32
NT = (((1,), (1,)), ((), ()))
VMEM_BYTES = 24 * 1024 * 1024
ALL_VMEM = 56 * 1024 * 1024


def up(value, unit):
    return -(-value // unit) * unit


def call(kernel, out_shape, room=VMEM_BYTES, flops=1024, **kw):
    return pl.pallas_call(
        kernel,
        out_shape=out_shape,
        cost_estimate=pl.CostEstimate(
            flops=flops, bytes_accessed=1024, transcendentals=0
        ),
        compiler_params=pltpu.CompilerParams(vmem_limit_bytes=room),
        **kw,
    )


def select(slots, table, cot_ref, outs, at=0):
    me = lax.axis_index("expert")
    tokens = cot_ref.shape[0]
    rows = lax.broadcasted_iota(jnp.int32, (slots, tokens), 0).astype(F32)
    pick = jnp.concatenate(
        [jnp.where(table[pl.ds(me ^ k, 1), :] == rows, 1.0, 0.0) for k in range(PLANE)], axis=0
    ).astype(BF)
    model = cot_ref.shape[1]
    step = min(512, model)
    for c in range(0, model, step):
        got = jnp.dot(pick, cot_ref[:, c : c + step], preferred_element_type=F32)
        for k in range(PLANE):
            outs[k][:, at + c : at + c + step] = got[k * slots : (k + 1) * slots, :].astype(BF)


def open_kernel(slots, flip, *refs):
    routes_hbm, num_hbm, hid_hbm, cot_hbm, ext_hbm, *refs = refs
    sent, (slot_ref, *refs) = refs[:PLANE], refs[PLANE:]
    ext, table, routes_ref, num_ref, hid_ref, done = refs
    experts, tokens = slot_ref.shape
    top_k, width = hid_ref.shape[:2]
    model = cot_hbm.shape[1]
    half = width // 2
    spare = up(width, BLOCK) - width
    pair = 2 * width
    pairs = (
        (routes_hbm, routes_ref),
        (cot_hbm, ext.at[:, pl.ds(0, model)]),
        (num_hbm, num_ref),
        (hid_hbm, hid_ref),
        (ext, ext_hbm),
    )
    copies = [pltpu.make_async_copy(*pair, done.at[n]) for n, pair in enumerate(pairs)]
    for copy in copies[:4]:
        copy.start()

    copies[0].wait()
    routes = routes_ref[...]
    ids = lax.broadcasted_iota(jnp.int32, (experts, tokens), 0)
    mask = jnp.zeros((experts, tokens), F32)
    for k in range(top_k):
        mask += jnp.where(routes[k : k + 1, :] == ids, 1.0, 0.0)
    earlier = lax.broadcasted_iota(jnp.int32, (tokens, tokens), 0) < lax.broadcasted_iota(
        jnp.int32, (tokens, tokens), 1
    )
    rank = jnp.dot(
        mask.astype(BF), jnp.where(earlier, 1.0, 0.0).astype(BF), preferred_element_type=F32
    )
    slot = jnp.where(mask > 0.5, rank, -1.0)
    slot_ref[...] = slot
    wide = jnp.concatenate([slot, jnp.zeros((BLOCK - experts, tokens), F32)], axis=0)
    ext[:, model : model + BLOCK] = wide.T.astype(BF)
    copies[1].wait()
    copies[4].start()
    parts = experts // PLANE * width
    lead = sent[0].shape[1] - parts
    select(slots, slot_ref, ext.at[:, pl.ds(0, lead)], sent, parts)
    me = lax.axis_index("expert")
    steps = (routes >> 2) - (me >> 2)
    steps = jnp.where(steps < 0, steps + experts // PLANE, steps)
    rel = steps * PLANE + ((routes & 3) ^ (me & 3))
    codes = []
    for k in range(top_k):
        own = jnp.sum(
            jnp.where(routes[k : k + 1, :] == ids, slot, 0.0), axis=0, keepdims=True
        ).astype(jnp.int32)
        codes.append(rel[k : k + 1, :] * slots + own)
    code = jnp.concatenate(codes, axis=1)
    rows = lax.broadcasted_iota(jnp.int32, (experts * slots, top_k * tokens), 0)
    pick = jnp.where(rows == code, 1.0, 0.0).astype(BF)
    copies[2].wait()
    copies[3].wait()
    blank = jnp.zeros((spare, top_k * tokens), BF)
    table[0:spare, :] = blank
    table[spare + width :, :] = blank
    for k in range(top_k):
        weight = num_ref[k : k + 1, :].astype(F32) * (1.0 / 1024.0)
        for n, part in enumerate(halves(flip)):
            at = pl.multiple_of(part * half, 16) if flip else part * half
            rows = (hid_ref[k, pl.ds(at, half), :].astype(F32) * weight).astype(BF)
            first = spare + n * half
            table[first : first + half, k * tokens : (k + 1) * tokens] = rows
    size = PLANE * slots
    whole = width + spare
    cut = whole - BLOCK
    for s in range(0, experts // PLANE, 2):
        left = lax.dot_general(
            pick[s * size : (s + 1) * size], table[spare:], NT, preferred_element_type=F32
        )
        right = lax.dot_general(
            pick[(s + 1) * size : (s + 2) * size], table[0:whole], NT, preferred_element_type=F32
        )
        at = s * width
        for k in range(PLANE):
            these = slice(k * slots, (k + 1) * slots)
            sent[k][:, at : at + cut] = left[these, 0:cut].astype(BF)
            sent[k][:, at + cut : at + whole] = (
                left[these, cut:] + right[these, 0:BLOCK]
            ).astype(BF)
            sent[k][:, at + whole : at + pair] = right[these, BLOCK:].astype(BF)
    for copy in copies[4:]:
        copy.wait()


def relay_kernel(slots, count, begin, *refs):
    blocks, outs, table = refs[:count], refs[-1 - PLANE : -1], refs[-1]
    part = outs[0].shape[1] // count
    model = begin + part
    for n, ext_ref in enumerate(blocks):
        table[...] = ext_ref[:, model : model + BLOCK].astype(F32).T
        select(slots, table, ext_ref.at[:, pl.ds(begin, part)], outs, n * part)


def forward_kernel(*refs):
    del refs


def moved(piece, by):
    return pltpu.roll(piece.astype(F32), by % piece.shape[1], 1) if by else piece.astype(F32)


def regroup_kernel(s, width, *refs):
    out_ref = refs[-1]
    whole = up(width, BLOCK)
    spare = whole - width
    cut = whole - BLOCK
    at = s // 2 * 2 * width + s % 2 * (width - spare)
    lanes = lax.broadcasted_iota(jnp.int32, (out_ref.shape[1], BLOCK), 1)
    for k in range(0, PLANE, 2):
        left = moved(refs[k][:, at : at + whole], -(s % 2) * spare)
        right = moved(refs[k + 1][:, at : at + whole], (1 - s % 2) * spare)
        out_ref[k // 2, :, 0:cut] = left[:, 0:cut].astype(BF)
        out_ref[k // 2, :, cut:whole] = jnp.where(
            lanes < width - cut, left[:, cut:], right[:, 0:BLOCK]
        ).astype(BF)
        out_ref[k // 2, :, whole:] = right[:, BLOCK:].astype(BF)


def fill(table, at, piece, stride):
    wide = piece.astype(F32)
    short = stride - wide.shape[0]
    if short:
        wide = jnp.concatenate([wide, jnp.zeros((short, wide.shape[1]), F32)], axis=0)
    table[at : at + stride, :] = wide.astype(table.dtype)


def halves(flip):
    mine = lax.axis_index("replica") if flip else 1
    return 1 - mine, mine


def stage_kernel(place, spans, stride, flip, *refs):
    arrays, refs = refs[: PLANE * len(spans)], refs[PLANE * len(spans) :]
    w_ref, refs = refs[0], refs[1:]
    hid_ref = refs[0]
    all_rows, all_hidw, gate_ref, rows, hids, hidw, done = refs[-7:]
    group = PLANE * stride
    width, model = w_ref.shape
    half = width // 2
    whole = hids.shape[1]
    spare = whole - width
    to = 0
    for n, (at, count) in enumerate(spans):
        for k in range(PLANE):
            piece = arrays[n * PLANE + k][:, at : at + count]
            fill(rows.at[:, pl.ds(to, count)], k * stride, piece, stride)
        to += count
    copy = pltpu.make_async_copy(rows, all_rows.at[pl.ds(place * group, group)], done.at[0])
    copy.start()
    for k in range(PLANE):
        at = k % 2 * (width - spare)
        fill(hids, k * stride, moved(hid_ref[k // 2, :, at : at + whole], -(k % 2) * spare), stride)
    flipped = hids[...].T
    hidw[...] = flipped[0:width, :].astype(BF)
    back = lax.dot_general(w_ref[...], rows[...], NT, preferred_element_type=F32)
    turned = halves(flip)[0] == 1
    low, high = flipped[0:half, :], flipped[half:width, :]
    terms = back[0:half, :] * jnp.where(turned, high, low)
    terms += back[half:width, :] * jnp.where(turned, low, high)
    gate = jnp.sum(terms, axis=0, keepdims=True)
    second = pltpu.make_async_copy(
        hidw, all_hidw.at[:, pl.ds(place * group, group)], done.at[1]
    )
    second.start()
    gate_ref[...] = jnp.zeros_like(gate_ref)
    for k in range(PLANE):
        gate_ref[k : k + 1, 0:stride] = gate[:, k * stride : (k + 1) * stride]
    copy.wait()
    second.wait()


def source(outer, s, k):
    me = lax.axis_index("expert")
    return lax.rem((me >> 2) - s + outer, outer) * PLANE + ((me & 3) ^ k)


def early_kernel(step, rows_ref, hidw_ref, out_ref, mark_ref):
    mark_ref[...] = jnp.zeros_like(mark_ref)
    for c in range(0, out_ref.shape[1], step):
        span = slice(c, c + step)
        got = jnp.dot(hidw_ref[...], rows_ref[:, span], preferred_element_type=F32)
        out_ref[:, span] = got.astype(BF)


def partial_kernel(first, step, rows_ref, hidw_ref, early_ref, *refs):
    send_ref, mine_ref = refs[-2:]
    half = mine_ref.shape[0]
    for c in range(0, mine_ref.shape[1], step):
        span, here = slice(first + c, first + c + step), slice(c, c + step)
        got = early_ref[:, span].astype(F32) + jnp.dot(
            hidw_ref[...], rows_ref[:, span], preferred_element_type=F32
        )
        send_ref[:, here] = got[0:half].astype(BF)
        mine_ref[:, here] = got[half:].astype(BF)


def combine_kernel(outer, *refs):
    gates, outs = refs[:outer], refs[-PLANE:]
    for k, out_ref in enumerate(outs):
        for s, gate_ref in enumerate(gates):
            out_ref[s : s + 1, :] = gate_ref[k : k + 1, :]


def pick_gates(slot_ref, routes_ref, num_ref, homes, gate_ref, rows):
    experts, tokens = slot_ref.shape
    for k in range(PLANE):
        for s in range(experts // PLANE):
            rows[pl.ds(source(experts // PLANE, -s, k), 1), :] = homes[k][s : s + 1, :]
    slot = jnp.maximum(slot_ref[...], 0.0).astype(jnp.int32)
    value = jnp.take_along_axis(rows[...], slot, axis=1)
    ids = lax.broadcasted_iota(jnp.int32, (experts, tokens), 0)
    for k in range(gate_ref.shape[0]):
        got = jnp.sum(
            jnp.where(routes_ref[k : k + 1, :] == ids, value, 0.0), axis=0, keepdims=True
        )
        gate_ref[k : k + 1, :] = got / (num_ref[k : k + 1, :].astype(F32) * (1.0 / 1024.0))


def finish_kernel(first, step, count, extra, *refs):
    own, others_ref, refs = refs[:count], refs[count], refs[count + 1 :]
    if extra:
        slot_ref, routes_ref, num_ref, *homes = refs[: 3 + PLANE]
        out_hbm, scale_hbm, gate_ref, out, scales, table, done, rows = refs[5 + PLANE :]
    else:
        out_hbm, scale_hbm, out, scales, table, done = refs
    share, width = out.shape
    lanes = lax.broadcasted_iota(jnp.int32, (share, BLOCK), 1)
    copies = []
    kept = jnp.zeros((share, BLOCK), F32)
    for c in range(0, width, step):
        for at in range(c, c + step, BLOCK):
            span = slice(at, at + BLOCK)
            terms = [others_ref[n, :, span].astype(F32) for n in range(others_ref.shape[0])]
            terms += [ref[:, span].astype(F32) for ref in own]
            top = functools.reduce(jnp.maximum, [jnp.abs(term) for term in terms])
            scale = jnp.max(top, axis=1, keepdims=True) + 1e-6
            out[:, span] = functools.reduce(jnp.add, terms) * (1.0 / scale)
            kept = jnp.where(lanes == at // BLOCK, scale, kept)
        copy = pltpu.make_async_copy(
            out.at[:, pl.ds(c, step)], out_hbm.at[:, pl.ds(first + c, step)], done.at[len(copies)]
        )
        copy.start()
        copies.append(copy)
    table[...] = jnp.zeros_like(table)
    table[0:share, :] = kept
    scales[...] = table[...].T[0 : scales.shape[0], 0:share]
    copy = pltpu.make_async_copy(
        scales, scale_hbm.at[pl.ds(first // BLOCK, scales.shape[0])], done.at[len(copies)]
    )
    copy.start()
    copies.append(copy)
    if extra:
        pick_gates(slot_ref, routes_ref, num_ref, homes, gate_ref, rows)
    for copy in copies:
        copy.wait()


def per_device(cotangent, hidden, routes, numerators, w_down):
    tokens, model = cotangent.shape
    top_k, width = hidden.shape[1], hidden.shape[2]
    experts, replicas = lax.axis_size("expert"), lax.axis_size("replica")
    outer = experts // PLANE
    slots = up(3 * tokens * top_k // (2 * experts), 8)
    stride = up(slots, 32)
    half = width // 2
    share = width // replicas
    group = PLANE * stride
    flip = replicas == 2
    sds = jax.ShapeDtypeStruct
    step, fine = 512, 256

    def ring(array, by):
        pairs = [(e, (e + by * PLANE) % experts) for e in range(experts)]
        return lax.ppermute(array, "expert", pairs)

    def swap(array, k):
        return lax.ppermute(array, "expert", [(e, e ^ k) for e in range(experts)])

    anywhere = pl.BlockSpec(memory_space=pl.ANY)
    inside = pl.BlockSpec(memory_space=pltpu.VMEM)

    lead = model // 2
    wide = outer * width + lead
    ext, *packed, slot = call(
        functools.partial(open_kernel, slots, flip),
        [sds((tokens, model + BLOCK), BF)]
        + [sds((slots, wide), BF)] * PLANE
        + [sds((experts, tokens), F32)],
        ALL_VMEM,
        in_specs=[anywhere] * 4,
        out_specs=[anywhere] + [inside] * (1 + PLANE),
        scratch_shapes=[
            pltpu.VMEM((tokens, model + BLOCK), BF),
            pltpu.VMEM((2 * up(width, BLOCK) - width, top_k * tokens), BF),
            pltpu.VMEM((top_k, tokens), jnp.int32),
            pltpu.VMEM((top_k, tokens), jnp.int32),
            pltpu.VMEM((top_k, width, tokens), BF),
            pltpu.SemaphoreType.DMA((5,)),
        ],
    )(routes.T, numerators.T, jnp.transpose(hidden, (1, 2, 0)), cotangent)
    opening = [packed[0]] + [swap(packed[k], k) for k in range(1, PLANE)]

    blocks = {0: ext}
    order = [0]
    for s in range(1, outer // 2 + 1):
        blocks[s] = ring(blocks[s - 1], 1)
        order.append(s)
        if outer - s != s:
            blocks[outer - s] = ring(blocks[(outer - s + 1) % outer], -1)
            order.append(outer - s)
    def regroup(s, after):
        return call(
            functools.partial(regroup_kernel, s, width),
            sds((PLANE // 2, slots, 2 * width), BF),
            in_specs=[inside] * PLANE + [anywhere] * len(after),
        )(*opening, *after)

    hids = {0: regroup(0, [])}
    for n, s in enumerate(order[1:]):
        hids[s] = ring(regroup(s, [blocks[order[-1]]] if n else []), s)

    def gated(arrays, after):
        return call(
            forward_kernel,
            [sds(array.shape, array.dtype) for array in arrays],
            in_specs=[anywhere] * (len(arrays) + len(after)),
            out_specs=[anywhere] * len(arrays),
            input_output_aliases={n: n for n in range(len(arrays))},
        )(*arrays, *after)

    def relay(batch, after, begin=0):
        sent = call(
            functools.partial(relay_kernel, slots, len(batch), begin),
            [sds((slots, len(batch) * (model - begin)), BF)] * PLANE,
            scratch_shapes=[pltpu.VMEM((BLOCK, tokens), F32)],
        )(*[blocks[s] for s in batch])
        moved = gated(sent[1:], after)
        return [sent[0]] + [swap(moved[k - 1], k) for k in range(1, PLANE)]

    middle = relay(order[1:-1], opening[1:])
    late = relay(order[-1:], [hids[order[1]]])
    final = relay([0], [*middle[1:], hids[order[-2]]], lead)

    def stage(parts, hid, place, count, after, rows):
        arrays = [array for got, _ in parts for array in got]
        fixed = len(arrays) + 2
        return call(
            functools.partial(stage_kernel, place, [span for _, span in parts], stride, flip),
            [
                sds((count * group, model), BF),
                sds((width, count * group), BF),
                sds((PLANE, BLOCK), F32),
            ],
            flops=2_000_000_000,
            in_specs=[inside] * fixed + [anywhere] * len(rows) + [inside] * len(after),
            out_specs=[anywhere, anywhere, inside],
            input_output_aliases={fixed + i: i for i in range(len(rows))},
            scratch_shapes=[
                pltpu.VMEM((group, model), BF),
                pltpu.VMEM((group, up(width, BLOCK)), F32),
                pltpu.VMEM((width, group), BF),
                pltpu.SemaphoreType.DMA((2,)),
            ],
        )(*arrays, w_down[0], hid, *rows, *after)

    sources = {s: [(middle, (n * model, model))] for n, s in enumerate(order[1:-1])}
    sources[order[-1]] = [(late, (0, model))]
    sources[0] = [(opening, (wide - lead, lead)), (final, (0, model - lead))]
    rows, gates = [], {}
    for n, s in enumerate(order[1:-1]):
        *rows, gates[s] = stage(sources[s], hids[s], n, outer - 2, [], rows)
    early, mark = call(
        functools.partial(early_kernel, step),
        [sds((width, model), BF), sds((8, BLOCK), F32)],
        flops=3_500_000_000,
    )(*rows)
    *rows, gates[order[-1]] = stage(
        sources[order[-1]], hids[order[-1]], 0, 2, [mark], []
    )
    for s, gate in zip(
        order[1:-1], gated([gates[s] for s in order[1:-1]], [gates[order[-1]]])
    ):
        gates[s] = gate
    *rows, gates[0] = stage(sources[0], hids[0], 1, 2, [], rows)
    gates = [ring(gates[s], -s) if s else gates[s] for s in range(outer)]

    def partial(first, after):
        return call(
            functools.partial(partial_kernel, first, step),
            [sds((half, model // 2), BF)] * 2,
            in_specs=[inside] * 3 + [anywhere] * len(after),
        )(*rows, early, *after)

    def finish(first, send, mine, out, extra):
        if flip:
            others = lax.ppermute(send, "replica", [(0, 1), (1, 0)])[None]
            own = [mine]
        else:
            both = jnp.concatenate([send, mine], axis=0).reshape(replicas, share, model // 2)
            others = lax.all_to_all(both, "replica", 0, 0, tiled=True)
            own = []
        fixed = len(own) + 1 + len(extra)
        outs = [sds((share, model), F32), sds((model // BLOCK, share), F32)]
        out_specs = [anywhere] * 2
        scratch = [
            pltpu.VMEM((share, model // 2), F32),
            pltpu.VMEM((model // 2 // BLOCK, share), F32),
            pltpu.VMEM((up(share, BLOCK), BLOCK), F32),
            pltpu.SemaphoreType.DMA((model // 2 // fine + 1,)),
        ]
        if extra:
            outs.append(sds((top_k, tokens), F32))
            out_specs.append(inside)
            scratch.append(pltpu.VMEM((experts, BLOCK), F32))
        return call(
            functools.partial(finish_kernel, first, fine, len(own), bool(extra)),
            outs,
            in_specs=[inside] * fixed + [anywhere] * len(out),
            out_specs=out_specs,
            input_output_aliases={fixed + n: n for n in range(len(out))},
            scratch_shapes=scratch,
        )(*own, others, *extra, *out)

    left = partial(0, [])
    right = partial(model // 2, gates[1:])
    homes = call(
        functools.partial(combine_kernel, outer),
        [sds((outer, BLOCK), F32)] * PLANE,
        in_specs=[inside] * outer + [anywhere],
    )(*gates, left[0])
    homes = [homes[0]] + [swap(homes[k], k) for k in range(1, PLANE)]
    out = finish(0, *left, [], [])
    out, scales, gate_grad = finish(model // 2, *right, out, [slot, routes.T, numerators.T, *homes])
    return gate_grad.T, scales.T[None], out[None]


def solution(mesh):
    return jax.shard_map(
        per_device,
        mesh=mesh,
        in_specs=(
            P(("expert", "replica"), None),
            P(("expert", "replica"), None, None),
            P(("expert", "replica"), None),
            P(("expert", "replica"), None),
            P("expert", None, None),
        ),
        out_specs=(
            P(("expert", "replica"), None),
            P("expert", "replica", None),
            P("expert", "replica", None),
        ),
        check_vma=False,
    )
```

```python
import functools

import jax
import jax.numpy as jnp
from jax import lax
from jax.experimental import pallas as pl
from jax.experimental.pallas import tpu as pltpu
from jax.sharding import PartitionSpec as P

BLOCK = 128
PLANE = 4
BF = jnp.bfloat16
F32 = jnp.float32
NT = (((1,), (1,)), ((), ()))
VMEM_BYTES = 24 * 1024 * 1024
ALL_VMEM = 56 * 1024 * 1024


def up(value, unit):
    return -(-value // unit) * unit


def call(kernel, out_shape, room=VMEM_BYTES, flops=1024, **kw):
    return pl.pallas_call(
        kernel,
        out_shape=out_shape,
        cost_estimate=pl.CostEstimate(
            flops=flops, bytes_accessed=1024, transcendentals=0
        ),
        compiler_params=pltpu.CompilerParams(vmem_limit_bytes=room),
        **kw,
    )


def select(slots, table, cot_ref, outs, at=0):
    me = lax.axis_index("expert")
    tokens = cot_ref.shape[0]
    rows = lax.broadcasted_iota(jnp.int32, (slots, tokens), 0).astype(F32)
    pick = jnp.concatenate(
        [jnp.where(table[pl.ds(me ^ k, 1), :] == rows, 1.0, 0.0) for k in range(PLANE)], axis=0
    ).astype(BF)
    model = cot_ref.shape[1]
    step = min(512, model)
    for c in range(0, model, step):
        got = jnp.dot(pick, cot_ref[:, c : c + step], preferred_element_type=F32)
        for k in range(PLANE):
            outs[k][:, at + c : at + c + step] = got[k * slots : (k + 1) * slots, :].astype(BF)


def open_kernel(slots, flip, *refs):
    routes_hbm, num_hbm, hid_hbm, cot_hbm, ext_hbm, *refs = refs
    sent, (slot_ref, *refs) = refs[:PLANE], refs[PLANE:]
    ext, table, routes_ref, num_ref, hid_ref, done = refs
    experts, tokens = slot_ref.shape
    top_k, width = hid_ref.shape[:2]
    model = cot_hbm.shape[1]
    half = width // 2
    spare = up(width, BLOCK) - width
    pair = 2 * width
    pairs = (
        (routes_hbm, routes_ref),
        (cot_hbm, ext.at[:, pl.ds(0, model)]),
        (num_hbm, num_ref),
        (hid_hbm, hid_ref),
        (ext, ext_hbm),
    )
    copies = [pltpu.make_async_copy(*pair, done.at[n]) for n, pair in enumerate(pairs)]
    for copy in copies[:4]:
        copy.start()

    copies[0].wait()
    routes = routes_ref[...]
    ids = lax.broadcasted_iota(jnp.int32, (experts, tokens), 0)
    mask = jnp.zeros((experts, tokens), F32)
    for k in range(top_k):
        mask += jnp.where(routes[k : k + 1, :] == ids, 1.0, 0.0)
    earlier = lax.broadcasted_iota(jnp.int32, (tokens, tokens), 0) < lax.broadcasted_iota(
        jnp.int32, (tokens, tokens), 1
    )
    rank = jnp.dot(
        mask.astype(BF), jnp.where(earlier, 1.0, 0.0).astype(BF), preferred_element_type=F32
    )
    slot = jnp.where(mask > 0.5, rank, -1.0)
    slot_ref[...] = slot
    wide = jnp.concatenate([slot, jnp.zeros((BLOCK - experts, tokens), F32)], axis=0)
    ext[:, model : model + BLOCK] = wide.T.astype(BF)
    copies[1].wait()
    copies[4].start()
    parts = experts // PLANE * width
    lead = sent[0].shape[1] - parts
    select(slots, slot_ref, ext.at[:, pl.ds(0, lead)], sent, parts)
    me = lax.axis_index("expert")
    steps = (routes >> 2) - (me >> 2)
    steps = jnp.where(steps < 0, steps + experts // PLANE, steps)
    rel = steps * PLANE + ((routes & 3) ^ (me & 3))
    codes = []
    for k in range(top_k):
        own = jnp.sum(
            jnp.where(routes[k : k + 1, :] == ids, slot, 0.0), axis=0, keepdims=True
        ).astype(jnp.int32)
        codes.append(rel[k : k + 1, :] * slots + own)
    code = jnp.concatenate(codes, axis=1)
    rows = lax.broadcasted_iota(jnp.int32, (experts * slots, top_k * tokens), 0)
    pick = jnp.where(rows == code, 1.0, 0.0).astype(BF)
    copies[2].wait()
    copies[3].wait()
    blank = jnp.zeros((spare, top_k * tokens), BF)
    table[0:spare, :] = blank
    table[spare + width :, :] = blank
    for k in range(top_k):
        weight = num_ref[k : k + 1, :].astype(F32) * (1.0 / 1024.0)
        for n, part in enumerate(halves(flip)):
            at = pl.multiple_of(part * half, 16) if flip else part * half
            rows = (hid_ref[k, pl.ds(at, half), :].astype(F32) * weight).astype(BF)
            first = spare + n * half
            table[first : first + half, k * tokens : (k + 1) * tokens] = rows
    size = PLANE * slots
    whole = width + spare
    cut = whole - BLOCK
    for s in range(0, experts // PLANE, 2):
        left = lax.dot_general(
            pick[s * size : (s + 1) * size], table[spare:], NT, preferred_element_type=F32
        )
        right = lax.dot_general(
            pick[(s + 1) * size : (s + 2) * size], table[0:whole], NT, preferred_element_type=F32
        )
        at = s * width
        for k in range(PLANE):
            these = slice(k * slots, (k + 1) * slots)
            sent[k][:, at : at + cut] = left[these, 0:cut].astype(BF)
            sent[k][:, at + cut : at + whole] = (
                left[these, cut:] + right[these, 0:BLOCK]
            ).astype(BF)
            sent[k][:, at + whole : at + pair] = right[these, BLOCK:].astype(BF)
    for copy in copies[4:]:
        copy.wait()


def relay_kernel(slots, count, begin, *refs):
    blocks, outs, table = refs[:count], refs[-1 - PLANE : -1], refs[-1]
    part = outs[0].shape[1] // count
    model = begin + part
    for n, ext_ref in enumerate(blocks):
        table[...] = ext_ref[:, model : model + BLOCK].astype(F32).T
        select(slots, table, ext_ref.at[:, pl.ds(begin, part)], outs, n * part)


def forward_kernel(*refs):
    del refs


def moved(piece, by):
    return pltpu.roll(piece.astype(F32), by % piece.shape[1], 1) if by else piece.astype(F32)


def regroup_kernel(s, width, *refs):
    out_ref = refs[-1]
    whole = up(width, BLOCK)
    spare = whole - width
    cut = whole - BLOCK
    at = s // 2 * 2 * width + s % 2 * (width - spare)
    lanes = lax.broadcasted_iota(jnp.int32, (out_ref.shape[1], BLOCK), 1)
    for k in range(0, PLANE, 2):
        left = moved(refs[k][:, at : at + whole], -(s % 2) * spare)
        right = moved(refs[k + 1][:, at : at + whole], (1 - s % 2) * spare)
        out_ref[k // 2, :, 0:cut] = left[:, 0:cut].astype(BF)
        out_ref[k // 2, :, cut:whole] = jnp.where(
            lanes < width - cut, left[:, cut:], right[:, 0:BLOCK]
        ).astype(BF)
        out_ref[k // 2, :, whole:] = right[:, BLOCK:].astype(BF)


def fill(table, at, piece, stride):
    wide = piece.astype(F32)
    short = stride - wide.shape[0]
    if short:
        wide = jnp.concatenate([wide, jnp.zeros((short, wide.shape[1]), F32)], axis=0)
    table[at : at + stride, :] = wide.astype(table.dtype)


def halves(flip):
    mine = lax.axis_index("replica") if flip else 1
    return 1 - mine, mine


def stage_kernel(place, spans, stride, flip, *refs):
    arrays, refs = refs[: PLANE * len(spans)], refs[PLANE * len(spans) :]
    w_ref, refs = refs[0], refs[1:]
    hid_ref = refs[0]
    all_rows, all_hidw, gate_ref, rows, hids, hidw, done = refs[-7:]
    group = PLANE * stride
    width, model = w_ref.shape
    half = width // 2
    whole = hids.shape[1]
    spare = whole - width
    to = 0
    for n, (at, count) in enumerate(spans):
        for k in range(PLANE):
            piece = arrays[n * PLANE + k][:, at : at + count]
            fill(rows.at[:, pl.ds(to, count)], k * stride, piece, stride)
        to += count
    copy = pltpu.make_async_copy(rows, all_rows.at[pl.ds(place * group, group)], done.at[0])
    copy.start()
    for k in range(PLANE):
        at = k % 2 * (width - spare)
        fill(hids, k * stride, moved(hid_ref[k // 2, :, at : at + whole], -(k % 2) * spare), stride)
    flipped = hids[...].T
    hidw[...] = flipped[0:width, :].astype(BF)
    back = lax.dot_general(w_ref[...], rows[...], NT, preferred_element_type=F32)
    turned = halves(flip)[0] == 1
    low, high = flipped[0:half, :], flipped[half:width, :]
    terms = back[0:half, :] * jnp.where(turned, high, low)
    terms += back[half:width, :] * jnp.where(turned, low, high)
    gate = jnp.sum(terms, axis=0, keepdims=True)
    second = pltpu.make_async_copy(
        hidw, all_hidw.at[:, pl.ds(place * group, group)], done.at[1]
    )
    second.start()
    gate_ref[...] = jnp.zeros_like(gate_ref)
    for k in range(PLANE):
        gate_ref[k : k + 1, 0:stride] = gate[:, k * stride : (k + 1) * stride]
    copy.wait()
    second.wait()


def own_left_kernel(stride, at, *refs):
    pieces, (w_ref, hid_ref) = refs[:PLANE], refs[PLANE : PLANE + 2]
    all_rows, all_hidw, back_ref, hidw_ref, rows, hids, done = refs[PLANE + 2 :]
    group, lead = rows.shape
    width, whole = hidw_ref.shape[0], hids.shape[1]
    spare = whole - width
    for k in range(PLANE):
        fill(rows, k * stride, pieces[k][:, at : at + lead], stride)
        first = k % 2 * (width - spare)
        piece = hid_ref[k // 2, :, first : first + whole]
        fill(hids, k * stride, moved(piece, -(k % 2) * spare), stride)
    hidw_ref[...] = hids[...].T[0:width, :].astype(BF)
    copies = [
        pltpu.make_async_copy(
            rows, all_rows.at[pl.ds(group, group), pl.ds(0, lead)], done.at[0]
        ),
        pltpu.make_async_copy(hidw_ref, all_hidw.at[:, pl.ds(group, group)], done.at[1]),
    ]
    for copy in copies:
        copy.start()
    back_ref[...] = lax.dot_general(
        w_ref[:, 0:lead], rows[...], NT, preferred_element_type=F32
    )
    for copy in copies:
        copy.wait()


def own_right_kernel(stride, flip, *refs):
    pieces, (w_ref, back_ref, hidw_ref) = refs[:PLANE], refs[PLANE : PLANE + 3]
    rows_ref, gate_ref = refs[-2:]
    lead = w_ref.shape[1] - rows_ref.shape[1]
    for k in range(PLANE):
        fill(rows_ref, k * stride, pieces[k][...], stride)
    back = back_ref[...] + lax.dot_general(
        w_ref[:, lead:], rows_ref[...], NT, preferred_element_type=F32
    )
    half = back.shape[0] // 2
    turned = halves(flip)[0] == 1
    low = hidw_ref[0:half, :].astype(F32)
    high = hidw_ref[half:, :].astype(F32)
    terms = back[0:half, :] * jnp.where(turned, high, low)
    terms += back[half:, :] * jnp.where(turned, low, high)
    gate = jnp.sum(terms, axis=0, keepdims=True)
    gate_ref[...] = jnp.zeros_like(gate_ref)
    for k in range(PLANE):
        gate_ref[k : k + 1, 0:stride] = gate[:, k * stride : (k + 1) * stride]


def source(outer, s, k):
    me = lax.axis_index("expert")
    return lax.rem((me >> 2) - s + outer, outer) * PLANE + ((me & 3) ^ k)


def early_kernel(step, rows_ref, hidw_ref, out_ref, mark_ref):
    mark_ref[...] = jnp.zeros_like(mark_ref)
    for c in range(0, out_ref.shape[1], step):
        span = slice(c, c + step)
        got = jnp.dot(hidw_ref[...], rows_ref[:, span], preferred_element_type=F32)
        out_ref[:, span] = got.astype(BF)


def partial_kernel(first, step, late, rows_ref, hidw_ref, early_ref, *refs):
    send_ref, mine_ref = refs[-2:]
    half = mine_ref.shape[0]
    for c in range(0, mine_ref.shape[1], step):
        span, here = slice(first + c, first + c + step), slice(c, c + step)
        got = early_ref[:, span].astype(F32)
        if late:
            group = refs[0].shape[0]
            got += jnp.dot(
                hidw_ref[:, 0:group], rows_ref[0:group, span], preferred_element_type=F32
            ) + jnp.dot(hidw_ref[:, group:], refs[0][:, here], preferred_element_type=F32)
        else:
            got += jnp.dot(hidw_ref[...], rows_ref[:, span], preferred_element_type=F32)
        send_ref[:, here] = got[0:half].astype(BF)
        mine_ref[:, here] = got[half:].astype(BF)


def combine_kernel(outer, *refs):
    gates, outs = refs[:outer], refs[-PLANE:]
    for k, out_ref in enumerate(outs):
        for s, gate_ref in enumerate(gates):
            out_ref[s : s + 1, :] = gate_ref[k : k + 1, :]


def pick_gates(slot_ref, routes_ref, num_ref, homes, gate_ref, rows):
    experts, tokens = slot_ref.shape
    for k in range(PLANE):
        for s in range(experts // PLANE):
            rows[pl.ds(source(experts // PLANE, -s, k), 1), :] = homes[k][s : s + 1, :]
    slot = jnp.maximum(slot_ref[...], 0.0).astype(jnp.int32)
    value = jnp.take_along_axis(rows[...], slot, axis=1)
    ids = lax.broadcasted_iota(jnp.int32, (experts, tokens), 0)
    for k in range(gate_ref.shape[0]):
        got = jnp.sum(
            jnp.where(routes_ref[k : k + 1, :] == ids, value, 0.0), axis=0, keepdims=True
        )
        gate_ref[k : k + 1, :] = got / (num_ref[k : k + 1, :].astype(F32) * (1.0 / 1024.0))


def finish_kernel(first, step, count, extra, *refs):
    own, others_ref, refs = refs[:count], refs[count], refs[count + 1 :]
    if extra:
        slot_ref, routes_ref, num_ref, *homes = refs[: 3 + PLANE]
        out_hbm, scale_hbm, gate_ref, out, scales, table, done, rows = refs[5 + PLANE :]
    else:
        out_hbm, scale_hbm, out, scales, table, done = refs
    share, width = out.shape
    lanes = lax.broadcasted_iota(jnp.int32, (share, BLOCK), 1)
    copies = []
    kept = jnp.zeros((share, BLOCK), F32)
    for c in range(0, width, step):
        for at in range(c, c + step, BLOCK):
            span = slice(at, at + BLOCK)
            terms = [others_ref[n, :, span].astype(F32) for n in range(others_ref.shape[0])]
            terms += [ref[:, span].astype(F32) for ref in own]
            top = functools.reduce(jnp.maximum, [jnp.abs(term) for term in terms])
            scale = jnp.max(top, axis=1, keepdims=True) + 1e-6
            out[:, span] = functools.reduce(jnp.add, terms) * (1.0 / scale)
            kept = jnp.where(lanes == at // BLOCK, scale, kept)
        copy = pltpu.make_async_copy(
            out.at[:, pl.ds(c, step)], out_hbm.at[:, pl.ds(first + c, step)], done.at[len(copies)]
        )
        copy.start()
        copies.append(copy)
    table[...] = jnp.zeros_like(table)
    table[0:share, :] = kept
    scales[...] = table[...].T[0 : scales.shape[0], 0:share]
    copy = pltpu.make_async_copy(
        scales, scale_hbm.at[pl.ds(first // BLOCK, scales.shape[0])], done.at[len(copies)]
    )
    copy.start()
    copies.append(copy)
    if extra:
        pick_gates(slot_ref, routes_ref, num_ref, homes, gate_ref, rows)
    for copy in copies:
        copy.wait()


def per_device(cotangent, hidden, routes, numerators, w_down):
    tokens, model = cotangent.shape
    top_k, width = hidden.shape[1], hidden.shape[2]
    experts, replicas = lax.axis_size("expert"), lax.axis_size("replica")
    outer = experts // PLANE
    slots = up(3 * tokens * top_k // (2 * experts), 8)
    stride = up(slots, 32)
    half = width // 2
    share = width // replicas
    group = PLANE * stride
    flip = replicas == 2
    sds = jax.ShapeDtypeStruct
    step, fine = 512, 256

    def ring(array, by):
        pairs = [(e, (e + by * PLANE) % experts) for e in range(experts)]
        return lax.ppermute(array, "expert", pairs)

    def swap(array, k):
        return lax.ppermute(array, "expert", [(e, e ^ k) for e in range(experts)])

    anywhere = pl.BlockSpec(memory_space=pl.ANY)
    inside = pl.BlockSpec(memory_space=pltpu.VMEM)

    lead = model // 2
    wide = outer * width + lead
    ext, *packed, slot = call(
        functools.partial(open_kernel, slots, flip),
        [sds((tokens, model + BLOCK), BF)]
        + [sds((slots, wide), BF)] * PLANE
        + [sds((experts, tokens), F32)],
        ALL_VMEM,
        in_specs=[anywhere] * 4,
        out_specs=[anywhere] + [inside] * (1 + PLANE),
        scratch_shapes=[
            pltpu.VMEM((tokens, model + BLOCK), BF),
            pltpu.VMEM((2 * up(width, BLOCK) - width, top_k * tokens), BF),
            pltpu.VMEM((top_k, tokens), jnp.int32),
            pltpu.VMEM((top_k, tokens), jnp.int32),
            pltpu.VMEM((top_k, width, tokens), BF),
            pltpu.SemaphoreType.DMA((5,)),
        ],
    )(routes.T, numerators.T, jnp.transpose(hidden, (1, 2, 0)), cotangent)
    opening = [packed[0]] + [swap(packed[k], k) for k in range(1, PLANE)]

    blocks = {0: ext}
    order = [0]
    for s in range(1, outer // 2 + 1):
        blocks[s] = ring(blocks[s - 1], 1)
        order.append(s)
        if outer - s != s:
            blocks[outer - s] = ring(blocks[(outer - s + 1) % outer], -1)
            order.append(outer - s)
    def regroup(s, after):
        return call(
            functools.partial(regroup_kernel, s, width),
            sds((PLANE // 2, slots, 2 * width), BF),
            in_specs=[inside] * PLANE + [anywhere] * len(after),
        )(*opening, *after)

    hids = {0: regroup(0, [])}
    for n, s in enumerate(order[1:]):
        hids[s] = ring(regroup(s, [blocks[order[-1]]] if n else []), s)

    def gated(arrays, after):
        return call(
            forward_kernel,
            [sds(array.shape, array.dtype) for array in arrays],
            in_specs=[anywhere] * (len(arrays) + len(after)),
            out_specs=[anywhere] * len(arrays),
            input_output_aliases={n: n for n in range(len(arrays))},
        )(*arrays, *after)

    def relay(batch, after, begin=0):
        sent = call(
            functools.partial(relay_kernel, slots, len(batch), begin),
            [sds((slots, len(batch) * (model - begin)), BF)] * PLANE,
            scratch_shapes=[pltpu.VMEM((BLOCK, tokens), F32)],
        )(*[blocks[s] for s in batch])
        moved = gated(sent[1:], after)
        return [sent[0]] + [swap(moved[k - 1], k) for k in range(1, PLANE)]

    middle = relay(order[1:-1], opening[1:])
    late = relay(order[-1:], [hids[order[1]]])
    final = relay([0], [*middle[1:], hids[order[-2]]], lead)

    def stage(parts, hid, place, count, after, rows):
        arrays = [array for got, _ in parts for array in got]
        fixed = len(arrays) + 2
        return call(
            functools.partial(stage_kernel, place, [span for _, span in parts], stride, flip),
            [
                sds((count * group, model), BF),
                sds((width, count * group), BF),
                sds((PLANE, BLOCK), F32),
            ],
            flops=2_000_000_000,
            in_specs=[inside] * fixed + [anywhere] * len(rows) + [inside] * len(after),
            out_specs=[anywhere, anywhere, inside],
            input_output_aliases={fixed + i: i for i in range(len(rows))},
            scratch_shapes=[
                pltpu.VMEM((group, model), BF),
                pltpu.VMEM((group, up(width, BLOCK)), F32),
                pltpu.VMEM((width, group), BF),
                pltpu.SemaphoreType.DMA((2,)),
            ],
        )(*arrays, w_down[0], hid, *rows, *after)

    sources = {s: [(middle, (n * model, model))] for n, s in enumerate(order[1:-1])}
    sources[order[-1]] = [(late, (0, model))]
    sources[0] = [(opening, (wide - lead, lead)), (final, (0, model - lead))]
    rows, gates = [], {}
    for n, s in enumerate(order[1:-1]):
        *rows, gates[s] = stage(sources[s], hids[s], n, outer - 2, [], rows)
    early, mark = call(
        functools.partial(early_kernel, step),
        [sds((width, model), BF), sds((8, BLOCK), F32)],
        flops=3_500_000_000,
    )(*rows)
    *rows, back, own_hidw = call(
        functools.partial(own_left_kernel, stride, wide - lead),
        [
            sds((2 * group, model), BF),
            sds((width, 2 * group), BF),
            sds((width, group), F32),
            sds((width, group), BF),
        ],
        flops=2_000_000_000,
        in_specs=[inside] * (PLANE + 2),
        out_specs=[anywhere] * 2 + [inside] * 2,
        scratch_shapes=[
            pltpu.VMEM((group, lead), BF),
            pltpu.VMEM((group, up(width, BLOCK)), F32),
            pltpu.SemaphoreType.DMA((2,)),
        ],
    )(*opening, w_down[0], hids[0])
    *rows, gates[order[-1]] = stage(
        sources[order[-1]], hids[order[-1]], 0, 2, [mark], rows
    )
    for s, gate in zip(
        order[1:-1], gated([gates[s] for s in order[1:-1]], [gates[order[-1]]])
    ):
        gates[s] = gate
    gates[0] = None
    gates = [ring(gates[s], -s) if s else gates[s] for s in range(outer)]

    def partial(first, more, after):
        return call(
            functools.partial(partial_kernel, first, step, bool(more)),
            [sds((half, model // 2), BF)] * 2,
            flops=4_000_000_000,
            in_specs=[inside] * (3 + len(more)) + [anywhere] * len(after),
        )(*rows, early, *more, *after)

    def finish(first, send, mine, out, extra):
        if flip:
            others = lax.ppermute(send, "replica", [(0, 1), (1, 0)])[None]
            own = [mine]
        else:
            both = jnp.concatenate([send, mine], axis=0).reshape(replicas, share, model // 2)
            others = lax.all_to_all(both, "replica", 0, 0, tiled=True)
            own = []
        fixed = len(own) + 1 + len(extra)
        outs = [sds((share, model), F32), sds((model // BLOCK, share), F32)]
        out_specs = [anywhere] * 2
        scratch = [
            pltpu.VMEM((share, model // 2), F32),
            pltpu.VMEM((model // 2 // BLOCK, share), F32),
            pltpu.VMEM((up(share, BLOCK), BLOCK), F32),
            pltpu.SemaphoreType.DMA((model // 2 // fine + 1,)),
        ]
        if extra:
            outs.append(sds((top_k, tokens), F32))
            out_specs.append(inside)
            scratch.append(pltpu.VMEM((experts, BLOCK), F32))
        return call(
            functools.partial(finish_kernel, first, fine, len(own), bool(extra)),
            outs,
            in_specs=[inside] * fixed + [anywhere] * len(out),
            out_specs=out_specs,
            input_output_aliases={fixed + n: n for n in range(len(out))},
            scratch_shapes=scratch,
        )(*own, others, *extra, *out)

    left = partial(0, [], [])
    own_rows, gates[0] = call(
        functools.partial(own_right_kernel, stride, flip),
        [sds((group, model - lead), BF), sds((PLANE, BLOCK), F32)],
        flops=4_000_000_000,
        in_specs=[inside] * (PLANE + 3) + [anywhere],
    )(*final, w_down[0], back, own_hidw, left[0])
    right = partial(model // 2, [own_rows], [])
    right = [*gated(right[:1], gates[1:]), right[1]]
    homes = call(
        functools.partial(combine_kernel, outer),
        [sds((outer, BLOCK), F32)] * PLANE,
        in_specs=[inside] * outer + [anywhere],
    )(*gates, left[0])
    homes = [homes[0]] + [swap(homes[k], k) for k in range(1, PLANE)]
    out = finish(0, *left, [], [])
    out, scales, gate_grad = finish(model // 2, *right, out, [slot, routes.T, numerators.T, *homes])
    return gate_grad.T, scales.T[None], out[None]


def solution(mesh):
    return jax.shard_map(
        per_device,
        mesh=mesh,
        in_specs=(
            P(("expert", "replica"), None),
            P(("expert", "replica"), None, None),
            P(("expert", "replica"), None),
            P(("expert", "replica"), None),
            P("expert", None, None),
        ),
        out_specs=(
            P(("expert", "replica"), None),
            P("expert", "replica", None),
            P("expert", "replica", None),
        ),
        check_vma=False,
    )
```

```python
import functools

import jax
import jax.numpy as jnp
from jax import lax
from jax.experimental import pallas as pl
from jax.experimental.pallas import tpu as pltpu
from jax.sharding import PartitionSpec as P

BLOCK = 128
PLANE = 4
BF = jnp.bfloat16
F32 = jnp.float32
NT = (((1,), (1,)), ((), ()))
VMEM_BYTES = 24 * 1024 * 1024
ALL_VMEM = 56 * 1024 * 1024


def up(value, unit):
    return -(-value // unit) * unit


def call(kernel, out_shape, room=VMEM_BYTES, flops=1024, **kw):
    return pl.pallas_call(
        kernel,
        out_shape=out_shape,
        cost_estimate=pl.CostEstimate(
            flops=flops, bytes_accessed=1024, transcendentals=0
        ),
        compiler_params=pltpu.CompilerParams(vmem_limit_bytes=room),
        **kw,
    )


def select(slots, table, cot_ref, outs, at=0):
    me = lax.axis_index("expert")
    tokens = cot_ref.shape[0]
    rows = lax.broadcasted_iota(jnp.int32, (slots, tokens), 0).astype(F32)
    pick = jnp.concatenate(
        [jnp.where(table[pl.ds(me ^ k, 1), :] == rows, 1.0, 0.0) for k in range(PLANE)], axis=0
    ).astype(BF)
    model = cot_ref.shape[1]
    step = min(512, model)
    for c in range(0, model, step):
        got = jnp.dot(pick, cot_ref[:, c : c + step], preferred_element_type=F32)
        for k in range(PLANE):
            outs[k][:, at + c : at + c + step] = got[k * slots : (k + 1) * slots, :].astype(BF)


def open_kernel(slots, flip, *refs):
    routes_hbm, num_hbm, hid_hbm, cot_hbm, ext_hbm, *refs = refs
    sent, (slot_ref, *refs) = refs[:PLANE], refs[PLANE:]
    ext, table, routes_ref, num_ref, hid_ref, done = refs
    experts, tokens = slot_ref.shape
    top_k, width = hid_ref.shape[:2]
    model = cot_hbm.shape[1]
    half = width // 2
    spare = up(width, BLOCK) - width
    pair = 2 * width
    pairs = (
        (routes_hbm, routes_ref),
        (cot_hbm, ext.at[:, pl.ds(0, model)]),
        (num_hbm, num_ref),
        (hid_hbm, hid_ref),
        (ext, ext_hbm),
    )
    copies = [pltpu.make_async_copy(*pair, done.at[n]) for n, pair in enumerate(pairs)]
    for copy in copies[:4]:
        copy.start()

    copies[0].wait()
    routes = routes_ref[...]
    ids = lax.broadcasted_iota(jnp.int32, (experts, tokens), 0)
    mask = jnp.zeros((experts, tokens), F32)
    for k in range(top_k):
        mask += jnp.where(routes[k : k + 1, :] == ids, 1.0, 0.0)
    earlier = lax.broadcasted_iota(jnp.int32, (tokens, tokens), 0) < lax.broadcasted_iota(
        jnp.int32, (tokens, tokens), 1
    )
    rank = jnp.dot(
        mask.astype(BF), jnp.where(earlier, 1.0, 0.0).astype(BF), preferred_element_type=F32
    )
    slot = jnp.where(mask > 0.5, rank, -1.0)
    slot_ref[...] = slot
    wide = jnp.concatenate([slot, jnp.zeros((BLOCK - experts, tokens), F32)], axis=0)
    ext[:, model : model + BLOCK] = wide.T.astype(BF)
    copies[1].wait()
    copies[4].start()
    parts = experts // PLANE * width
    lead = sent[0].shape[1] - parts
    select(slots, slot_ref, ext.at[:, pl.ds(0, lead)], sent, parts)
    me = lax.axis_index("expert")
    steps = (routes >> 2) - (me >> 2)
    steps = jnp.where(steps < 0, steps + experts // PLANE, steps)
    rel = steps * PLANE + ((routes & 3) ^ (me & 3))
    codes = []
    for k in range(top_k):
        own = jnp.sum(
            jnp.where(routes[k : k + 1, :] == ids, slot, 0.0), axis=0, keepdims=True
        ).astype(jnp.int32)
        codes.append(rel[k : k + 1, :] * slots + own)
    code = jnp.concatenate(codes, axis=1)
    rows = lax.broadcasted_iota(jnp.int32, (experts * slots, top_k * tokens), 0)
    pick = jnp.where(rows == code, 1.0, 0.0).astype(BF)
    copies[2].wait()
    copies[3].wait()
    blank = jnp.zeros((spare, top_k * tokens), BF)
    table[0:spare, :] = blank
    table[spare + width :, :] = blank
    for k in range(top_k):
        weight = num_ref[k : k + 1, :].astype(F32) * (1.0 / 1024.0)
        for n, part in enumerate(halves(flip)):
            at = pl.multiple_of(part * half, 16) if flip else part * half
            rows = (hid_ref[k, pl.ds(at, half), :].astype(F32) * weight).astype(BF)
            first = spare + n * half
            table[first : first + half, k * tokens : (k + 1) * tokens] = rows
    size = PLANE * slots
    whole = width + spare
    cut = whole - BLOCK
    for s in range(0, experts // PLANE, 2):
        left = lax.dot_general(
            pick[s * size : (s + 1) * size], table[spare:], NT, preferred_element_type=F32
        )
        right = lax.dot_general(
            pick[(s + 1) * size : (s + 2) * size], table[0:whole], NT, preferred_element_type=F32
        )
        at = s * width
        for k in range(PLANE):
            these = slice(k * slots, (k + 1) * slots)
            sent[k][:, at : at + cut] = left[these, 0:cut].astype(BF)
            sent[k][:, at + cut : at + whole] = (
                left[these, cut:] + right[these, 0:BLOCK]
            ).astype(BF)
            sent[k][:, at + whole : at + pair] = right[these, BLOCK:].astype(BF)
    for copy in copies[4:]:
        copy.wait()


def relay_kernel(slots, count, begin, *refs):
    blocks, outs, table = refs[:count], refs[-1 - PLANE : -1], refs[-1]
    part = outs[0].shape[1] // count
    model = begin + part
    for n, ext_ref in enumerate(blocks):
        table[...] = ext_ref[:, model : model + BLOCK].astype(F32).T
        select(slots, table, ext_ref.at[:, pl.ds(begin, part)], outs, n * part)


def forward_kernel(*refs):
    del refs


def moved(piece, by):
    return pltpu.roll(piece.astype(F32), by % piece.shape[1], 1) if by else piece.astype(F32)


def regroup_kernel(s, width, *refs):
    out_ref = refs[-1]
    whole = up(width, BLOCK)
    spare = whole - width
    cut = whole - BLOCK
    at = s // 2 * 2 * width + s % 2 * (width - spare)
    lanes = lax.broadcasted_iota(jnp.int32, (out_ref.shape[1], BLOCK), 1)
    for k in range(0, PLANE, 2):
        left = moved(refs[k][:, at : at + whole], -(s % 2) * spare)
        right = moved(refs[k + 1][:, at : at + whole], (1 - s % 2) * spare)
        out_ref[k // 2, :, 0:cut] = left[:, 0:cut].astype(BF)
        out_ref[k // 2, :, cut:whole] = jnp.where(
            lanes < width - cut, left[:, cut:], right[:, 0:BLOCK]
        ).astype(BF)
        out_ref[k // 2, :, whole:] = right[:, BLOCK:].astype(BF)


def fill(table, at, piece, stride):
    wide = piece.astype(F32)
    short = stride - wide.shape[0]
    if short:
        wide = jnp.concatenate([wide, jnp.zeros((short, wide.shape[1]), F32)], axis=0)
    table[at : at + stride, :] = wide.astype(table.dtype)


def halves(flip):
    mine = lax.axis_index("replica") if flip else 1
    return 1 - mine, mine


def stage_kernel(place, spans, stride, flip, *refs):
    arrays, refs = refs[: PLANE * len(spans)], refs[PLANE * len(spans) :]
    w_ref, refs = refs[0], refs[1:]
    hid_ref = refs[0]
    all_rows, all_hidw, gate_ref, rows, hids, hidw, done = refs[-7:]
    group = PLANE * stride
    width, model = w_ref.shape
    half = width // 2
    whole = hids.shape[1]
    spare = whole - width
    to = 0
    for n, (at, count) in enumerate(spans):
        for k in range(PLANE):
            piece = arrays[n * PLANE + k][:, at : at + count]
            fill(rows.at[:, pl.ds(to, count)], k * stride, piece, stride)
        to += count
    copy = pltpu.make_async_copy(rows, all_rows.at[pl.ds(place * group, group)], done.at[0])
    copy.start()
    for k in range(PLANE):
        at = k % 2 * (width - spare)
        fill(hids, k * stride, moved(hid_ref[k // 2, :, at : at + whole], -(k % 2) * spare), stride)
    flipped = hids[...].T
    hidw[...] = flipped[0:width, :].astype(BF)
    back = lax.dot_general(w_ref[...], rows[...], NT, preferred_element_type=F32)
    turned = halves(flip)[0] == 1
    low, high = flipped[0:half, :], flipped[half:width, :]
    terms = back[0:half, :] * jnp.where(turned, high, low)
    terms += back[half:width, :] * jnp.where(turned, low, high)
    gate = jnp.sum(terms, axis=0, keepdims=True)
    second = pltpu.make_async_copy(
        hidw, all_hidw.at[:, pl.ds(place * group, group)], done.at[1]
    )
    second.start()
    gate_ref[...] = jnp.zeros_like(gate_ref)
    for k in range(PLANE):
        gate_ref[k : k + 1, 0:stride] = gate[:, k * stride : (k + 1) * stride]
    copy.wait()
    second.wait()


def own_left_kernel(stride, at, *refs):
    pieces, (w_ref, hid_ref) = refs[:PLANE], refs[PLANE : PLANE + 2]
    all_rows, all_hidw, back_ref, hidw_ref, rows, hids, done = refs[PLANE + 2 :]
    group, lead = rows.shape
    width, whole = hidw_ref.shape[0], hids.shape[1]
    spare = whole - width
    for k in range(PLANE):
        fill(rows, k * stride, pieces[k][:, at : at + lead], stride)
        first = k % 2 * (width - spare)
        piece = hid_ref[k // 2, :, first : first + whole]
        fill(hids, k * stride, moved(piece, -(k % 2) * spare), stride)
    hidw_ref[...] = hids[...].T[0:width, :].astype(BF)
    copies = [
        pltpu.make_async_copy(
            rows, all_rows.at[pl.ds(group, group), pl.ds(0, lead)], done.at[0]
        ),
        pltpu.make_async_copy(hidw_ref, all_hidw.at[:, pl.ds(group, group)], done.at[1]),
    ]
    for copy in copies:
        copy.start()
    back_ref[...] = lax.dot_general(
        w_ref[:, 0:lead], rows[...], NT, preferred_element_type=F32
    )
    for copy in copies:
        copy.wait()


def own_right_kernel(stride, flip, *refs):
    pieces, (w_ref, back_ref, hidw_ref) = refs[:PLANE], refs[PLANE : PLANE + 3]
    rows_ref, gate_ref = refs[-2:]
    lead = w_ref.shape[1] - rows_ref.shape[1]
    for k in range(PLANE):
        fill(rows_ref, k * stride, pieces[k][...], stride)
    back = back_ref[...] + lax.dot_general(
        w_ref[:, lead:], rows_ref[...], NT, preferred_element_type=F32
    )
    half = back.shape[0] // 2
    turned = halves(flip)[0] == 1
    low = hidw_ref[0:half, :].astype(F32)
    high = hidw_ref[half:, :].astype(F32)
    terms = back[0:half, :] * jnp.where(turned, high, low)
    terms += back[half:, :] * jnp.where(turned, low, high)
    gate = jnp.sum(terms, axis=0, keepdims=True)
    gate_ref[...] = jnp.zeros_like(gate_ref)
    for k in range(PLANE):
        gate_ref[k : k + 1, 0:stride] = gate[:, k * stride : (k + 1) * stride]


def source(outer, s, k):
    me = lax.axis_index("expert")
    return lax.rem((me >> 2) - s + outer, outer) * PLANE + ((me & 3) ^ k)


def early_kernel(step, rows_ref, hidw_ref, out_ref, mark_ref):
    mark_ref[...] = jnp.zeros_like(mark_ref)
    for c in range(0, out_ref.shape[1], step):
        span = slice(c, c + step)
        got = jnp.dot(hidw_ref[...], rows_ref[:, span], preferred_element_type=F32)
        out_ref[:, span] = got.astype(BF)


def partial_kernel(first, step, late, rows_ref, hidw_ref, early_ref, *refs):
    send_ref, mine_ref = refs[-2:]
    half = mine_ref.shape[0]
    for c in range(0, mine_ref.shape[1], step):
        span, here = slice(first + c, first + c + step), slice(c, c + step)
        got = early_ref[:, span].astype(F32)
        if late:
            group = refs[0].shape[0]
            got += jnp.dot(
                hidw_ref[:, 0:group], rows_ref[0:group, span], preferred_element_type=F32
            ) + jnp.dot(hidw_ref[:, group:], refs[0][:, here], preferred_element_type=F32)
        else:
            got += jnp.dot(hidw_ref[...], rows_ref[:, span], preferred_element_type=F32)
        send_ref[:, here] = got[0:half].astype(BF)
        mine_ref[:, here] = got[half:].astype(BF)


def combine_kernel(outer, *refs):
    gates, outs = refs[:outer], refs[-PLANE:]
    for k, out_ref in enumerate(outs):
        for s, gate_ref in enumerate(gates):
            out_ref[s : s + 1, :] = gate_ref[k : k + 1, :]


def pick_kernel(slot_ref, routes_ref, num_ref, *refs):
    homes, gate_ref, rows = refs[:PLANE], refs[-2], refs[-1]
    experts, tokens = slot_ref.shape
    for k in range(PLANE):
        for s in range(experts // PLANE):
            rows[pl.ds(source(experts // PLANE, -s, k), 1), :] = homes[k][s : s + 1, :]
    slot = jnp.maximum(slot_ref[...], 0.0).astype(jnp.int32)
    value = jnp.take_along_axis(rows[...], slot, axis=1)
    ids = lax.broadcasted_iota(jnp.int32, (experts, tokens), 0)
    for k in range(gate_ref.shape[0]):
        got = jnp.sum(
            jnp.where(routes_ref[k : k + 1, :] == ids, value, 0.0), axis=0, keepdims=True
        )
        gate_ref[k : k + 1, :] = got / (num_ref[k : k + 1, :].astype(F32) * (1.0 / 1024.0))


def finish_kernel(first, step, count, extra, *refs):
    own, others_ref, refs = refs[:count], refs[count], refs[count + 1 :]
    out_hbm, scale_hbm, mark_ref, out, scales, table, done = refs[2 if extra else 0 :]
    mark_ref[...] = jnp.zeros_like(mark_ref)
    share, width = out.shape
    lanes = lax.broadcasted_iota(jnp.int32, (share, BLOCK), 1)
    copies = []
    kept = jnp.zeros((share, BLOCK), F32)
    for c in range(0, width, step):
        for at in range(c, c + step, BLOCK):
            span = slice(at, at + BLOCK)
            terms = [others_ref[n, :, span].astype(F32) for n in range(others_ref.shape[0])]
            terms += [ref[:, span].astype(F32) for ref in own]
            top = functools.reduce(jnp.maximum, [jnp.abs(term) for term in terms])
            scale = jnp.max(top, axis=1, keepdims=True) + 1e-6
            out[:, span] = functools.reduce(jnp.add, terms) * (1.0 / scale)
            kept = jnp.where(lanes == at // BLOCK, scale, kept)
        copy = pltpu.make_async_copy(
            out.at[:, pl.ds(c, step)], out_hbm.at[:, pl.ds(first + c, step)], done.at[len(copies)]
        )
        copy.start()
        copies.append(copy)
    table[...] = jnp.zeros_like(table)
    table[0:share, :] = kept
    scales[...] = table[...].T[0 : scales.shape[0], 0:share]
    copy = pltpu.make_async_copy(
        scales, scale_hbm.at[pl.ds(first // BLOCK, scales.shape[0])], done.at[len(copies)]
    )
    copy.start()
    copies.append(copy)
    for copy in copies:
        copy.wait()


def per_device(cotangent, hidden, routes, numerators, w_down):
    tokens, model = cotangent.shape
    top_k, width = hidden.shape[1], hidden.shape[2]
    experts, replicas = lax.axis_size("expert"), lax.axis_size("replica")
    outer = experts // PLANE
    slots = up(3 * tokens * top_k // (2 * experts), 8)
    stride = up(slots, 32)
    half = width // 2
    share = width // replicas
    group = PLANE * stride
    flip = replicas == 2
    sds = jax.ShapeDtypeStruct
    step, fine = 512, 256

    def ring(array, by):
        pairs = [(e, (e + by * PLANE) % experts) for e in range(experts)]
        return lax.ppermute(array, "expert", pairs)

    def swap(array, k):
        return lax.ppermute(array, "expert", [(e, e ^ k) for e in range(experts)])

    anywhere = pl.BlockSpec(memory_space=pl.ANY)
    inside = pl.BlockSpec(memory_space=pltpu.VMEM)

    lead = model // 2
    wide = outer * width + lead
    ext, *packed, slot = call(
        functools.partial(open_kernel, slots, flip),
        [sds((tokens, model + BLOCK), BF)]
        + [sds((slots, wide), BF)] * PLANE
        + [sds((experts, tokens), F32)],
        ALL_VMEM,
        in_specs=[anywhere] * 4,
        out_specs=[anywhere] + [inside] * (1 + PLANE),
        scratch_shapes=[
            pltpu.VMEM((tokens, model + BLOCK), BF),
            pltpu.VMEM((2 * up(width, BLOCK) - width, top_k * tokens), BF),
            pltpu.VMEM((top_k, tokens), jnp.int32),
            pltpu.VMEM((top_k, tokens), jnp.int32),
            pltpu.VMEM((top_k, width, tokens), BF),
            pltpu.SemaphoreType.DMA((5,)),
        ],
    )(routes.T, numerators.T, jnp.transpose(hidden, (1, 2, 0)), cotangent)
    opening = [packed[0]] + [swap(packed[k], k) for k in range(1, PLANE)]

    blocks = {0: ext}
    order = [0]
    for s in range(1, outer // 2 + 1):
        blocks[s] = ring(blocks[s - 1], 1)
        order.append(s)
        if outer - s != s:
            blocks[outer - s] = ring(blocks[(outer - s + 1) % outer], -1)
            order.append(outer - s)
    def regroup(s, after):
        return call(
            functools.partial(regroup_kernel, s, width),
            sds((PLANE // 2, slots, 2 * width), BF),
            in_specs=[inside] * PLANE + [anywhere] * len(after),
        )(*opening, *after)

    hids = {0: regroup(0, [])}
    for n, s in enumerate(order[1:]):
        hids[s] = ring(regroup(s, [blocks[order[-1]]] if n else []), s)

    def gated(arrays, after):
        return call(
            forward_kernel,
            [sds(array.shape, array.dtype) for array in arrays],
            in_specs=[anywhere] * (len(arrays) + len(after)),
            out_specs=[anywhere] * len(arrays),
            input_output_aliases={n: n for n in range(len(arrays))},
        )(*arrays, *after)

    def relay(batch, after, begin=0):
        sent = call(
            functools.partial(relay_kernel, slots, len(batch), begin),
            [sds((slots, len(batch) * (model - begin)), BF)] * PLANE,
            scratch_shapes=[pltpu.VMEM((BLOCK, tokens), F32)],
        )(*[blocks[s] for s in batch])
        moved = gated(sent[1:], after)
        return [sent[0]] + [swap(moved[k - 1], k) for k in range(1, PLANE)]

    middle = relay(order[1:-1], opening[1:])
    late = relay(order[-1:], [hids[order[1]]])
    final = relay([0], [*middle[1:], hids[order[-2]]], lead)

    def stage(parts, hid, place, count, after, rows):
        arrays = [array for got, _ in parts for array in got]
        fixed = len(arrays) + 2
        return call(
            functools.partial(stage_kernel, place, [span for _, span in parts], stride, flip),
            [
                sds((count * group, model), BF),
                sds((width, count * group), BF),
                sds((PLANE, BLOCK), F32),
            ],
            flops=2_000_000_000,
            in_specs=[inside] * fixed + [anywhere] * len(rows) + [inside] * len(after),
            out_specs=[anywhere, anywhere, inside],
            input_output_aliases={fixed + i: i for i in range(len(rows))},
            scratch_shapes=[
                pltpu.VMEM((group, model), BF),
                pltpu.VMEM((group, up(width, BLOCK)), F32),
                pltpu.VMEM((width, group), BF),
                pltpu.SemaphoreType.DMA((2,)),
            ],
        )(*arrays, w_down[0], hid, *rows, *after)

    sources = {s: [(middle, (n * model, model))] for n, s in enumerate(order[1:-1])}
    sources[order[-1]] = [(late, (0, model))]
    sources[0] = [(opening, (wide - lead, lead)), (final, (0, model - lead))]
    rows, gates = [], {}
    for n, s in enumerate(order[1:-1]):
        *rows, gates[s] = stage(sources[s], hids[s], n, outer - 2, [], rows)
    early, mark = call(
        functools.partial(early_kernel, step),
        [sds((width, model), BF), sds((8, BLOCK), F32)],
        flops=3_500_000_000,
    )(*rows)
    *rows, back, own_hidw = call(
        functools.partial(own_left_kernel, stride, wide - lead),
        [
            sds((2 * group, model), BF),
            sds((width, 2 * group), BF),
            sds((width, group), F32),
            sds((width, group), BF),
        ],
        flops=2_000_000_000,
        in_specs=[inside] * (PLANE + 2),
        out_specs=[anywhere] * 2 + [inside] * 2,
        scratch_shapes=[
            pltpu.VMEM((group, lead), BF),
            pltpu.VMEM((group, up(width, BLOCK)), F32),
            pltpu.SemaphoreType.DMA((2,)),
        ],
    )(*opening, w_down[0], hids[0])
    *rows, gates[order[-1]] = stage(
        sources[order[-1]], hids[order[-1]], 0, 2, [mark], rows
    )
    for s, gate in zip(
        order[1:-1], gated([gates[s] for s in order[1:-1]], [gates[order[-1]]])
    ):
        gates[s] = gate
    gates[0] = None
    gates = [ring(gates[s], -s) if s else gates[s] for s in range(outer)]

    def partial(first, more, after):
        return call(
            functools.partial(partial_kernel, first, step, bool(more)),
            [sds((half, model // 2), BF)] * 2,
            flops=4_000_000_000,
            in_specs=[inside] * (3 + len(more)) + [anywhere] * len(after),
        )(*rows, early, *more, *after)

    def finish(first, send, mine, out):
        if flip:
            others = lax.ppermute(send, "replica", [(0, 1), (1, 0)])[None]
            own = [mine]
        else:
            both = jnp.concatenate([send, mine], axis=0).reshape(replicas, share, model // 2)
            others = lax.all_to_all(both, "replica", 0, 0, tiled=True)
            own = []
        fixed = len(own) + 1
        outs = [sds((share, model), F32), sds((model // BLOCK, share), F32), sds((8, BLOCK), F32)]
        out_specs = [anywhere] * 2 + [inside]
        scratch = [
            pltpu.VMEM((share, model // 2), F32),
            pltpu.VMEM((model // 2 // BLOCK, share), F32),
            pltpu.VMEM((up(share, BLOCK), BLOCK), F32),
            pltpu.SemaphoreType.DMA((model // 2 // fine + 1,)),
        ]
        return call(
            functools.partial(finish_kernel, first, fine, len(own), bool(out)),
            outs,
            in_specs=[inside] * fixed + [anywhere] * len(out),
            out_specs=out_specs,
            input_output_aliases={fixed + n: n for n in range(len(out))},
            scratch_shapes=scratch,
        )(*own, others, *out)

    left = partial(0, [], [])
    own_rows, gates[0] = call(
        functools.partial(own_right_kernel, stride, flip),
        [sds((group, model - lead), BF), sds((PLANE, BLOCK), F32)],
        flops=4_000_000_000,
        in_specs=[inside] * (PLANE + 3) + [anywhere],
    )(*final, w_down[0], back, own_hidw, left[0])
    right = partial(model // 2, [own_rows], [])
    right = [*gated(right[:1], gates[1:]), right[1]]
    homes = call(
        functools.partial(combine_kernel, outer),
        [sds((outer, BLOCK), F32)] * PLANE,
        in_specs=[inside] * outer + [anywhere],
    )(*gates, left[0])
    homes = [homes[0]] + [swap(homes[k], k) for k in range(1, PLANE)]
    *out, _ = finish(0, *left, [])
    out, scales, mark = finish(model // 2, *right, out)
    gate_grad = call(
        pick_kernel,
        sds((top_k, tokens), F32),
        scratch_shapes=[pltpu.VMEM((experts, BLOCK), F32)],
    )(slot, routes.T, numerators.T, *homes, mark)
    return gate_grad.T, scales.T[None], out[None]


def solution(mesh):
    return jax.shard_map(
        per_device,
        mesh=mesh,
        in_specs=(
            P(("expert", "replica"), None),
            P(("expert", "replica"), None, None),
            P(("expert", "replica"), None),
            P(("expert", "replica"), None),
            P("expert", None, None),
        ),
        out_specs=(
            P(("expert", "replica"), None),
            P("expert", "replica", None),
            P("expert", "replica", None),
        ),
        check_vma=False,
    )
```

```python
import functools

import jax
import jax.numpy as jnp
from jax import lax
from jax.experimental import pallas as pl
from jax.experimental.pallas import tpu as pltpu
from jax.sharding import PartitionSpec as P

BLOCK = 128
PLANE = 4
BF = jnp.bfloat16
F32 = jnp.float32
NT = (((1,), (1,)), ((), ()))
VMEM_BYTES = 24 * 1024 * 1024
ALL_VMEM = 56 * 1024 * 1024


def up(value, unit):
    return -(-value // unit) * unit


def call(kernel, out_shape, room=VMEM_BYTES, flops=1024, **kw):
    return pl.pallas_call(
        kernel,
        out_shape=out_shape,
        cost_estimate=pl.CostEstimate(
            flops=flops, bytes_accessed=1024, transcendentals=0
        ),
        compiler_params=pltpu.CompilerParams(vmem_limit_bytes=room),
        **kw,
    )


def select(slots, table, cot_ref, outs, at=0):
    me = lax.axis_index("expert")
    tokens = cot_ref.shape[0]
    rows = lax.broadcasted_iota(jnp.int32, (slots, tokens), 0).astype(F32)
    pick = jnp.concatenate(
        [jnp.where(table[pl.ds(me ^ k, 1), :] == rows, 1.0, 0.0) for k in range(PLANE)], axis=0
    ).astype(BF)
    model = cot_ref.shape[1]
    step = min(512, model)
    for c in range(0, model, step):
        got = jnp.dot(pick, cot_ref[:, c : c + step], preferred_element_type=F32)
        for k in range(PLANE):
            outs[k][:, at + c : at + c + step] = got[k * slots : (k + 1) * slots, :].astype(BF)


def open_kernel(slots, flip, *refs):
    routes_hbm, num_hbm, hid_hbm, cot_hbm, ext_hbm, *refs = refs
    sent, (slot_ref, *refs) = refs[:PLANE], refs[PLANE:]
    ext, table, routes_ref, num_ref, hid_ref, done = refs
    experts, tokens = slot_ref.shape
    top_k, width = hid_ref.shape[:2]
    model = cot_hbm.shape[1]
    half = width // 2
    spare = up(width, BLOCK) - width
    pair = 2 * width
    pairs = (
        (routes_hbm, routes_ref),
        (cot_hbm, ext.at[:, pl.ds(0, model)]),
        (num_hbm, num_ref),
        (hid_hbm, hid_ref),
        (ext, ext_hbm),
    )
    copies = [pltpu.make_async_copy(*pair, done.at[n]) for n, pair in enumerate(pairs)]
    for copy in copies[:4]:
        copy.start()

    copies[0].wait()
    routes = routes_ref[...]
    ids = lax.broadcasted_iota(jnp.int32, (experts, tokens), 0)
    mask = jnp.zeros((experts, tokens), F32)
    for k in range(top_k):
        mask += jnp.where(routes[k : k + 1, :] == ids, 1.0, 0.0)
    earlier = lax.broadcasted_iota(jnp.int32, (tokens, tokens), 0) < lax.broadcasted_iota(
        jnp.int32, (tokens, tokens), 1
    )
    rank = jnp.dot(
        mask.astype(BF), jnp.where(earlier, 1.0, 0.0).astype(BF), preferred_element_type=F32
    )
    slot = jnp.where(mask > 0.5, rank, -1.0)
    slot_ref[...] = slot
    wide = jnp.concatenate([slot, jnp.zeros((BLOCK - experts, tokens), F32)], axis=0)
    ext[:, model : model + BLOCK] = wide.T.astype(BF)
    copies[1].wait()
    copies[4].start()
    parts = experts // PLANE * width
    lead = sent[0].shape[1] - parts
    select(slots, slot_ref, ext.at[:, pl.ds(0, lead)], sent, parts)
    me = lax.axis_index("expert")
    steps = (routes >> 2) - (me >> 2)
    steps = jnp.where(steps < 0, steps + experts // PLANE, steps)
    rel = steps * PLANE + ((routes & 3) ^ (me & 3))
    codes = []
    for k in range(top_k):
        own = jnp.sum(
            jnp.where(routes[k : k + 1, :] == ids, slot, 0.0), axis=0, keepdims=True
        ).astype(jnp.int32)
        codes.append(rel[k : k + 1, :] * slots + own)
    code = jnp.concatenate(codes, axis=1)
    rows = lax.broadcasted_iota(jnp.int32, (experts * slots, top_k * tokens), 0)
    pick = jnp.where(rows == code, 1.0, 0.0).astype(BF)
    copies[2].wait()
    copies[3].wait()
    blank = jnp.zeros((spare, top_k * tokens), BF)
    table[0:spare, :] = blank
    table[spare + width :, :] = blank
    for k in range(top_k):
        weight = num_ref[k : k + 1, :].astype(F32) * (1.0 / 1024.0)
        for n, part in enumerate(halves(flip)):
            at = pl.multiple_of(part * half, 16) if flip else part * half
            rows = (hid_ref[k, pl.ds(at, half), :].astype(F32) * weight).astype(BF)
            first = spare + n * half
            table[first : first + half, k * tokens : (k + 1) * tokens] = rows
    size = PLANE * slots
    whole = width + spare
    cut = whole - BLOCK
    for s in range(0, experts // PLANE, 2):
        left = lax.dot_general(
            pick[s * size : (s + 1) * size], table[spare:], NT, preferred_element_type=F32
        )
        right = lax.dot_general(
            pick[(s + 1) * size : (s + 2) * size], table[0:whole], NT, preferred_element_type=F32
        )
        at = s * width
        for k in range(PLANE):
            these = slice(k * slots, (k + 1) * slots)
            sent[k][:, at : at + cut] = left[these, 0:cut].astype(BF)
            sent[k][:, at + cut : at + whole] = (
                left[these, cut:] + right[these, 0:BLOCK]
            ).astype(BF)
            sent[k][:, at + whole : at + pair] = right[these, BLOCK:].astype(BF)
    for copy in copies[4:]:
        copy.wait()


def relay_kernel(slots, count, begin, *refs):
    blocks, outs, table = refs[:count], refs[-1 - PLANE : -1], refs[-1]
    part = outs[0].shape[1] // count
    model = begin + part
    for n, ext_ref in enumerate(blocks):
        table[...] = ext_ref[:, model : model + BLOCK].astype(F32).T
        select(slots, table, ext_ref.at[:, pl.ds(begin, part)], outs, n * part)


def forward_kernel(*refs):
    del refs


def moved(piece, by):
    return pltpu.roll(piece.astype(F32), by % piece.shape[1], 1) if by else piece.astype(F32)


def regroup_kernel(s, width, *refs):
    out_ref = refs[-1]
    whole = up(width, BLOCK)
    spare = whole - width
    cut = whole - BLOCK
    at = s // 2 * 2 * width + s % 2 * (width - spare)
    lanes = lax.broadcasted_iota(jnp.int32, (out_ref.shape[1], BLOCK), 1)
    for k in range(0, PLANE, 2):
        left = moved(refs[k][:, at : at + whole], -(s % 2) * spare)
        right = moved(refs[k + 1][:, at : at + whole], (1 - s % 2) * spare)
        out_ref[k // 2, :, 0:cut] = left[:, 0:cut].astype(BF)
        out_ref[k // 2, :, cut:whole] = jnp.where(
            lanes < width - cut, left[:, cut:], right[:, 0:BLOCK]
        ).astype(BF)
        out_ref[k // 2, :, whole:] = right[:, BLOCK:].astype(BF)


def fill(table, at, piece, stride):
    wide = piece.astype(F32)
    short = stride - wide.shape[0]
    if short:
        wide = jnp.concatenate([wide, jnp.zeros((short, wide.shape[1]), F32)], axis=0)
    table[at : at + stride, :] = wide.astype(table.dtype)


def halves(flip):
    mine = lax.axis_index("replica") if flip else 1
    return 1 - mine, mine


def stage_kernel(place, spans, stride, flip, *refs):
    arrays, refs = refs[: PLANE * len(spans)], refs[PLANE * len(spans) :]
    w_ref, refs = refs[0], refs[1:]
    hid_ref = refs[0]
    all_rows, all_hidw, gate_ref, rows, hids, hidw, done = refs[-7:]
    group = PLANE * stride
    width, model = w_ref.shape
    half = width // 2
    whole = hids.shape[1]
    spare = whole - width
    to = 0
    for n, (at, count) in enumerate(spans):
        for k in range(PLANE):
            piece = arrays[n * PLANE + k][:, at : at + count]
            fill(rows.at[:, pl.ds(to, count)], k * stride, piece, stride)
        to += count
    copy = pltpu.make_async_copy(rows, all_rows.at[pl.ds(place * group, group)], done.at[0])
    copy.start()
    for k in range(PLANE):
        at = k % 2 * (width - spare)
        fill(hids, k * stride, moved(hid_ref[k // 2, :, at : at + whole], -(k % 2) * spare), stride)
    flipped = hids[...].T
    hidw[...] = flipped[0:width, :].astype(BF)
    back = lax.dot_general(w_ref[...], rows[...], NT, preferred_element_type=F32)
    turned = halves(flip)[0] == 1
    low, high = flipped[0:half, :], flipped[half:width, :]
    terms = back[0:half, :] * jnp.where(turned, high, low)
    terms += back[half:width, :] * jnp.where(turned, low, high)
    gate = jnp.sum(terms, axis=0, keepdims=True)
    second = pltpu.make_async_copy(
        hidw, all_hidw.at[:, pl.ds(place * group, group)], done.at[1]
    )
    second.start()
    gate_ref[...] = jnp.zeros_like(gate_ref)
    for k in range(PLANE):
        gate_ref[k : k + 1, 0:stride] = gate[:, k * stride : (k + 1) * stride]
    copy.wait()
    second.wait()


def own_left_kernel(stride, at, *refs):
    pieces, (w_ref, hid_ref) = refs[:PLANE], refs[PLANE : PLANE + 2]
    all_rows, all_hidw, back_ref, hidw_ref, rows, hids, done = refs[PLANE + 2 :]
    group, lead = rows.shape
    width, whole = hidw_ref.shape[0], hids.shape[1]
    spare = whole - width
    for k in range(PLANE):
        fill(rows, k * stride, pieces[k][:, at : at + lead], stride)
        first = k % 2 * (width - spare)
        piece = hid_ref[k // 2, :, first : first + whole]
        fill(hids, k * stride, moved(piece, -(k % 2) * spare), stride)
    hidw_ref[...] = hids[...].T[0:width, :].astype(BF)
    copies = [
        pltpu.make_async_copy(
            rows, all_rows.at[pl.ds(group, group), pl.ds(0, lead)], done.at[0]
        ),
        pltpu.make_async_copy(hidw_ref, all_hidw.at[:, pl.ds(group, group)], done.at[1]),
    ]
    for copy in copies:
        copy.start()
    back_ref[...] = lax.dot_general(
        w_ref[:, 0:lead], rows[...], NT, preferred_element_type=F32
    )
    for copy in copies:
        copy.wait()


def own_right_kernel(stride, flip, *refs):
    pieces, (w_ref, back_ref, hidw_ref) = refs[:PLANE], refs[PLANE : PLANE + 3]
    rows_ref, gate_ref = refs[-2:]
    lead = w_ref.shape[1] - rows_ref.shape[1]
    for k in range(PLANE):
        fill(rows_ref, k * stride, pieces[k][...], stride)
    back = back_ref[...] + lax.dot_general(
        w_ref[:, lead:], rows_ref[...], NT, preferred_element_type=F32
    )
    half = back.shape[0] // 2
    turned = halves(flip)[0] == 1
    low = hidw_ref[0:half, :].astype(F32)
    high = hidw_ref[half:, :].astype(F32)
    terms = back[0:half, :] * jnp.where(turned, high, low)
    terms += back[half:, :] * jnp.where(turned, low, high)
    gate = jnp.sum(terms, axis=0, keepdims=True)
    gate_ref[...] = jnp.zeros_like(gate_ref)
    for k in range(PLANE):
        gate_ref[k : k + 1, 0:stride] = gate[:, k * stride : (k + 1) * stride]


def source(outer, s, k):
    me = lax.axis_index("expert")
    return lax.rem((me >> 2) - s + outer, outer) * PLANE + ((me & 3) ^ k)


def early_kernel(step, rows_ref, hidw_ref, out_ref, mark_ref):
    mark_ref[...] = jnp.zeros_like(mark_ref)
    for c in range(0, out_ref.shape[1], step):
        span = slice(c, c + step)
        got = jnp.dot(hidw_ref[...], rows_ref[:, span], preferred_element_type=F32)
        out_ref[:, span] = got.astype(BF)


def partial_kernel(first, step, late, rows_ref, hidw_ref, early_ref, *refs):
    send_ref, mine_ref = refs[-2:]
    half = mine_ref.shape[0]
    for c in range(0, mine_ref.shape[1], step):
        span, here = slice(first + c, first + c + step), slice(c, c + step)
        got = early_ref[:, span].astype(F32)
        if late:
            group = refs[0].shape[0]
            got += jnp.dot(
                hidw_ref[:, 0:group], rows_ref[0:group, span], preferred_element_type=F32
            ) + jnp.dot(hidw_ref[:, group:], refs[0][:, here], preferred_element_type=F32)
        else:
            got += jnp.dot(hidw_ref[...], rows_ref[:, span], preferred_element_type=F32)
        send_ref[:, here] = got[0:half].astype(BF)
        mine_ref[:, here] = got[half:].astype(BF)


def combine_kernel(outer, *refs):
    gates, outs = refs[:outer], refs[-PLANE:]
    for k, out_ref in enumerate(outs):
        for s, gate_ref in enumerate(gates):
            out_ref[s : s + 1, :] = gate_ref[k : k + 1, :]


def pick_kernel(slot_ref, routes_ref, num_ref, *refs):
    homes, gate_ref, rows = refs[:PLANE], refs[-2], refs[-1]
    experts, tokens = slot_ref.shape
    for k in range(PLANE):
        for s in range(experts // PLANE):
            rows[pl.ds(source(experts // PLANE, -s, k), 1), :] = homes[k][s : s + 1, :]
    slot = jnp.maximum(slot_ref[...], 0.0).astype(jnp.int32)
    value = jnp.take_along_axis(rows[...], slot, axis=1)
    ids = lax.broadcasted_iota(jnp.int32, (experts, tokens), 0)
    for k in range(gate_ref.shape[0]):
        got = jnp.sum(
            jnp.where(routes_ref[k : k + 1, :] == ids, value, 0.0), axis=0, keepdims=True
        )
        gate_ref[k : k + 1, :] = got / (num_ref[k : k + 1, :].astype(F32) * (1.0 / 1024.0))


def finish_kernel(first, step, count, extra, *refs):
    own, others_ref, refs = refs[:count], refs[count], refs[count + 1 :]
    out_hbm, scale_hbm, mark_ref, out, scales, table, done = refs[2 if extra else 0 :]
    mark_ref[...] = jnp.zeros_like(mark_ref)
    share, width = out.shape
    lanes = lax.broadcasted_iota(jnp.int32, (share, BLOCK), 1)
    copies = []
    kept = jnp.zeros((share, BLOCK), F32)
    for c in range(0, width, step):
        for at in range(c, c + step, BLOCK):
            span = slice(at, at + BLOCK)
            terms = [others_ref[n, :, span].astype(F32) for n in range(others_ref.shape[0])]
            terms += [ref[:, span].astype(F32) for ref in own]
            top = functools.reduce(jnp.maximum, [jnp.abs(term) for term in terms])
            scale = jnp.max(top, axis=1, keepdims=True) + 1e-6
            out[:, span] = functools.reduce(jnp.add, terms) * (1.0 / scale)
            kept = jnp.where(lanes == at // BLOCK, scale, kept)
        copy = pltpu.make_async_copy(
            out.at[:, pl.ds(c, step)], out_hbm.at[:, pl.ds(first + c, step)], done.at[len(copies)]
        )
        copy.start()
        copies.append(copy)
    table[...] = jnp.zeros_like(table)
    table[0:share, :] = kept
    scales[...] = table[...].T[0 : scales.shape[0], 0:share]
    copy = pltpu.make_async_copy(
        scales, scale_hbm.at[pl.ds(first // BLOCK, scales.shape[0])], done.at[len(copies)]
    )
    copy.start()
    copies.append(copy)
    for copy in copies:
        copy.wait()


def per_device(cotangent, hidden, routes, numerators, w_down):
    tokens, model = cotangent.shape
    top_k, width = hidden.shape[1], hidden.shape[2]
    experts, replicas = lax.axis_size("expert"), lax.axis_size("replica")
    outer = experts // PLANE
    slots = up(3 * tokens * top_k // (2 * experts), 8)
    stride = up(slots, 32)
    half = width // 2
    share = width // replicas
    group = PLANE * stride
    flip = replicas == 2
    sds = jax.ShapeDtypeStruct
    step, fine = 512, 256

    def ring(array, by):
        pairs = [(e, (e + by * PLANE) % experts) for e in range(experts)]
        return lax.ppermute(array, "expert", pairs)

    def swap(array, k):
        return lax.ppermute(array, "expert", [(e, e ^ k) for e in range(experts)])

    anywhere = pl.BlockSpec(memory_space=pl.ANY)
    inside = pl.BlockSpec(memory_space=pltpu.VMEM)

    lead = model // 2
    wide = outer * width + lead
    ext, *packed, slot = call(
        functools.partial(open_kernel, slots, flip),
        [sds((tokens, model + BLOCK), BF)]
        + [sds((slots, wide), BF)] * PLANE
        + [sds((experts, tokens), F32)],
        ALL_VMEM,
        in_specs=[anywhere] * 4,
        out_specs=[anywhere] + [inside] * (1 + PLANE),
        scratch_shapes=[
            pltpu.VMEM((tokens, model + BLOCK), BF),
            pltpu.VMEM((2 * up(width, BLOCK) - width, top_k * tokens), BF),
            pltpu.VMEM((top_k, tokens), jnp.int32),
            pltpu.VMEM((top_k, tokens), jnp.int32),
            pltpu.VMEM((top_k, width, tokens), BF),
            pltpu.SemaphoreType.DMA((5,)),
        ],
    )(routes.T, numerators.T, jnp.transpose(hidden, (1, 2, 0)), cotangent)
    opening = [packed[0]] + [swap(packed[k], k) for k in range(1, PLANE)]

    blocks = {0: ext}
    order = [0]
    for s in range(1, outer // 2 + 1):
        blocks[s] = ring(blocks[s - 1], 1)
        order.append(s)
        if outer - s != s:
            blocks[outer - s] = ring(blocks[(outer - s + 1) % outer], -1)
            order.append(outer - s)
    def regroup(s, after):
        return call(
            functools.partial(regroup_kernel, s, width),
            sds((PLANE // 2, slots, 2 * width), BF),
            in_specs=[inside] * PLANE + [anywhere] * len(after),
        )(*opening, *after)

    hids = {0: regroup(0, [])}
    for n, s in enumerate(order[1:]):
        hids[s] = ring(regroup(s, [blocks[order[-1]]] if n else []), s)

    def gated(arrays, after):
        return call(
            forward_kernel,
            [sds(array.shape, array.dtype) for array in arrays],
            in_specs=[anywhere] * (len(arrays) + len(after)),
            out_specs=[anywhere] * len(arrays),
            input_output_aliases={n: n for n in range(len(arrays))},
        )(*arrays, *after)

    def relay(batch, after, begin=0):
        sent = call(
            functools.partial(relay_kernel, slots, len(batch), begin),
            [sds((slots, len(batch) * (model - begin)), BF)] * PLANE,
            scratch_shapes=[pltpu.VMEM((BLOCK, tokens), F32)],
        )(*[blocks[s] for s in batch])
        moved = gated(sent[1:], after)
        return [sent[0]] + [swap(moved[k - 1], k) for k in range(1, PLANE)]

    middle = relay(order[1:-1], opening[1:])
    late = relay(order[-1:], [hids[order[1]]])
    final = relay([0], [*middle[1:], hids[order[-2]]], lead)

    def stage(parts, hid, place, count, after, rows):
        arrays = [array for got, _ in parts for array in got]
        fixed = len(arrays) + 2
        return call(
            functools.partial(stage_kernel, place, [span for _, span in parts], stride, flip),
            [
                sds((count * group, model), BF),
                sds((width, count * group), BF),
                sds((PLANE, BLOCK), F32),
            ],
            flops=2_000_000_000,
            in_specs=[inside] * fixed + [anywhere] * len(rows) + [inside] * len(after),
            out_specs=[anywhere, anywhere, inside],
            input_output_aliases={fixed + i: i for i in range(len(rows))},
            scratch_shapes=[
                pltpu.VMEM((group, model), BF),
                pltpu.VMEM((group, up(width, BLOCK)), F32),
                pltpu.VMEM((width, group), BF),
                pltpu.SemaphoreType.DMA((2,)),
            ],
        )(*arrays, w_down[0], hid, *rows, *after)

    sources = {s: [(middle, (n * model, model))] for n, s in enumerate(order[1:-1])}
    sources[order[-1]] = [(late, (0, model))]
    sources[0] = [(opening, (wide - lead, lead)), (final, (0, model - lead))]
    rows, gates = [], {}
    for n, s in enumerate(order[1:-1]):
        *rows, gates[s] = stage(sources[s], hids[s], n, outer - 2, [], rows)
    early, mark = call(
        functools.partial(early_kernel, step),
        [sds((width, model), BF), sds((8, BLOCK), F32)],
        flops=3_500_000_000,
    )(*rows)
    *rows, back, own_hidw = call(
        functools.partial(own_left_kernel, stride, wide - lead),
        [
            sds((2 * group, model), BF),
            sds((width, 2 * group), BF),
            sds((width, group), F32),
            sds((width, group), BF),
        ],
        flops=2_000_000_000,
        in_specs=[inside] * (PLANE + 2),
        out_specs=[anywhere] * 2 + [inside] * 2,
        scratch_shapes=[
            pltpu.VMEM((group, lead), BF),
            pltpu.VMEM((group, up(width, BLOCK)), F32),
            pltpu.SemaphoreType.DMA((2,)),
        ],
    )(*opening, w_down[0], hids[0])
    *rows, gates[order[-1]] = stage(
        sources[order[-1]], hids[order[-1]], 0, 2, [mark], rows
    )
    for s, gate in zip(
        order[1:-1], gated([gates[s] for s in order[1:-1]], [gates[order[-1]]])
    ):
        gates[s] = gate
    gates[0] = None
    gates = [ring(gates[s], -s) if s else gates[s] for s in range(outer)]

    def partial(first, more, after):
        return call(
            functools.partial(partial_kernel, first, step, bool(more)),
            [sds((half, model // 2), BF)] * 2,
            flops=4_000_000_000,
            in_specs=[inside] * (3 + len(more)) + [anywhere] * len(after),
        )(*rows, early, *more, *after)

    def finish(first, send, mine, out):
        if flip:
            others = lax.ppermute(send, "replica", [(0, 1), (1, 0)])[None]
            own = [mine]
        else:
            both = jnp.concatenate([send, mine], axis=0).reshape(replicas, share, model // 2)
            others = lax.all_to_all(both, "replica", 0, 0, tiled=True)
            own = []
        fixed = len(own) + 1
        outs = [sds((share, model), F32), sds((model // BLOCK, share), F32), sds((8, BLOCK), F32)]
        out_specs = [anywhere] * 2 + [inside]
        scratch = [
            pltpu.VMEM((share, model // 2), F32),
            pltpu.VMEM((model // 2 // BLOCK, share), F32),
            pltpu.VMEM((up(share, BLOCK), BLOCK), F32),
            pltpu.SemaphoreType.DMA((model // 2 // fine + 1,)),
        ]
        return call(
            functools.partial(finish_kernel, first, fine, len(own), bool(out)),
            outs,
            in_specs=[inside] * fixed + [anywhere] * len(out),
            out_specs=out_specs,
            input_output_aliases={fixed + n: n for n in range(len(out))},
            scratch_shapes=scratch,
        )(*own, others, *out)

    left = partial(0, [], [])
    own_rows, gates[0] = call(
        functools.partial(own_right_kernel, stride, flip),
        [sds((group, model - lead), BF), sds((PLANE, BLOCK), F32)],
        flops=4_000_000_000,
        in_specs=[inside] * (PLANE + 3) + [anywhere],
    )(*final, w_down[0], back, own_hidw, left[0])
    right = partial(model // 2, [own_rows], [])
    right = [right[0], *gated(right[1:], gates[1:])]
    homes = call(
        functools.partial(combine_kernel, outer),
        [sds((outer, BLOCK), F32)] * PLANE,
        in_specs=[inside] * outer + [anywhere],
    )(*gates, left[0])
    homes = [homes[0]] + [swap(homes[k], k) for k in range(1, PLANE)]
    *out, _ = finish(0, *left, [])
    out, scales, mark = finish(model // 2, *right, out)
    gate_grad = call(
        pick_kernel,
        sds((top_k, tokens), F32),
        scratch_shapes=[pltpu.VMEM((experts, BLOCK), F32)],
    )(slot, routes.T, numerators.T, *homes, mark)
    return gate_grad.T, scales.T[None], out[None]


def solution(mesh):
    return jax.shard_map(
        per_device,
        mesh=mesh,
        in_specs=(
            P(("expert", "replica"), None),
            P(("expert", "replica"), None, None),
            P(("expert", "replica"), None),
            P(("expert", "replica"), None),
            P("expert", None, None),
        ),
        out_specs=(
            P(("expert", "replica"), None),
            P("expert", "replica", None),
            P("expert", "replica", None),
        ),
        check_vma=False,
    )
```
